32 devices in a mesh: section: 4 (over z), batch: 4 (over y, x), mp: 2 (over core).
Axes of the slice: x: 2, y: 2, z: 4, core: 2. Of those that a mesh axis runs over, the one named last changes fastest.
Arguments:
- tokens: bfloat16 [4, 2, 1024, 1024], P('batch', None, 'mp'), may hold values from -6 to 6
- cotangent: bfloat16 [4, 2, 1024, 1024], P('batch', None, 'mp'), may hold values from -6 to 6
- document_starts: int32 [4, 2, 1, 4], P('batch'), may hold values from 0 to 1023, as said below
- pre_gain: bfloat16 [4, 2, 1024], P('section'), may hold values from 0.099609375 to 1.8984375
- pre_bias: bfloat16 [4, 2, 1024], P('section'), may hold values from -1.75 to 1.75
- project_weight: bfloat16 [4, 3, 1024, 1024], P('section', None, None, 'mp'), may hold values from -0.1875 to 0.1875
- project_bias: bfloat16 [4, 2, 1024], P('section', None, 'mp'), may hold values from -3 to 3
- head_scale: bfloat16 [4, 16], P('section', 'mp'), may hold values from 0.5 to 2
- post_gain: bfloat16 [4, 1024], P('section', 'mp'), may hold values from 0.099609375 to 1.8984375
- post_bias: bfloat16 [4, 1024], P('section', 'mp'), may hold values from -1.75 to 1.75
- output_weight: bfloat16 [4, 1024, 1024], P('section', 'mp'), may hold values from -0.1875 to 0.1875
- expand_weight: bfloat16 [4, 1024, 4096], P('section', None, 'mp'), may hold values from -0.1875 to 0.1875
- expand_bias: bfloat16 [4, 4096], P('section', 'mp'), may hold values from -3 to 3
- middle_gain: bfloat16 [4, 4096], P('section', 'mp'), may hold values from 0.099609375 to 1.8984375
- middle_bias: bfloat16 [4, 4096], P('section', 'mp'), may hold values from -1.75 to 1.75
- reduce_weight: bfloat16 [4, 4096, 1024], P('section', 'mp'), may hold values from -0.09375 to 0.09375
- branch_bias: bfloat16 [4, 2, 1024], P('section'), may hold values from -1.75 to 1.75
Outputs:
- hidden_states: bfloat16 [4, 4, 2, 1024, 1024], P('section', 'batch', None, 'mp')
- input_gradient: bfloat16 [4, 4, 2, 1024, 1024], P('section', 'batch', None, 'mp')
- pre_gain_gradient: float32 [4, 2, 1024], P('section')
- pre_bias_gradient: float32 [4, 2, 1024], P('section')
- project_weight_gradient: float32 [4, 3, 1024, 1024], P('section', None, None, 'mp')
- project_bias_gradient: float32 [4, 2, 1024], P('section', None, 'mp')
- head_scale_gradient: float32 [4, 16], P('section', 'mp')
- post_gain_gradient: float32 [4, 1024], P('section', 'mp')
- post_bias_gradient: float32 [4, 1024], P('section', 'mp')
- output_weight_gradient: float32 [4, 1024, 1024], P('section', 'mp')
- expand_weight_gradient: float32 [4, 1024, 4096], P('section', None, 'mp')
- expand_bias_gradient: float32 [4, 4096], P('section', 'mp')
- middle_gain_gradient: float32 [4, 4096], P('section', 'mp')
- middle_bias_gradient: float32 [4, 4096], P('section', 'mp')
- reduce_weight_gradient: float32 [4, 4096, 1024], P('section', 'mp')
- branch_bias_gradient: float32 [4, 2, 1024], P('section')
The draws below stay inside these ranges and needn't reach their ends.
Inputs may be any that keep to these rules, and one draw needn't show every extreme that they name: `document_starts`: each row's offsets are non-decreasing and begin with 0; in every batch shard one of its 2 x 1 row is a single document (all offsets 0).
All inputs are finite; a program needn't handle non-finite values.
Results may differ from the reference program's by a relative error of at most 0.025.
Values may be sent and summed in bfloat16 or wider, within the bound.
No kernel may reach another device: no remote copies, remote signals or barrier semaphores. Data moves between devices by JAX's collectives and lax.ppermute only.
A program may use at most 512 MiB of HBM per device.

```python
import math
import jax
import jax.numpy as jnp
from jax import lax

D = 1024
HEADS = 16
FF = 4096
HEAD = 64
LENGTH = 1024
SEQS = 1
MICRO = 2
NDOC = 4
LAYERS = 4
NB = 4
MTOK = 1024


def draw_document_starts(key, part):
    rows = MICRO * SEQS
    picked = jax.random.randint(jax.random.fold_in(key, 11), (NB, 1), 0, rows)
    inner = jax.random.randint(jax.random.fold_in(key, 12), (NB, rows, NDOC - 1), 1, LENGTH)
    inner = jnp.sort(inner, axis=-1)
    row_ids = jnp.arange(rows, dtype=jnp.int32)[None, :]
    single = row_ids == picked
    closing = row_ids == (picked + 1) % rows
    final = jnp.where(closing, LENGTH - 1, inner[:, :, NDOC - 2])
    inner = jnp.concatenate([inner[:, :, :NDOC - 2], final[:, :, None]], axis=-1)
    inner = jnp.where(single[:, :, None], 0, inner)
    starts = jnp.concatenate([jnp.zeros((NB, rows, 1), jnp.int32), inner], axis=-1)
    return starts.reshape(NB, MICRO, SEQS, NDOC).astype(jnp.int32)


def steps_of(key, dims, pieces, smallest, high):
    def one(dim, parts):
        draws = jax.random.uniform(jax.random.fold_in(jax.random.fold_in(key, 6), dim), (parts,), jnp.float32, smallest / len(pieces), high / len(pieces))
        return jnp.repeat(jnp.exp(draws), dims[dim] // parts).reshape((-1,) + (1,) * (len(dims) - dim - 1))

    gain = one(*pieces[0])
    for cut in pieces[1:]:
        gain = gain * one(*cut)
    return gain


def scatter_about(key, extent, deviation, bound, pieces=(), held_as=jnp.bfloat16):
    result = deviation * jax.random.normal(key, extent, jnp.float32)
    if pieces:
        result = result * steps_of(key, extent, pieces, -0.22, 0.18)
    return jnp.clip(result, -bound, bound).astype(held_as)


def setup_inputs(seed: int = 0) -> dict:
    keys = jax.random.split(jax.random.key(seed), 18)
    return {
        "tokens": scatter_about(keys[0], (NB, MICRO, MTOK, D), 1.0, 6.0, ((0, 4), (2, 2))),
        "cotangent": scatter_about(keys[1], (NB, MICRO, MTOK, D), 1.0, 6.0, ((0, 4), (2, 2))),
        "document_starts": draw_document_starts(jax.random.fold_in(keys[17], 71), 0),
        "pre_gain": jnp.clip(1.0 + 0.18 * jax.random.normal(keys[3], (LAYERS, 2, D), jnp.float32), 0.099609375, 1.8984375).astype(jnp.bfloat16),
        "pre_bias": scatter_about(keys[4], (LAYERS, 2, D), 0.3, 1.75, ((0, 4),)),
        "project_weight": scatter_about(keys[5], (LAYERS, 3, D, D), D ** -0.5, 0.1875, ((0, 4), (3, 2))),
        "project_bias": scatter_about(keys[6], (LAYERS, 2, D), 0.5, 3.0, ((0, 4), (2, 2))),
        "head_scale": jnp.clip(jnp.exp(math.log(2.0) - 1.3862944 * jax.random.uniform(keys[7], (LAYERS, HEADS), jnp.float32) ** steps_of(keys[7], (LAYERS, HEADS), ((0, 4), (1, 2)), -0.2, 0.2)), 0.5, 2.0).astype(jnp.bfloat16),
        "post_gain": jnp.clip(1.0 + 0.18 * jax.random.normal(keys[8], (LAYERS, D), jnp.float32), 0.099609375, 1.8984375).astype(jnp.bfloat16),
        "post_bias": scatter_about(keys[9], (LAYERS, D), 0.3, 1.75, ((0, 4), (1, 2))),
        "output_weight": scatter_about(keys[10], (LAYERS, D, D), D ** -0.5, 0.1875, ((0, 4), (1, 2))),
        "expand_weight": scatter_about(keys[11], (LAYERS, D, FF), D ** -0.5, 0.1875, ((0, 4), (2, 2))),
        "expand_bias": scatter_about(keys[12], (LAYERS, FF), 0.5, 3.0, ((0, 4), (1, 2))),
        "middle_gain": jnp.clip(1.0 + 0.18 * jax.random.normal(keys[13], (LAYERS, FF), jnp.float32), 0.099609375, 1.8984375).astype(jnp.bfloat16),
        "middle_bias": scatter_about(keys[14], (LAYERS, FF), 0.3, 1.75, ((0, 4), (1, 2))),
        "reduce_weight": scatter_about(keys[15], (LAYERS, FF, D), FF ** -0.5, 0.09375, ((0, 4), (1, 2))),
        "branch_bias": scatter_about(keys[16], (LAYERS, 2, D), 0.3, 1.75, ((0, 4),)),
    }


HIGHEST = lax.Precision.HIGHEST
EPSILON = 1e-05

@jax.custom_vjp
def low(v):
    return lax.optimization_barrier(v.astype(jnp.bfloat16)).astype(jnp.float32)

@jax.custom_vjp
def low_back(v):
    return v

def low_keep(v):
    return (low(v), None)

def low_pass(kept, grad):
    return (grad,)

def back_keep(v):
    return (v, None)

def back_low(kept, grad):
    return (low(grad),)
low.defvjp(low_keep, low_pass)
low_back.defvjp(back_keep, back_low)

def layer_norm(values, norm_gain, norm_bias):
    centre = values - lax.optimization_barrier(jnp.mean(values, axis=-1, keepdims=True))
    inv_std = lax.rsqrt(lax.optimization_barrier(jnp.mean(centre * centre, axis=-1, keepdims=True)) + EPSILON)
    return centre * inv_std * norm_gain + norm_bias

def attend_one(items):
    queries, key_rows, value_rows, starts = items
    place = lax.iota(jnp.int32, LENGTH)
    doc_ids = lax.optimization_barrier(jnp.sum((starts[:, None] <= place[None, :]).astype(jnp.int32), axis=0))
    allowed = (place[None, :] <= place[:, None]) & (doc_ids[:, None] == doc_ids[None, :])
    scores = low_back(jnp.dot(queries, key_rows.T, precision=HIGHEST)) * HEAD ** (-0.5)
    masked = jnp.where(allowed, scores, -1e+30)
    top = lax.optimization_barrier(jnp.max(masked, axis=-1, keepdims=True))
    totals = top + jnp.log(lax.optimization_barrier(jnp.sum(jnp.exp(masked - top), axis=-1, keepdims=True)))
    probs = low(jnp.exp(masked - totals))
    return jnp.dot(probs, value_rows, precision=HIGHEST)

def by_head(tensor):
    return tensor.reshape(SEQS, LENGTH, HEADS, HEAD).transpose(0, 2, 1, 3).reshape(SEQS * HEADS, LENGTH, HEAD)

def layer_forward(layer_in, weight_set, starts):
    pre_gain, pre_bias, project_weight, project_bias, head_scale, post_gain, post_bias, output_weight, expand_weight, expand_bias, middle_gain, middle_bias, reduce_weight, branch_bias = weight_set
    first = low(layer_norm(layer_in, pre_gain[0], pre_bias[0]))
    project = jnp.einsum('td,cdf->ctf', first, project_weight, precision=HIGHEST)
    queries = low(low_back(project[0]) + project_bias[0])
    key_part = low(low_back(project[1]))
    value_part = low(low_back(project[2]) + project_bias[1])
    head_starts = jnp.repeat(starts, HEADS, axis=0)
    attended = lax.map(jax.checkpoint(attend_one), (by_head(queries), by_head(key_part), by_head(value_part), head_starts))
    attended = attended.reshape(SEQS, HEADS, LENGTH, HEAD).transpose(0, 2, 1, 3).reshape(MTOK, HEADS, HEAD)
    attended = low_back(attended)
    mixed_heads = (attended * head_scale[None, :, None]).reshape(MTOK, D)
    post = low(layer_norm(mixed_heads, post_gain, post_bias))
    middle = layer_in + low_back(jnp.dot(post, output_weight, precision=HIGHEST)) + branch_bias[0]
    second = low(layer_norm(middle, pre_gain[1], pre_bias[1]))
    pre_act = low_back(jnp.dot(second, expand_weight, precision=HIGHEST)) + expand_bias
    active = low(layer_norm(jax.nn.gelu(pre_act, approximate=False), middle_gain, middle_bias))
    return middle + low_back(jnp.dot(active, reduce_weight, precision=HIGHEST)) + branch_bias[1]

def run_block(block_tokens, shifts, weights, starts):
    carry = block_tokens
    outputs = []
    for layer in range(LAYERS):
        layer_in = low_back(carry + shifts[layer])
        carry = low(layer_forward(layer_in, tuple((weight[layer] for weight in weights)), starts))
        outputs.append(carry)
    return jnp.stack(outputs)

def reference(tokens, cotangent, document_starts, pre_gain, pre_bias, project_weight, project_bias, head_scale, post_gain, post_bias, output_weight, expand_weight, expand_bias, middle_gain, middle_bias, reduce_weight, branch_bias):
    weights = tuple((weight.astype(jnp.float32) for weight in (pre_gain, pre_bias, project_weight, project_bias, head_scale, post_gain, post_bias, output_weight, expand_weight, expand_bias, middle_gain, middle_bias, reduce_weight, branch_bias)))
    flat_tokens = tokens.astype(jnp.float32).reshape(NB * MICRO, MTOK, D)
    flat_cotangent = cotangent.astype(jnp.float32).reshape(NB * MICRO, MTOK, D)
    flat_starts = document_starts.reshape(NB * MICRO, SEQS, NDOC)
    zero_shifts = jnp.zeros((LAYERS, MTOK, D), jnp.float32)

    def one_block(summed, items):
        block_tokens, block_cotangent, block_starts = items

        def forward_only(shifts, weight_set):
            return run_block(block_tokens, shifts, weight_set, block_starts)
        outputs, back = jax.vjp(forward_only, zero_shifts, weights)
        wanted = jnp.zeros_like(outputs).at[LAYERS - 1].set(block_cotangent)
        shift_grads, weight_grads = back(wanted)

        def add_up(left, right):
            return left + right
        summed = jax.tree.map(add_up, summed, weight_grads)
        return (summed, (outputs, shift_grads))
    start_sums = jax.tree.map(jnp.zeros_like, weights)
    summed, (outputs, shift_grads) = lax.scan(one_block, start_sums, (flat_tokens, flat_cotangent, flat_starts))
    hidden = outputs.reshape(NB, MICRO, LAYERS, MTOK, D).transpose(2, 0, 1, 3, 4).astype(jnp.bfloat16)
    gradient = shift_grads.reshape(NB, MICRO, LAYERS, MTOK, D).transpose(2, 0, 1, 3, 4).astype(jnp.bfloat16)
    return (hidden, gradient, summed[0], summed[1], summed[2], summed[3], summed[4], summed[5], summed[6], summed[7], summed[8], summed[9], summed[10], summed[11], summed[12], summed[13])
```

```python
from functools import partial

import jax
import jax.numpy as jnp
from jax import lax
from jax.experimental import pallas as pl
from jax.experimental.pallas import tpu as pltpu
from jax.sharding import PartitionSpec as P

EPSILON = 1e-05
CHUNK = 128
KEYS = 256
TILE = 512
HIDE = -1e30
F32 = jnp.float32
BF16 = jnp.bfloat16
VMEM = pl.BlockSpec(memory_space=pltpu.VMEM)
SMEM = pl.BlockSpec(memory_space=pltpu.SMEM)
HBM = pl.BlockSpec(memory_space=pltpu.HBM)


def dot_nn(left, right):
    return jnp.dot(left, right, preferred_element_type=F32)


def dot_nt(left, right):
    return lax.dot_general(left, right, (((1,), (1,)), ((), ())), preferred_element_type=F32)


def dot_tn(left, right):
    return lax.dot_general(left, right, (((0,), (0,)), ((), ())), preferred_element_type=F32)


def norm_parts(values):
    centre = values - jnp.mean(values, axis=-1, keepdims=True)
    inv_std = lax.rsqrt(jnp.mean(centre * centre, axis=-1, keepdims=True) + EPSILON)
    return centre * inv_std, inv_std


def norm_back(scaled, normed, inv_std):
    mean_one = jnp.mean(scaled, axis=-1, keepdims=True)
    mean_two = jnp.mean(scaled * normed, axis=-1, keepdims=True)
    return inv_std * (scaled - mean_one - normed * mean_two)


def column_sum(values):
    return jnp.sum(values, axis=0, keepdims=True)


def document_start(starts_ref, place):
    first = jnp.zeros_like(place)
    for k in range(starts_ref.shape[0]):
        start = starts_ref[k]
        first = jnp.maximum(first, jnp.where(place >= start, start, 0))
    return first


def half_masks():
    lane = lax.broadcasted_iota(jnp.int32, (1, 128), 1)
    return (lane < 64).astype(BF16), (lane >= 64).astype(BF16)


def stack_heads(pair):
    even, odd = half_masks()
    return jnp.concatenate([pair * even, pair * odd], axis=0)


def pick_heads(stacked):
    rows = stacked.shape[0] // 2
    lane = lax.broadcasted_iota(jnp.int32, (1, 128), 1)
    return jnp.where(lane < 64, stacked[:rows], stacked[rows:])


def copies_of(pairs, sems):
    return [pltpu.make_async_copy(a, b, sems.at[i]) for i, (a, b) in enumerate(pairs)]


def attend_kernel(
    tick_ref, section_ref, starts_ref, tok_ref, inc_ref, wp_a, wp_b, wo_a, wo_b, vec_ref,
    k_in, v_in, x_in, h1_in, q_in, o_in, lse_in, post_in, mid_in,
    k_ref, v_ref, x_buf, h1_buf, q_buf, o_buf, lse_buf, post_buf, mid_buf, mid_ref,
    x_s, h1_s, q_s, o_s, lse_s, post_s, hide_s, sems,
):
    del k_in, v_in, x_in, h1_in, q_in, o_in, lse_in, post_in, mid_in
    rows = mid_ref.shape[0]
    length, width = k_ref.shape
    half = width // 2
    section = section_ref[0]
    chunk = tick_ref[0] - 2 * section
    live = (chunk >= 0) & (chunk < length // rows)

    @pl.when(live)
    def _():
        first = pl.multiple_of(chunk * rows, rows)
        here = pl.ds(first, rows)

        @pl.when(section == 0)
        def _():
            x_s[...] = tok_ref[here, :]

        @pl.when(section != 0)
        def _():
            x_s[...] = inc_ref[...]

        layer_in = x_s[...].astype(F32)
        normed, _ = norm_parts(layer_in)
        h1 = (normed * vec_ref[0:1] + vec_ref[1:2]).astype(BF16)
        h1_s[...] = h1
        for side, weight in ((0, wp_a), (1, wp_b)):
            at = slice(side * half, (side + 1) * half)
            q = (dot_nn(h1, weight[0]) + vec_ref[2:3, at]).astype(BF16)
            q_s[:, at] = q * jnp.asarray(0.125, BF16)
            k_ref[here, at] = dot_nn(h1, weight[1]).astype(BF16)
            v_ref[here, at] = (dot_nn(h1, weight[2]) + vec_ref[3:4, at]).astype(BF16)

        def attend(keys):
            place = first + lax.broadcasted_iota(jnp.int32, (rows, 1), 0)
            start = document_start(starts_ref, place)
            key_at = lax.broadcasted_iota(jnp.int32, (rows, keys), 1)
            hide_s[:, :keys] = jnp.where((key_at <= place) & (key_at >= start), 0.0, HIDE)
            lane = lax.broadcasted_iota(jnp.int32, (rows, 128), 1)

            def one_pair(pair, lse):
                at = pl.ds(pl.multiple_of(pair * 128, 128), 128)
                queries = stack_heads(q_s[:, at])
                hide = hide_s[:, :keys]
                scores = dot_nt(queries, k_ref[0:keys, at]) + jnp.concatenate([hide, hide], axis=0)
                top = jnp.max(scores, axis=-1, keepdims=True)
                raised = jnp.exp(scores - top)
                total = jnp.sum(raised, axis=-1, keepdims=True)
                out = dot_nn(raised.astype(BF16), v_ref[0:keys, at]) / total
                o_s[:, at] = pick_heads(out)
                now = top + jnp.log(total)
                lse = jnp.where(lane == 2 * pair, now[:rows], lse)
                return jnp.where(lane == 2 * pair + 1, now[rows:], lse)

            lse = lax.fori_loop(0, width // 128, one_pair, jnp.zeros((rows, 128), F32))
            lse_s[...] = lse.T

        for count in range(length // KEYS):

            @pl.when(first // KEYS == count)
            def _():
                attend((count + 1) * KEYS)

        post_normed, _ = norm_parts(o_s[...] * vec_ref[4:5])
        post = (post_normed * vec_ref[5:6] + vec_ref[6:7]).astype(BF16)
        post_s[...] = post
        mid_ref[...] = (
            layer_in + dot_nn(post[:, :half], wo_a[...]) + dot_nn(post[:, half:], wo_b[...])
            + vec_ref[7:8]
        )
        copies = copies_of(
            (
                (x_s, x_buf.at[here]), (h1_s, h1_buf.at[here]), (q_s, q_buf.at[here]),
                (o_s, o_buf.at[here]), (lse_s, lse_buf.at[chunk]), (post_s, post_buf.at[here]),
                (mid_ref, mid_buf.at[here]),
            ),
            sems,
        )
        for copy in copies:
            copy.start()
        for copy in copies:
            copy.wait()


def gelu_parts(pre):
    phi = 0.5 + 0.5 * lax.erf(pre * 0.7071067811865476)
    density = jnp.exp(pre * pre * -0.5) * 0.3989422804014327
    return pre * phi, phi + pre * density


def expand_kernel(
    tick_ref, section_ref, mid_ref, we_a, we_b, wr_a, wr_b, vec_ref, wide_ref,
    h2_in, g_in, gp_in, m_in, st_in, hid_in,
    h2_buf, g_buf, gp_buf, m_buf, st_buf, hid_buf, out_ref,
    h2_s, gf_s, g_s, gp_s, m_s, st_s, sems,
):
    del h2_in, g_in, gp_in, m_in, st_in, hid_in
    rows = mid_ref.shape[0]
    half = we_a.shape[1]
    units = 2 * half
    length = h2_buf.shape[0]
    chunk = tick_ref[0] - 2 * section_ref[0]

    @pl.when((chunk >= 0) & (chunk < length // rows))
    def _():
        here = pl.ds(pl.multiple_of(chunk * rows, rows), rows)
        normed, _ = norm_parts(mid_ref[...])
        h2 = (normed * vec_ref[0:1] + vec_ref[1:2]).astype(BF16)
        h2_s[...] = h2
        total = jnp.zeros((rows, 1), F32)
        for tile in range(units // TILE):
            weight = we_a if tile * TILE < half else we_b
            inner = tile * TILE % half
            at = slice(tile * TILE, (tile + 1) * TILE)
            pre = dot_nn(h2, weight[:, inner:inner + TILE]) + wide_ref[0:1, at]
            active, slope = gelu_parts(pre)
            gf_s[:, at] = active
            g_s[:, at] = active.astype(BF16)
            gp_s[:, at] = slope.astype(BF16)
            total += jnp.sum(active, axis=-1, keepdims=True)
        mean = total / units
        square = jnp.zeros((rows, 1), F32)
        for tile in range(units // TILE):
            centre = gf_s[:, tile * TILE:(tile + 1) * TILE] - mean
            square += jnp.sum(centre * centre, axis=-1, keepdims=True)
        inv_std = lax.rsqrt(square / units + EPSILON)
        lane = lax.broadcasted_iota(jnp.int32, (rows, 128), 1)
        st_s[...] = jnp.where(lane == 0, mean, inv_std)
        out = mid_ref[...] + vec_ref[2:3]
        for tile in range(units // TILE):
            weight = wr_a if tile * TILE < half else wr_b
            inner = tile * TILE % half
            at = slice(tile * TILE, (tile + 1) * TILE)
            active = (gf_s[:, at] - mean) * inv_std * wide_ref[1:2, at] + wide_ref[2:3, at]
            active = active.astype(BF16)
            m_s[:, at] = active
            out += dot_nn(active, weight[inner:inner + TILE, :])
        out_ref[...] = out.astype(BF16)
        copies = copies_of(
            (
                (h2_s, h2_buf.at[here]), (g_s, g_buf.at[here]), (gp_s, gp_buf.at[here]),
                (m_s, m_buf.at[here]), (st_s, st_buf.at[here]), (out_ref, hid_buf.at[here]),
            ),
            sems,
        )
        for copy in copies:
            copy.start()
        for copy in copies:
            copy.wait()


def expand_back_kernel(
    tick_ref, section_ref, cot_ref, inc_ref, wr_a, wr_b, we_a, we_b, vec_ref, wide_ref,
    g_buf, gp_buf, st_buf, mid_buf,
    sum_in, wsum_in, df_in, dur_in, dmr_in,
    sum_ref, wsum_ref, df_buf, dur_buf, dmr_buf, dmid_ref,
    g_s, gp_s, st_s, mid_s, df_s, z_s, dur_s, dmr_s, in_sems, out_sems,
):
    del sum_in, wsum_in, df_in, dur_in, dmr_in
    rows = dmid_ref.shape[0]
    half = wr_a.shape[1]
    units = 2 * half
    length = g_buf.shape[0]
    count = length // rows
    section = section_ref[0]
    last = section_ref[1] - 1
    chunk = count - 1 - (tick_ref[0] - 2 * (last - section))

    @pl.when((chunk >= 0) & (chunk < count))
    def _():
        here = pl.ds(pl.multiple_of(chunk * rows, rows), rows)
        loads = copies_of(
            (
                (g_buf.at[here], g_s), (gp_buf.at[here], gp_s), (st_buf.at[here], st_s),
                (mid_buf.at[here], mid_s),
            ),
            in_sems,
        )
        for copy in loads:
            copy.start()

        @pl.when(section == last)
        def _():
            df_s[...] = cot_ref[here, :]

        @pl.when(section != last)
        def _():
            df_s[...] = inc_ref[...]

        grad_low = df_s[...]
        sum_ref[0:1] += column_sum(grad_low.astype(F32))
        for copy in loads:
            copy.wait()
        mean = st_s[:, 0:1]
        inv_std = st_s[:, 1:2]
        one = jnp.zeros((rows, 1), F32)
        two = jnp.zeros((rows, 1), F32)
        for tile in range(units // TILE):
            weight = wr_a if tile * TILE < half else wr_b
            inner = tile * TILE % half
            at = slice(tile * TILE, (tile + 1) * TILE)
            grad = dot_nn(grad_low, weight[:, inner:inner + TILE])
            normed = (g_s[:, at].astype(F32) - mean) * inv_std
            wsum_ref[0:1, at] += column_sum(grad * normed)
            wsum_ref[1:2, at] += column_sum(grad)
            scaled = grad * wide_ref[1:2, at]
            z_s[:, at] = scaled
            one += jnp.sum(scaled, axis=-1, keepdims=True)
            two += jnp.sum(scaled * normed, axis=-1, keepdims=True)
        one = one / units
        two = two / units
        grad_second = jnp.zeros((rows, dmid_ref.shape[1]), F32)
        for tile in range(units // TILE):
            weight = we_a if tile * TILE < half else we_b
            inner = tile * TILE % half
            at = slice(tile * TILE, (tile + 1) * TILE)
            normed = (g_s[:, at].astype(F32) - mean) * inv_std
            grad = inv_std * (z_s[:, at] - one - normed * two) * gp_s[:, at].astype(F32)
            wsum_ref[2:3, at] += column_sum(grad)
            low = grad.astype(BF16)
            dur_s[:, at] = low
            grad_second += dot_nn(low, weight[inner:inner + TILE, :])
        normed, inv_std = norm_parts(mid_s[...])
        sum_ref[1:2] += column_sum(grad_second * normed)
        sum_ref[2:3] += column_sum(grad_second)
        grad_mid = grad_low.astype(F32) + norm_back(grad_second * vec_ref[0:1], normed, inv_std)
        sum_ref[3:4] += column_sum(grad_mid)
        dmid_ref[...] = grad_mid
        dmr_s[...] = grad_mid.astype(BF16)
        stores = copies_of(
            ((df_s, df_buf.at[here]), (dur_s, dur_buf.at[here]), (dmr_s, dmr_buf.at[here])),
            out_sems,
        )
        for copy in stores:
            copy.start()
        for copy in stores:
            copy.wait()


def attend_back_kernel(
    tick_ref, section_ref, starts_ref, dmid_ref, wo_a, wo_b, wp_a, wp_b, vec_ref, k_ref, v_ref,
    x_buf, q_buf, o_buf, lse_buf,
    sum_in, dk_in, dv_in, dq_in, dkr_in, dvr_in, ig_in,
    sum_ref, dk_ref, dv_ref, dq_buf, dkr_buf, dvr_buf, ig_buf, out_ref,
    x_s, q_s, o_s, lse_s, do_s, dqf_s, hide_s, dq_s, dkr_s, dvr_s, in_sems, out_sems,
):
    del sum_in, dk_in, dv_in, dq_in, dkr_in, dvr_in, ig_in
    rows = dmid_ref.shape[0]
    length, width = k_ref.shape
    half = width // 2
    count = length // rows
    section = section_ref[0]
    last = section_ref[1] - 1
    chunk = count - 1 - (tick_ref[0] - 2 * (last - section))

    @pl.when((chunk >= 0) & (chunk < count))
    def _():
        first = pl.multiple_of(chunk * rows, rows)
        here = pl.ds(first, rows)
        loads = copies_of(
            (
                (x_buf.at[here], x_s), (q_buf.at[here], q_s), (o_buf.at[here], o_s),
                (lse_buf.at[chunk], lse_s),
            ),
            in_sems,
        )
        for copy in loads:
            copy.start()

        @pl.when(chunk == count - 1)
        def _():
            dk_ref[...] = jnp.zeros_like(dk_ref)
            dv_ref[...] = jnp.zeros_like(dv_ref)

        low = dmid_ref[...].astype(BF16)
        grad_post = jnp.concatenate([dot_nn(low, wo_a[...]), dot_nn(low, wo_b[...])], axis=1)
        for copy in loads:
            copy.wait()
        attended = o_s[...]
        normed, inv_std = norm_parts(attended * vec_ref[4:5])
        sum_ref[0:1] += column_sum(grad_post * normed)
        sum_ref[1:2] += column_sum(grad_post)
        grad_mixed = norm_back(grad_post * vec_ref[5:6], normed, inv_std)
        sum_ref[2:3] += column_sum(grad_mixed * attended)
        do_s[...] = (grad_mixed * vec_ref[4:5]).astype(BF16)

        def attend(keys):
            place = first + lax.broadcasted_iota(jnp.int32, (1, rows), 1)
            start = document_start(starts_ref, place)
            key_at = lax.broadcasted_iota(jnp.int32, (keys, rows), 0)
            hide_s[:keys, :] = jnp.where((key_at <= place) & (key_at >= start), 0.0, HIDE)

            def one_pair(pair, carry):
                at = pl.ds(pl.multiple_of(pair * 128, 128), 128)
                queries = stack_heads(q_s[:, at])
                grad_pair = do_s[:, at]
                grads = stack_heads(grad_pair)
                product = (grad_pair.astype(F32) * o_s[:, at]).T
                delta = jnp.concatenate(
                    [column_sum(product[:64]), column_sum(product[64:])], axis=1
                )
                lse = jnp.concatenate(
                    [lse_s[pl.ds(2 * pair, 1), :], lse_s[pl.ds(2 * pair + 1, 1), :]], axis=1
                )
                hide = hide_s[:keys, :]
                key_pair = k_ref[0:keys, at]
                scores = dot_nt(key_pair, queries) + jnp.concatenate([hide, hide], axis=1)
                probs = jnp.exp(scores - lse)
                grad_probs = dot_nt(v_ref[0:keys, at], grads)
                grad_scores = (probs * (grad_probs - delta)).astype(BF16)
                dk_ref[0:keys, at] += dot_nn(grad_scores, queries)
                dv_ref[0:keys, at] += dot_nn(probs.astype(BF16), grads)
                dqf_s[:, at] = pick_heads(dot_tn(grad_scores, key_pair)) * 0.125
                return carry

            lax.fori_loop(0, width // 128, one_pair, 0)

        for number in range(length // KEYS):

            @pl.when(first // KEYS == number)
            def _():
                attend((number + 1) * KEYS)

        grad_query = dqf_s[...]
        grad_value = dv_ref[here, :]
        sum_ref[3:4] += column_sum(grad_query)
        sum_ref[4:5] += column_sum(grad_value)
        dq_s[...] = grad_query.astype(BF16)
        dkr_s[...] = dk_ref[here, :].astype(BF16)
        dvr_s[...] = grad_value.astype(BF16)
        grad_first = jnp.zeros((rows, width), F32)
        for number, part in enumerate((dq_s, dkr_s, dvr_s)):
            grad_first += dot_nn(part[:, :half], wp_a[number])
            grad_first += dot_nn(part[:, half:], wp_b[number])
        normed, inv_std = norm_parts(x_s[...].astype(F32))
        sum_ref[5:6] += column_sum(grad_first * normed)
        sum_ref[6:7] += column_sum(grad_first)
        out = dmid_ref[...] + norm_back(grad_first * vec_ref[0:1], normed, inv_std)
        out_ref[...] = out.astype(BF16)
        stores = copies_of(
            (
                (dq_s, dq_buf.at[here]), (dkr_s, dkr_buf.at[here]), (dvr_s, dvr_buf.at[here]),
                (out_ref, ig_buf.at[here]),
            ),
            out_sems,
        )
        for copy in stores:
            copy.start()
        for copy in stores:
            copy.wait()


def flip_kernel(in_ref, out_ref):
    size = in_ref.shape[0]
    across = lax.broadcasted_iota(jnp.int32, (size, size), 1)
    down = lax.broadcasted_iota(jnp.int32, (size, size), 0)
    same = (across == down).astype(BF16)
    width = in_ref.shape[1]
    for part in range(width // size):
        at = slice(part * size, (part + 1) * size)
        out_ref[at, :] = dot_nt(same, in_ref[:, at]).astype(BF16)


def flipped(weight):
    rows, columns = weight.shape
    size = 256
    return pl.pallas_call(
        flip_kernel,
        grid=(rows // size,),
        in_specs=[pl.BlockSpec((size, columns), lambda i: (i, 0))],
        out_specs=pl.BlockSpec((columns, size), lambda i: (0, i)),
        out_shape=jax.ShapeDtypeStruct((columns, rows), weight.dtype),
        compiler_params=pltpu.CompilerParams(vmem_limit_bytes=16 * 2**20),
    )(weight)


def empty_kernel(*refs):
    del refs


def empty(shapes):
    return pl.pallas_call(
        empty_kernel,
        out_specs=[HBM] * len(shapes),
        out_shape=[pltpu.HBM(shape, dtype) for shape, dtype in shapes],
    )()


def call(kernel, inputs, specs, carried, carried_specs, fresh, fresh_specs, scratch, limit, flops):
    first = len(inputs)
    shapes = [
        pltpu.HBM(a.shape, a.dtype) if spec is HBM else jax.ShapeDtypeStruct(a.shape, a.dtype)
        for a, spec in zip(carried, carried_specs)
    ] + fresh
    return pl.pallas_call(
        kernel,
        in_specs=specs + carried_specs,
        out_specs=carried_specs + fresh_specs,
        out_shape=shapes,
        scratch_shapes=scratch,
        input_output_aliases={first + i: i for i in range(len(carried))},
        compiler_params=pltpu.CompilerParams(vmem_limit_bytes=limit),
        cost_estimate=pl.CostEstimate(flops=flops, bytes_accessed=2**22, transcendentals=0),
    )(*inputs, *carried)


def local(
    tokens, cotangent, document_starts, pre_gain, pre_bias, project_weight, project_bias,
    head_scale, post_gain, post_bias, output_weight, expand_weight, expand_bias, middle_gain,
    middle_bias, reduce_weight, branch_bias,
):
    sections = lax.axis_size("section")
    section = lax.axis_index("section")
    parts = lax.axis_size("mp")
    part = lax.axis_index("mp")
    micro, rows_here, width = tokens.shape[1:]
    length = rows_here * parts
    chunk = CHUNK
    count = length // chunk
    heads = head_scale.shape[1] * parts
    head = width // heads
    units = expand_bias.shape[1] * parts
    paired = parts == 2 and micro == 2

    if paired:

        def swapped(value):
            return lax.ppermute(value, "mp", [(0, 1), (1, 0)])

        def both(value, axis):
            del axis
            return value, swapped(value)

        def whole_rows(value):
            mine = lax.dynamic_index_in_dim(value, part, 0, keepdims=False)
            theirs = swapped(lax.dynamic_index_in_dim(value, 1 - part, 0, keepdims=False))
            return jnp.where(
                part == 0, jnp.concatenate([mine, theirs]), jnp.concatenate([theirs, mine])
            )

        def spread_rows(value):
            mine = lax.dynamic_slice_in_dim(value, part * rows_here, rows_here, 0)
            theirs = swapped(
                lax.dynamic_slice_in_dim(value, (1 - part) * rows_here, rows_here, 0)
            )
            return jnp.where(part == 0, jnp.stack([mine, theirs]), jnp.stack([theirs, mine]))

        def owned_sum(own, other):
            return own + swapped(other).astype(F32)

        block = part
        copies = 1.0
    else:

        def both(value, axis):
            whole = lax.all_gather(value, "mp", axis=axis, tiled=True)
            return tuple(jnp.split(whole, 2, axis=axis))

        def whole_rows(value):
            whole = lax.all_gather(value, "mp", axis=1, tiled=True)
            return lax.dynamic_index_in_dim(whole, part * micro // parts, 0, keepdims=False)

        def spread_rows(value):
            whole = lax.all_gather(value, "mp", axis=0)
            whole = whole[:: parts // micro]
            return lax.dynamic_slice_in_dim(whole, part * rows_here, rows_here, 1)

        block = part * micro // parts
        copies = micro / parts

    def wide(value, axis=0):
        return jnp.concatenate(both(value, axis), axis=axis)

    split = jnp.concatenate(
        [
            project_bias[0], jnp.repeat(head_scale[0], head)[None], post_gain, post_bias,
            expand_bias.reshape(-1, width // parts), middle_gain.reshape(-1, width // parts),
            middle_bias.reshape(-1, width // parts),
        ]
    )
    split_own, split_other = both(split, 1) if paired else (None, None)
    ratio = units // width

    def feature(first):
        if paired:
            return jnp.concatenate([split_own[first], split_other[first]]).astype(F32)
        return wide(split[first]).astype(F32)

    def unit(first):
        if paired:
            return jnp.concatenate(
                [split_own[first:first + ratio], split_other[first:first + ratio]]
            ).reshape(-1).astype(F32)
        return wide(split[first:first + ratio].reshape(-1)).astype(F32)

    gains = pre_gain[0].astype(F32)
    shifts = pre_bias[0].astype(F32)
    branch = branch_bias[0].astype(F32)
    vec_a = jnp.stack(
        [gains[0], shifts[0], feature(0), feature(1), feature(2), feature(3), feature(4), branch[0]]
    )
    vec_f = jnp.stack([gains[1], shifts[1], branch[1]])
    wide_f = jnp.stack([unit(5), unit(5 + ratio), unit(5 + 2 * ratio)])

    wp_a, wp_b = both(project_weight[0], 2)
    wo_a, wo_b = both(output_weight[0], 0)
    we_a, we_b = both(expand_weight[0], 1)
    wr_a, wr_b = both(reduce_weight[0], 0)
    token_rows = whole_rows(tokens[0])
    cotangent_rows = whole_rows(cotangent[0])
    starts = lax.dynamic_index_in_dim(document_starts[0], block, 0, keepdims=False)[0]
    place = jnp.stack([section, jnp.int32(sections)]).astype(jnp.int32)

    def sized(columns, dtype):
        return ((length, columns), dtype)

    (
        x_buf, h1_buf, q_buf, o_buf, lse_buf, post_buf, mid_buf,
        h2_buf, g_buf, gp_buf, m_buf, st_buf, hid_buf,
        df_buf, dur_buf, dmr_buf, dq_buf, dkr_buf, dvr_buf, ig_buf, dk_acc, dv_acc,
    ) = empty(
        [
            sized(width, BF16), sized(width, BF16), sized(width, BF16), sized(width, F32),
            ((count, 128, chunk), F32), sized(width, BF16), sized(width, F32),
            sized(width, BF16), sized(units, BF16), sized(units, BF16), sized(units, BF16),
            sized(128, F32), sized(width, BF16),
            sized(width, BF16), sized(units, BF16), sized(width, BF16), sized(width, BF16),
            sized(width, BF16), sized(width, BF16), sized(width, BF16), sized(width, F32),
            sized(width, F32),
        ]
    )
    k_all = jnp.zeros((length, width), BF16)
    v_all = jnp.zeros((length, width), BF16)
    dma = pltpu.SemaphoreType.DMA
    dense = 2 * chunk * width

    def shifted(value, distance):
        route = [(i, i + distance) for i in range(sections) if 0 <= i + distance < sections]
        return lax.ppermute(value, "section", route)

    ticks = count + 2 * (sections - 1)
    blank = jnp.zeros((chunk, width), BF16)
    incoming = blank
    sent = None
    for tick in range(ticks):
        now = jnp.full((1,), tick, jnp.int32)
        arriving = shifted(sent, 1) if sent is not None and tick + 1 < ticks else blank
        (
            k_all, v_all, x_buf, h1_buf, q_buf, o_buf, lse_buf, post_buf, mid_buf, middle,
        ) = call(
            attend_kernel,
            (now, place, starts, token_rows, incoming, wp_a, wp_b, wo_a, wo_b, vec_a),
            [SMEM, SMEM, SMEM] + [VMEM] * 7,
            (k_all, v_all, x_buf, h1_buf, q_buf, o_buf, lse_buf, post_buf, mid_buf),
            [VMEM, VMEM] + [HBM] * 7,
            [jax.ShapeDtypeStruct((chunk, width), F32)],
            [VMEM],
            [
                pltpu.VMEM((chunk, width), BF16), pltpu.VMEM((chunk, width), BF16),
                pltpu.VMEM((chunk, width), BF16), pltpu.VMEM((chunk, width), F32),
                pltpu.VMEM((128, chunk), F32), pltpu.VMEM((chunk, width), BF16),
                pltpu.VMEM((chunk, length), F32), dma((7,)),
            ],
            24 * 2**20,
            8 * dense * width,
        )
        h2_buf, g_buf, gp_buf, m_buf, st_buf, hid_buf, sent = call(
            expand_kernel,
            (now, place, middle, we_a, we_b, wr_a, wr_b, vec_f, wide_f),
            [SMEM, SMEM] + [VMEM] * 7,
            (h2_buf, g_buf, gp_buf, m_buf, st_buf, hid_buf),
            [HBM] * 6,
            [jax.ShapeDtypeStruct((chunk, width), BF16)],
            [VMEM],
            [
                pltpu.VMEM((chunk, width), BF16), pltpu.VMEM((chunk, units), F32),
                pltpu.VMEM((chunk, units), BF16), pltpu.VMEM((chunk, units), BF16),
                pltpu.VMEM((chunk, units), BF16), pltpu.VMEM((chunk, 128), F32), dma((6,)),
            ],
            24 * 2**20,
            2 * dense * units,
        )
        incoming = arriving

    wrt_a, wrt_b = flipped(wr_a), flipped(wr_b)
    wet_a, wet_b = flipped(we_a), flipped(we_b)
    wot_a, wot_b = flipped(wo_a), flipped(wo_b)
    wpt_a = jnp.stack([flipped(wp_a[i]) for i in range(3)])
    wpt_b = jnp.stack([flipped(wp_b[i]) for i in range(3)])
    sum_f = jnp.zeros((4, width), F32)
    sum_w = jnp.zeros((3, units), F32)
    sum_a = jnp.zeros((7, width), F32)
    incoming = blank
    sent = None
    for tick in range(ticks):
        now = jnp.full((1,), tick, jnp.int32)
        arriving = shifted(sent, -1) if sent is not None and tick + 1 < ticks else blank
        sum_f, sum_w, df_buf, dur_buf, dmr_buf, grad_mid = call(
            expand_back_kernel,
            (
                now, place, cotangent_rows, incoming, wrt_a, wrt_b, wet_a, wet_b, vec_f, wide_f,
                g_buf, gp_buf, st_buf, mid_buf,
            ),
            [SMEM, SMEM] + [VMEM] * 8 + [HBM] * 4,
            (sum_f, sum_w, df_buf, dur_buf, dmr_buf),
            [VMEM, VMEM] + [HBM] * 3,
            [jax.ShapeDtypeStruct((chunk, width), F32)],
            [VMEM],
            [
                pltpu.VMEM((chunk, units), BF16), pltpu.VMEM((chunk, units), BF16),
                pltpu.VMEM((chunk, 128), F32), pltpu.VMEM((chunk, width), F32),
                pltpu.VMEM((chunk, width), BF16), pltpu.VMEM((chunk, units), F32),
                pltpu.VMEM((chunk, units), BF16), pltpu.VMEM((chunk, width), BF16),
                dma((4,)), dma((3,)),
            ],
            24 * 2**20,
            2 * dense * units,
        )
        sum_a, dk_acc, dv_acc, dq_buf, dkr_buf, dvr_buf, ig_buf, sent = call(
            attend_back_kernel,
            (
                now, place, starts, grad_mid, wot_a, wot_b, wpt_a, wpt_b, vec_a, k_all, v_all,
                x_buf, q_buf, o_buf, lse_buf,
            ),
            [SMEM, SMEM, SMEM] + [VMEM] * 8 + [HBM] * 4,
            (sum_a, dk_acc, dv_acc, dq_buf, dkr_buf, dvr_buf, ig_buf),
            [VMEM, VMEM, VMEM] + [HBM] * 4,
            [jax.ShapeDtypeStruct((chunk, width), BF16)],
            [VMEM],
            [
                pltpu.VMEM((chunk, width), BF16), pltpu.VMEM((chunk, width), BF16),
                pltpu.VMEM((chunk, width), F32), pltpu.VMEM((128, chunk), F32),
                pltpu.VMEM((chunk, width), BF16), pltpu.VMEM((chunk, width), F32),
                pltpu.VMEM((length, chunk), F32), pltpu.VMEM((chunk, width), BF16),
                pltpu.VMEM((chunk, width), BF16), pltpu.VMEM((chunk, width), BF16),
                dma((4,)), dma((4,)),
            ],
            24 * 2**20,
            12 * dense * width,
        )
        incoming = arriving

    def weight_gradient(left, right, axis):
        whole = left.shape[1], right.shape[1]
        if paired:
            cut = whole[axis] // 2
            pieces = []
            for side in (1, 0):
                a, b = left, right
                if axis == 0:
                    a = left[:, side * cut:(side + 1) * cut]
                else:
                    b = right[:, side * cut:(side + 1) * cut]
                pieces.append(dot_tn(a, b))
            return (pieces[1] + swapped(pieces[0].astype(BF16)).astype(F32)).astype(BF16)
        full = dot_tn(left, right).astype(BF16)
        summed = lax.psum_scatter(full, "mp", scatter_dimension=axis, tiled=True)
        return (summed.astype(F32) * copies).astype(BF16)

    def over_batch(value):
        return lax.psum(value, "batch").astype(F32)

    reduce_grad = over_batch(weight_gradient(m_buf, df_buf, 0))
    expand_grad = over_batch(weight_gradient(h2_buf, dur_buf, 1))
    output_grad = weight_gradient(post_buf, dmr_buf, 0)
    project_grad = jnp.stack(
        [weight_gradient(h1_buf, right, 1) for right in (dq_buf, dkr_buf, dvr_buf)]
    )
    output_grad, project_grad = lax.psum((output_grad, project_grad), "batch")
    output_grad, project_grad = output_grad.astype(F32), project_grad.astype(F32)

    shared = jnp.stack([sum_a[5], sum_f[1], sum_a[6], sum_f[2], sum_f[3], sum_f[0]])
    narrow = jnp.stack([sum_a[3], sum_a[4], sum_a[2], sum_a[0], sum_a[1]])
    broad = jnp.stack([sum_w[2], sum_w[0], sum_w[1]])

    def packed(side):
        cut, wide_cut = width // 2, units // 2
        return jnp.concatenate(
            [
                shared.reshape(-1),
                narrow[:, side * cut:(side + 1) * cut].reshape(-1),
                broad[:, side * wide_cut:(side + 1) * wide_cut].reshape(-1),
            ]
        )

    if paired:
        small = lax.psum(owned_sum(packed(0), packed(1)), "batch")
        here, there = width // 2, units // 2
        shared = small[:6 * width].reshape(6, width)
        narrow = small[6 * width:6 * width + 5 * here].reshape(5, here)
        broad = small[6 * width + 5 * here:].reshape(3, there)
    else:
        small = lax.psum(
            jnp.concatenate([shared.reshape(-1), narrow.reshape(-1), broad.reshape(-1)]),
            ("batch", "mp"),
        ) * copies
        shared = small[:6 * width].reshape(6, width)
        narrow = small[6 * width:11 * width].reshape(5, width)
        broad = small[11 * width:].reshape(3, units)
        narrow = lax.dynamic_slice_in_dim(narrow, part * (width // parts), width // parts, 1)
        broad = lax.dynamic_slice_in_dim(broad, part * (units // parts), units // parts, 1)

    return (
        spread_rows(hid_buf)[None, None],
        spread_rows(ig_buf)[None, None],
        shared[0:2][None],
        shared[2:4][None],
        project_grad[None],
        narrow[0:2][None],
        jnp.sum(narrow[2].reshape(-1, head), axis=1)[None],
        narrow[3][None],
        narrow[4][None],
        output_grad[None],
        expand_grad[None],
        broad[0][None],
        broad[1][None],
        broad[2][None],
        reduce_grad[None],
        shared[4:6][None],
    )


def solution(mesh):
    layered = P("section", None, None)
    split = P("section", "mp")
    rows = P("section", "mp", None)
    columns = P("section", None, "mp")
    projected = P("section", None, None, "mp")
    tokens = P("batch", None, "mp", None)
    states = P("section", "batch", None, "mp", None)
    return jax.shard_map(
        local,
        mesh=mesh,
        in_specs=(
            tokens, tokens, P("batch", None, None, None), layered, layered, projected, columns,
            split, split, split, rows, columns, split, split, split, rows, layered,
        ),
        out_specs=(
            states, states, layered, layered, projected, columns, split, split, split, rows,
            columns, split, split, split, rows, layered,
        ),
        check_vma=False,
    )
```

```python
from functools import partial

import jax
import jax.numpy as jnp
from jax import lax
from jax.experimental import pallas as pl
from jax.experimental.pallas import tpu as pltpu
from jax.sharding import PartitionSpec as P

EPSILON = 1e-05
CHUNK = 128
KEYS = 256
TILE = 512
HIDE = -1e30
COSTS = (100, 15, 10, 5, 5)
LIMITS = tuple(size * 2**20 for size in (6, 8, 12, 10))
F32 = jnp.float32
BF16 = jnp.bfloat16
VMEM = pl.BlockSpec(memory_space=pltpu.VMEM)
SMEM = pl.BlockSpec(memory_space=pltpu.SMEM)
HBM = pl.BlockSpec(memory_space=pltpu.HBM)
ANY = pl.BlockSpec(memory_space=pl.ANY)


def lasts(microseconds):
    flops = int(microseconds * 1.1e9)
    return pl.CostEstimate(flops=flops, bytes_accessed=1024, transcendentals=0)


def dot_nn(left, right):
    return jnp.dot(left, right, preferred_element_type=F32)


def dot_nt(left, right):
    return lax.dot_general(left, right, (((1,), (1,)), ((), ())), preferred_element_type=F32)


def dot_tn(left, right):
    return lax.dot_general(left, right, (((0,), (0,)), ((), ())), preferred_element_type=F32)


def norm_parts(values):
    centre = values - jnp.mean(values, axis=-1, keepdims=True)
    inv_std = lax.rsqrt(jnp.mean(centre * centre, axis=-1, keepdims=True) + EPSILON)
    return centre * inv_std, inv_std


def norm_back(scaled, normed, inv_std):
    mean_one = jnp.mean(scaled, axis=-1, keepdims=True)
    mean_two = jnp.mean(scaled * normed, axis=-1, keepdims=True)
    return inv_std * (scaled - mean_one - normed * mean_two)


def column_sum(values):
    return jnp.sum(values, axis=0, keepdims=True)


def document_start(starts_ref, place):
    first = jnp.zeros_like(place)
    for k in range(starts_ref.shape[0]):
        start = starts_ref[k]
        first = jnp.maximum(first, jnp.where(place >= start, start, 0))
    return first


def half_masks():
    lane = lax.broadcasted_iota(jnp.int32, (1, 128), 1)
    return (lane < 64).astype(BF16), (lane >= 64).astype(BF16)


def stack_heads(pair):
    even, odd = half_masks()
    return jnp.concatenate([pair * even, pair * odd], axis=0)


def pick_heads(stacked):
    rows = stacked.shape[0] // 2
    lane = lax.broadcasted_iota(jnp.int32, (1, 128), 1)
    return jnp.where(lane < 64, stacked[:rows], stacked[rows:])


def copies_of(pairs, sems):
    return [pltpu.make_async_copy(a, b, sems.at[i]) for i, (a, b) in enumerate(pairs)]


def chunk_rows(place_ref, near_ref, far_ref, first, rows, into, sem):
    half = far_ref.shape[0]
    side = first // half
    inner = first - side * half

    @pl.when(side == place_ref[2])
    def _():
        at = pl.ds(pl.multiple_of(place_ref[3] + inner, rows), rows)
        copy = pltpu.make_async_copy(near_ref.at[at], into, sem)
        copy.start()
        copy.wait()

    @pl.when(side != place_ref[2])
    def _():
        at = pl.ds(pl.multiple_of(inner, rows), rows)
        copy = pltpu.make_async_copy(far_ref.at[at], into, sem)
        copy.start()
        copy.wait()


def row_of(pair, first, size):
    return jnp.concatenate(
        [pair[0][:, first:first + size], pair[1][:, first:first + size]], axis=1
    ).astype(F32)


def attend_kernel(
    tick_ref, section_ref, starts_ref, near_ref, far_ref, inc_ref, wp_a, wp_b, wo_a, wo_b,
    own_ref, other_ref, gain_ref, bias_ref, branch_ref,
    k_in, v_in, x_in, h1_in, q_in, o_in, lse_in, post_in, mid_in,
    k_ref, v_ref, x_buf, h1_buf, q_buf, o_buf, lse_buf, post_buf, mid_buf, mid_ref,
    x_s, h1_s, q_s, o_s, lse_s, post_s, hide_s, sems,
):
    del k_in, v_in, x_in, h1_in, q_in, o_in, lse_in, post_in, mid_in
    rows = mid_ref.shape[0]
    length, width = k_ref.shape
    half = width // 2
    section = section_ref[0]
    chunk = tick_ref[0] - 2 * section
    live = (chunk >= 0) & (chunk < length // rows)

    @pl.when(live)
    def _():
        first = pl.multiple_of(chunk * rows, rows)
        here = pl.ds(first, rows)

        @pl.when(section == 0)
        def _():
            chunk_rows(section_ref, near_ref, far_ref, first, rows, x_s, sems.at[0])

        @pl.when(section != 0)
        def _():
            x_s[...] = inc_ref[...]

        sent = []

        def send(source, target):
            copy = pltpu.make_async_copy(source, target, sems.at[len(sent)])
            copy.start()
            sent.append(copy)

        pair = (own_ref, other_ref)
        layer_in = x_s[...].astype(F32)
        send(x_s, x_buf.at[here])
        normed, _ = norm_parts(layer_in)
        h1 = (normed * gain_ref[0:1].astype(F32) + bias_ref[0:1].astype(F32)).astype(BF16)
        h1_s[...] = h1
        send(h1_s, h1_buf.at[here])
        for side, weight in ((0, wp_a), (1, wp_b)):
            at = slice(side * half, (side + 1) * half)
            q = (dot_nn(h1, weight[0]) + pair[side][:, :half].astype(F32)).astype(BF16)
            q_s[:, at] = q * jnp.asarray(0.125, BF16)
            k_ref[here, at] = dot_nn(h1, weight[1]).astype(BF16)
            value = dot_nn(h1, weight[2]) + pair[side][:, half:width].astype(F32)
            v_ref[here, at] = value.astype(BF16)
        send(q_s, q_buf.at[here])

        def attend(keys):
            place = first + lax.broadcasted_iota(jnp.int32, (rows, 1), 0)
            start = document_start(starts_ref, place)
            key_at = lax.broadcasted_iota(jnp.int32, (rows, keys), 1)
            hide_s[:, :keys] = jnp.where((key_at <= place) & (key_at >= start), 0.0, HIDE)
            lane = lax.broadcasted_iota(jnp.int32, (rows, 128), 1)

            def one_pair(pair, lse):
                at = pl.ds(pl.multiple_of(pair * 128, 128), 128)
                queries = stack_heads(q_s[:, at])
                hide = hide_s[:, :keys]
                scores = dot_nt(queries, k_ref[0:keys, at]) + jnp.concatenate([hide, hide], axis=0)
                top = jnp.max(scores, axis=-1, keepdims=True)
                raised = jnp.exp(scores - top)
                total = jnp.sum(raised, axis=-1, keepdims=True)
                out = dot_nn(raised.astype(BF16), v_ref[0:keys, at]) / total
                o_s[:, at] = pick_heads(out)
                now = top + jnp.log(total)
                lse = jnp.where(lane == 2 * pair, now[:rows], lse)
                return jnp.where(lane == 2 * pair + 1, now[rows:], lse)

            lse = lax.fori_loop(0, width // 128, one_pair, jnp.zeros((rows, 128), F32))
            lse_s[...] = lse.T

        for count in range(length // KEYS):

            @pl.when(first // KEYS == count)
            def _():
                attend((count + 1) * KEYS)

        send(o_s, o_buf.at[here])
        send(lse_s, lse_buf.at[chunk])
        post_normed, _ = norm_parts(o_s[...] * row_of(pair, 2 * half, half))
        post = post_normed * row_of(pair, 3 * half, half) + row_of(pair, 4 * half, half)
        post = post.astype(BF16)
        post_s[...] = post
        send(post_s, post_buf.at[here])
        mid_ref[...] = (
            x_s[...].astype(F32) + dot_nn(post[:, :half], wo_a[...])
            + dot_nn(post[:, half:], wo_b[...]) + branch_ref[0:1].astype(F32)
        )
        send(mid_ref, mid_buf.at[here])
        for copy in sent:
            copy.wait()


def gelu_parts(pre):
    phi = 0.5 + 0.5 * lax.erf(pre * 0.7071067811865476)
    density = jnp.exp(pre * pre * -0.5) * 0.3989422804014327
    return pre * phi, phi + pre * density


def expand_kernel(
    tick_ref, section_ref, mid_ref, we_a, we_b, wr_a, wr_b,
    own_ref, other_ref, gain_ref, bias_ref, branch_ref,
    h2_in, g_in, gp_in, m_in, st_in, keep_in, send_in,
    h2_buf, g_buf, gp_buf, m_buf, st_buf, keep_buf, send_buf, out_ref,
    h2_s, gf_s, g_s, gp_s, m_s, st_s, sems,
):
    del h2_in, g_in, gp_in, m_in, st_in, keep_in, send_in
    rows = mid_ref.shape[0]
    half = we_a.shape[1]
    units = 2 * half
    length = h2_buf.shape[0]
    chunk = tick_ref[0] - 2 * section_ref[0]

    @pl.when((chunk >= 0) & (chunk < length // rows))
    def _():
        here = pl.ds(pl.multiple_of(chunk * rows, rows), rows)
        sent = []

        def send(source, target):
            copy = pltpu.make_async_copy(source, target, sems.at[len(sent)])
            copy.start()
            sent.append(copy)

        def wide(tile, which):
            ref = own_ref if tile * TILE < half else other_ref
            first = 5 * mid_ref.shape[1] // 2 + which * half + tile * TILE % half
            return ref[:, first:first + TILE].astype(F32)

        normed, _ = norm_parts(mid_ref[...])
        h2 = (normed * gain_ref[1:2].astype(F32) + bias_ref[1:2].astype(F32)).astype(BF16)
        h2_s[...] = h2
        send(h2_s, h2_buf.at[here])
        total = jnp.zeros((rows, 1), F32)
        for tile in range(units // TILE):
            weight = we_a if tile * TILE < half else we_b
            inner = tile * TILE % half
            at = slice(tile * TILE, (tile + 1) * TILE)
            pre = dot_nn(h2, weight[:, inner:inner + TILE]) + wide(tile, 0)
            active, slope = gelu_parts(pre)
            gf_s[:, at] = active
            g_s[:, at] = active.astype(BF16)
            gp_s[:, at] = slope.astype(BF16)
            total += jnp.sum(active, axis=-1, keepdims=True)
        send(g_s, g_buf.at[here])
        send(gp_s, gp_buf.at[here])
        mean = total / units
        square = jnp.zeros((rows, 1), F32)
        for tile in range(units // TILE):
            centre = gf_s[:, tile * TILE:(tile + 1) * TILE] - mean
            square += jnp.sum(centre * centre, axis=-1, keepdims=True)
        inv_std = lax.rsqrt(square / units + EPSILON)
        lane = lax.broadcasted_iota(jnp.int32, (rows, 128), 1)
        st_s[...] = jnp.where(lane == 0, mean, inv_std)
        send(st_s, st_buf.at[here])
        out = mid_ref[...] + branch_ref[1:2].astype(F32)
        for tile in range(units // TILE):
            weight = wr_a if tile * TILE < half else wr_b
            inner = tile * TILE % half
            at = slice(tile * TILE, (tile + 1) * TILE)
            active = (gf_s[:, at] - mean) * inv_std * wide(tile, 1) + wide(tile, 2)
            active = active.astype(BF16)
            m_s[:, at] = active
            out += dot_nn(active, weight[inner:inner + TILE, :])
        send(m_s, m_buf.at[here])
        out_ref[...] = out.astype(BF16)
        state = (section_ref, keep_buf, send_buf, chunk * rows, out_ref, sems.at[5])
        store_rows(*state, "start")
        for copy in sent:
            copy.wait()
        store_rows(*state, "wait")


def expand_back_kernel(
    tick_ref, section_ref, near_ref, far_ref, inc_ref, wr_a, wr_b, we_a, we_b,
    own_ref, other_ref, gain_ref,
    g_buf, gp_buf, st_buf, mid_buf,
    sum_in, wsum_in, df_in, dur_in, dmr_in,
    sum_ref, wsum_ref, df_buf, dur_buf, dmr_buf, dmid_ref,
    g_s, gp_s, st_s, mid_s, df_s, z_s, dur_s, dmr_s, in_sems, out_sems,
):
    del sum_in, wsum_in, df_in, dur_in, dmr_in
    rows = dmid_ref.shape[0]
    half = wr_a.shape[1]
    units = 2 * half
    length = g_buf.shape[0]
    count = length // rows
    section = section_ref[0]
    last = section_ref[1] - 1
    chunk = count - 1 - (tick_ref[0] - 2 * (last - section))

    @pl.when((chunk >= 0) & (chunk < count))
    def _():
        here = pl.ds(pl.multiple_of(chunk * rows, rows), rows)
        loads = copies_of(
            (
                (g_buf.at[here], g_s), (gp_buf.at[here], gp_s), (st_buf.at[here], st_s),
                (mid_buf.at[here], mid_s),
            ),
            in_sems,
        )
        for copy in loads:
            copy.start()

        @pl.when(section == last)
        def _():
            chunk_rows(
                section_ref, near_ref, far_ref, chunk * rows, rows, df_s, out_sems.at[0]
            )

        @pl.when(section != last)
        def _():
            df_s[...] = inc_ref[...]

        sent = []

        def send(source, target):
            copy = pltpu.make_async_copy(source, target, out_sems.at[len(sent)])
            copy.start()
            sent.append(copy)

        def gain_of(tile):
            ref = own_ref if tile * TILE < half else other_ref
            first = 5 * dmid_ref.shape[1] // 2 + half + tile * TILE % half
            return ref[:, first:first + TILE].astype(F32)

        grad_low = df_s[...]
        send(df_s, df_buf.at[here])
        sum_ref[0:1] += column_sum(grad_low.astype(F32))
        for copy in loads:
            copy.wait()
        mean = st_s[:, 0:1]
        inv_std = st_s[:, 1:2]
        one = jnp.zeros((rows, 1), F32)
        two = jnp.zeros((rows, 1), F32)
        for tile in range(units // TILE):
            weight = wr_a if tile * TILE < half else wr_b
            inner = tile * TILE % half
            at = slice(tile * TILE, (tile + 1) * TILE)
            grad = dot_nn(grad_low, weight[:, inner:inner + TILE])
            normed = (g_s[:, at].astype(F32) - mean) * inv_std
            wsum_ref[0:1, at] += column_sum(grad * normed)
            wsum_ref[1:2, at] += column_sum(grad)
            scaled = grad * gain_of(tile)
            z_s[:, at] = scaled
            one += jnp.sum(scaled, axis=-1, keepdims=True)
            two += jnp.sum(scaled * normed, axis=-1, keepdims=True)
        one = one / units
        two = two / units
        grad_second = jnp.zeros((rows, dmid_ref.shape[1]), F32)
        for tile in range(units // TILE):
            weight = we_a if tile * TILE < half else we_b
            inner = tile * TILE % half
            at = slice(tile * TILE, (tile + 1) * TILE)
            normed = (g_s[:, at].astype(F32) - mean) * inv_std
            grad = inv_std * (z_s[:, at] - one - normed * two) * gp_s[:, at].astype(F32)
            wsum_ref[2:3, at] += column_sum(grad)
            low = grad.astype(BF16)
            dur_s[:, at] = low
            grad_second += dot_nn(low, weight[inner:inner + TILE, :])
        send(dur_s, dur_buf.at[here])
        normed, inv_std = norm_parts(mid_s[...])
        sum_ref[1:2] += column_sum(grad_second * normed)
        sum_ref[2:3] += column_sum(grad_second)
        grad_mid = grad_low.astype(F32) + norm_back(
            grad_second * gain_ref[1:2].astype(F32), normed, inv_std
        )
        sum_ref[3:4] += column_sum(grad_mid)
        dmid_ref[...] = grad_mid
        dmr_s[...] = grad_mid.astype(BF16)
        send(dmr_s, dmr_buf.at[here])
        for copy in sent:
            copy.wait()


def attend_back_kernel(
    tick_ref, section_ref, starts_ref, after, dmid_ref, wo_a, wo_b, wp_a, wp_b,
    own_ref, other_ref, gain_ref, k_ref, v_ref,
    x_buf, q_buf, o_buf, lse_buf,
    sum_in, dk_in, dv_in, dq_in, dkr_in, dvr_in, keep_in, send_in,
    sum_ref, dk_ref, dv_ref, dq_buf, dkr_buf, dvr_buf, keep_buf, send_buf, out_ref,
    x_s, q_s, o_s, lse_s, do_s, dqf_s, hide_s, dq_s, dkr_s, dvr_s, in_sems, out_sems,
):
    del after, sum_in, dk_in, dv_in, dq_in, dkr_in, dvr_in, keep_in, send_in
    rows = dmid_ref.shape[0]
    length, width = k_ref.shape
    half = width // 2
    count = length // rows
    section = section_ref[0]
    last = section_ref[1] - 1
    chunk = count - 1 - (tick_ref[0] - 2 * (last - section))

    @pl.when((chunk >= 0) & (chunk < count))
    def _():
        first = pl.multiple_of(chunk * rows, rows)
        here = pl.ds(first, rows)
        loads = copies_of(
            (
                (x_buf.at[here], x_s), (q_buf.at[here], q_s), (o_buf.at[here], o_s),
                (lse_buf.at[chunk], lse_s),
            ),
            in_sems,
        )
        for copy in loads:
            copy.start()

        @pl.when(chunk == count - 1)
        def _():
            dk_ref[...] = jnp.zeros_like(dk_ref)
            dv_ref[...] = jnp.zeros_like(dv_ref)

        low = dmid_ref[...].astype(BF16)
        grad_post = jnp.concatenate([dot_nn(low, wo_a[...]), dot_nn(low, wo_b[...])], axis=1)
        for copy in loads:
            copy.wait()
        attended = o_s[...]
        pair_refs = (own_ref, other_ref)
        scale = row_of(pair_refs, 2 * half, half)
        normed, inv_std = norm_parts(attended * scale)
        sum_ref[0:1] += column_sum(grad_post * normed)
        sum_ref[1:2] += column_sum(grad_post)
        grad_mixed = norm_back(grad_post * row_of(pair_refs, 3 * half, half), normed, inv_std)
        sum_ref[2:3] += column_sum(grad_mixed * attended)
        do_s[...] = (grad_mixed * scale).astype(BF16)

        def attend(keys):
            place = first + lax.broadcasted_iota(jnp.int32, (1, rows), 1)
            start = document_start(starts_ref, place)
            key_at = lax.broadcasted_iota(jnp.int32, (keys, rows), 0)
            hide_s[:keys, :] = jnp.where((key_at <= place) & (key_at >= start), 0.0, HIDE)

            def one_pair(pair, carry):
                at = pl.ds(pl.multiple_of(pair * 128, 128), 128)
                queries = stack_heads(q_s[:, at])
                grad_pair = do_s[:, at]
                grads = stack_heads(grad_pair)
                product = (grad_pair.astype(F32) * o_s[:, at]).T
                delta = jnp.concatenate(
                    [column_sum(product[:64]), column_sum(product[64:])], axis=1
                )
                lse = jnp.concatenate(
                    [lse_s[pl.ds(2 * pair, 1), :], lse_s[pl.ds(2 * pair + 1, 1), :]], axis=1
                )
                hide = hide_s[:keys, :]
                key_pair = k_ref[0:keys, at]
                scores = dot_nt(key_pair, queries) + jnp.concatenate([hide, hide], axis=1)
                probs = jnp.exp(scores - lse)
                grad_probs = dot_nt(v_ref[0:keys, at], grads)
                grad_scores = (probs * (grad_probs - delta)).astype(BF16)
                dk_ref[0:keys, at] += dot_nn(grad_scores, queries)
                dv_ref[0:keys, at] += dot_nn(probs.astype(BF16), grads)
                dqf_s[:, at] = pick_heads(dot_tn(grad_scores, key_pair)) * 0.125
                return carry

            lax.fori_loop(0, width // 128, one_pair, 0)

        for number in range(length // KEYS):

            @pl.when(first // KEYS == number)
            def _():
                attend((number + 1) * KEYS)

        sent = []

        def send(source, target):
            copy = pltpu.make_async_copy(source, target, out_sems.at[len(sent)])
            copy.start()
            sent.append(copy)

        grad_query = dqf_s[...]
        grad_value = dv_ref[here, :]
        sum_ref[3:4] += column_sum(grad_query)
        sum_ref[4:5] += column_sum(grad_value)
        dq_s[...] = grad_query.astype(BF16)
        dkr_s[...] = dk_ref[here, :].astype(BF16)
        dvr_s[...] = grad_value.astype(BF16)
        send(dq_s, dq_buf.at[here])
        send(dkr_s, dkr_buf.at[here])
        send(dvr_s, dvr_buf.at[here])
        grad_first = jnp.zeros((rows, width), F32)
        for number, part in enumerate((dq_s, dkr_s, dvr_s)):
            grad_first += dot_nn(part[:, :half], wp_a[number])
            grad_first += dot_nn(part[:, half:], wp_b[number])
        normed, inv_std = norm_parts(x_s[...].astype(F32))
        sum_ref[5:6] += column_sum(grad_first * normed)
        sum_ref[6:7] += column_sum(grad_first)
        out = dmid_ref[...] + norm_back(
            grad_first * gain_ref[0:1].astype(F32), normed, inv_std
        )
        out_ref[...] = out.astype(BF16)
        state = (section_ref, keep_buf, send_buf, first, out_ref, out_sems.at[3])
        store_rows(*state, "start")
        for copy in sent:
            copy.wait()
        store_rows(*state, "wait")


def flip_kernel(first, second, after, first_out, second_out):
    del after
    size = 256
    for source, target in ((first, first_out), (second, second_out)):
        numbers = range(source.shape[0]) if len(source.shape) == 3 else (None,)
        for number in numbers:
            one = source if number is None else source.at[number]
            two = target if number is None else target.at[number]

            def body(step, carry, one=one, two=two):
                at = pl.ds(pl.multiple_of(step * size, size), size)
                two[:, at] = one[at, :].T
                return carry

            lax.fori_loop(0, one.shape[0] // size, body, 0)


def flipped(first, second, after):
    shape = first.shape[:-2] + (first.shape[-1], first.shape[-2])
    return pl.pallas_call(
        flip_kernel,
        in_specs=[VMEM] * 2 + [ANY],
        out_specs=[VMEM] * 2,
        out_shape=[pltpu.VMEM(shape, BF16)] * 2,
        compiler_params=pltpu.CompilerParams(vmem_limit_bytes=2 * 2**20),
    )(first, second, after)


def load_kernel(source, after, target, sem):
    del after
    copy = pltpu.make_async_copy(source, target, sem)
    copy.start()
    copy.wait()


def loaded(value, after):
    return pl.pallas_call(
        load_kernel,
        in_specs=[HBM, ANY],
        out_specs=VMEM,
        out_shape=pltpu.VMEM(value.shape, value.dtype),
        scratch_shapes=[pltpu.SemaphoreType.DMA],
        compiler_params=pltpu.CompilerParams(vmem_limit_bytes=2**20),
    )(pltpu.with_memory_space_constraint(value, pltpu.HBM), after)


def empty_kernel(*refs):
    del refs


def empty(shapes, space, *after):
    return pl.pallas_call(
        empty_kernel,
        in_specs=[ANY] * len(after),
        out_specs=[pl.BlockSpec(memory_space=space)] * len(shapes),
        out_shape=[space(shape, dtype) for shape, dtype in shapes],
        compiler_params=pltpu.CompilerParams(vmem_limit_bytes=2**20),
    )(*after)


def call(kernel, inputs, specs, carried, carried_specs, fresh, fresh_specs, scratch, limit, flops):
    first = len(inputs)
    inputs = [
        pltpu.with_memory_space_constraint(a, pltpu.HBM) if spec is HBM else a
        for a, spec in zip(inputs, specs)
    ]
    shapes = [
        pltpu.HBM(a.shape, a.dtype) if spec is HBM else jax.ShapeDtypeStruct(a.shape, a.dtype)
        for a, spec in zip(carried, carried_specs)
    ] + fresh
    return pl.pallas_call(
        kernel,
        in_specs=specs + carried_specs,
        out_specs=carried_specs + fresh_specs,
        out_shape=shapes,
        scratch_shapes=scratch,
        input_output_aliases={first + i: i for i in range(len(carried))},
        compiler_params=pltpu.CompilerParams(vmem_limit_bytes=limit),
        cost_estimate=pl.CostEstimate(flops=flops, bytes_accessed=2**22, transcendentals=0),
    )(*inputs, *carried)


def settle_kernel(place_ref, *refs):
    pieces, (*outs, wide_s, turn_s, sems) = refs[:8], refs[8:]
    rows = pieces[0].shape[0]
    low, high = place_ref[4], place_ref[5]
    copies = []
    for number, piece in enumerate(pieces):
        half, flips = number // 4, number % 4
        first = (low, high)[half] ^ (flips // 2)
        second = (high, low)[half] ^ (flips % 2)
        slot = number % 2
        if number >= 2:
            for copy in copies[number - 2]:
                copy.wait()
        wide_s[slot] = piece[...].astype(F32)
        at = pl.ds(pl.multiple_of((half * 4 + first * 2 + second) * rows, rows), rows)
        moves = []
        if len(outs) == 1:
            moves.append((wide_s.at[slot], outs[0].at[at]))
        else:
            layers, _, columns = outs[0].shape
            for layer in range(layers):
                source = wide_s.at[slot, :, layer * columns:(layer + 1) * columns]
                moves.append((source, outs[0].at[layer, at]))
            turn_s[slot] = wide_s[slot, :, layers * columns:].T
            moves.append((turn_s.at[slot], outs[1].at[:, at]))
        started = [
            pltpu.make_async_copy(source, target, sems.at[slot, i])
            for i, (source, target) in enumerate(moves)
        ]
        for copy in started:
            copy.start()
        copies.append(started)
    for copy in copies[6] + copies[7]:
        copy.wait()


def settle(place, pieces, shapes, after, cost):
    rows, columns = pieces[0].shape
    turn = (2, shapes[1][0], rows) if len(shapes) > 1 else (2, 8, 128)

    def kernel(place_ref, *refs):
        settle_kernel(place_ref, *refs[:8], *refs[9:])

    return pl.pallas_call(
        kernel,
        grid=(1,),
        in_specs=[SMEM]
        + [pl.BlockSpec((rows, columns), lambda i: (0, 0), pipeline_mode=pl.Buffered(1))] * 8
        + [HBM],
        out_specs=[HBM] * len(shapes),
        out_shape=[pltpu.HBM(shape, F32) for shape in shapes],
        scratch_shapes=[
            pltpu.VMEM((2, rows, columns), F32), pltpu.VMEM(turn, F32),
            pltpu.SemaphoreType.DMA((2, 4)),
        ],
        compiler_params=pltpu.CompilerParams(vmem_limit_bytes=14 * 2**20),
        cost_estimate=lasts(cost),
    )(place, *pieces, *in_hbm([after]))


def crossed(value, bit):
    route = [(i, i ^ bit) for i in range(lax.axis_size("batch"))]
    return lax.ppermute(value, "batch", route)


def in_hbm(values):
    return [pltpu.with_memory_space_constraint(value, pltpu.HBM) for value in values]


def product(lefts, rights, pairs, columns, number):
    left = lefts[pairs[number]][...]
    return slice(number * columns, (number + 1) * columns), dot_tn(left, rights[number][...])


def other_part(lefts, rights, pairs, axis, after, cost=1):
    length = lefts[0].shape[0]
    rows = lefts[0].shape[1] // (2 if axis == 0 else 1)
    columns = rights[0].shape[1] // (1 if axis == 0 else 2)
    tile = rows // 4
    skip = 4 if axis == 0 else 0
    side = 0 if axis == 0 else 1

    def kernel(*refs):
        for number in range(len(rights)):
            at, value = product(
                refs[:len(lefts)], refs[len(lefts):], pairs, columns, number
            )
            refs[-1][:, at] = value.astype(BF16)

    return pl.pallas_call(
        kernel,
        grid=(rows // tile,),
        in_specs=[pl.BlockSpec((length, tile), lambda i: (0, skip + i))] * len(lefts)
        + [pl.BlockSpec((length, columns), lambda i: (0, side), pipeline_mode=pl.Buffered(1))]
        * len(rights)
        + [HBM],
        out_specs=pl.BlockSpec((tile, columns * len(rights)), lambda i: (i, 0)),
        out_shape=pltpu.HBM((rows, columns * len(rights)), BF16),
        compiler_params=pltpu.CompilerParams(vmem_limit_bytes=14 * 2**20),
        cost_estimate=lasts(cost),
    )(*in_hbm(lefts), *in_hbm(rights), *in_hbm([after]))


def own_part(lefts, rights, pairs, come, place, after, cost=1):
    length = lefts[0].shape[0]
    rows, whole = come.shape
    columns = whole // len(rights)
    tile = rows // 4

    def at(i, place):
        low, high = place[4], place[5]
        first = jnp.where(i == 0, 1 - low, 3 - high)
        return jnp.where(i < 2, first, jnp.where(i == 2, low, 2 + high))

    def kernel(place_ref, *refs):
        del place_ref
        come_ref, outs = refs[len(lefts) + len(rights)], refs[-4:]
        for number in range(len(rights)):
            where, value = product(
                refs[:len(lefts)], refs[len(lefts):], pairs, columns, number
            )
            low = (value + come_ref[:, where].astype(F32)).astype(BF16)
            for step, out in enumerate(outs):

                @pl.when(pl.program_id(0) == step)
                def _():
                    out[:, where] = low

    return pl.pallas_call(
        kernel,
        grid_spec=pltpu.PrefetchScalarGridSpec(
            num_scalar_prefetch=1,
            grid=(4,),
            in_specs=[pl.BlockSpec((length, tile), lambda i, place: (0, at(i, place)))]
            * len(lefts)
            + [
                pl.BlockSpec(
                    (length, columns), lambda i, place: (0, 0), pipeline_mode=pl.Buffered(1)
                )
            ]
            * len(rights)
            + [pl.BlockSpec((tile, whole), lambda i, place: (at(i, place), 0)), HBM],
            out_specs=[pl.BlockSpec((tile, whole), lambda i, place: (0, 0))] * 4,
        ),
        out_shape=[pltpu.HBM((tile, whole), BF16)] * 4,
        compiler_params=pltpu.CompilerParams(vmem_limit_bytes=20 * 2**20),
        cost_estimate=lasts(cost),
    )(place, *in_hbm(lefts), *in_hbm(rights), come, *in_hbm([after]))


def add_kernel(split, place_ref, *refs):
    keeps, comes = (refs[0], refs[2]), (refs[1], refs[3])
    outs = refs[5:]
    for half, bit in ((0, 5), (1, 4)):
        keep, come = keeps[half], comes[half]
        if split:
            rows = keep.shape[0] // 2
            side = place_ref[bit]
            for number, where in ((0, 1 - side), (1, side)):
                at = pl.ds(pl.multiple_of(where * rows, rows), rows)
                outs[2 * half + number][...] = (
                    keep[at, :].astype(F32) + come[at, :].astype(F32)
                ).astype(BF16)
        else:
            outs[half][...] = (keep[...].astype(F32) + come[...].astype(F32)).astype(BF16)


def added(keeps, comes, place, split, after, cost):
    rows, columns = keeps[0].shape
    kept = rows // 2 if split else rows
    count = 4 if split else 2
    return pl.pallas_call(
        partial(add_kernel, split),
        grid=(1,),
        in_specs=[SMEM]
        + [pl.BlockSpec((rows, columns), lambda i: (0, 0), pipeline_mode=pl.Buffered(1))] * 4
        + [HBM],
        out_specs=[
            pl.BlockSpec((kept, columns), lambda i: (0, 0), pipeline_mode=pl.Buffered(1))
        ]
        * count,
        out_shape=[pltpu.HBM((kept, columns), BF16)] * count,
        compiler_params=pltpu.CompilerParams(vmem_limit_bytes=12 * 2**20),
        cost_estimate=lasts(cost),
    )(place, keeps[0], comes[0], keeps[1], comes[1], *in_hbm([after]))


class BatchSum:
    def __init__(self, pieces, place):
        send_a, send_b, keep_a, keep_b = pieces
        self.place = place
        self.keeps = keep_a, keep_b
        self.comes = crossed(send_a, 1), crossed(send_b, 2)

    def second(self, after, cost):
        send_a, keep_a, send_b, keep_b = added(self.keeps, self.comes, self.place, True, after, cost)
        self.keeps = keep_a, keep_b
        self.comes = crossed(send_a, 2), crossed(send_b, 1)
        return keep_a

    def third(self, after, cost):
        a, b = added(self.keeps, self.comes, self.place, False, after, cost)
        across_a, across_b = crossed(a, 2), crossed(b, 1)
        self.pieces = [
            a, across_a, crossed(a, 1), crossed(across_a, 1),
            b, across_b, crossed(b, 2), crossed(across_b, 2),
        ]
        return a

    def result(self, shapes, after, cost=1):
        return settle(self.place, self.pieces, shapes, after, cost)


def keep_kernel(place_ref, come_ref, in_ref, out_ref, sem):
    del in_ref
    copy = pltpu.make_async_copy(come_ref, out_ref.at[1 - place_ref[2]], sem)
    copy.start()
    copy.wait()


def with_other_half(kept, come, place, after):
    def kernel(place_ref, come_ref, after_ref, *refs):
        keep_kernel(place_ref, come_ref, *refs)

    return pl.pallas_call(
        kernel,
        in_specs=[SMEM, VMEM, HBM, HBM],
        out_specs=HBM,
        out_shape=pltpu.HBM(kept.shape, kept.dtype),
        scratch_shapes=[pltpu.SemaphoreType.DMA],
        compiler_params=pltpu.CompilerParams(vmem_limit_bytes=4 * 2**20),
        input_output_aliases={3: 0},
        cost_estimate=lasts(3),
    )(place, come, *in_hbm([after]), kept)


def plus_kernel(one, two, after, out):
    del after
    out[...] = one[...] + two[...]


def plus(one, two, after):
    return pl.pallas_call(
        plus_kernel,
        in_specs=[VMEM, VMEM, HBM],
        out_specs=VMEM,
        out_shape=jax.ShapeDtypeStruct(one.shape, one.dtype),
        compiler_params=pltpu.CompilerParams(vmem_limit_bytes=2**20),
        cost_estimate=lasts(1),
    )(one, two, *in_hbm([after]))


def store_rows(place_ref, keep_buf, send_buf, first, source, sem, back):
    rows = source.shape[0]
    half = send_buf.shape[0]
    side = first // half
    at = pl.ds(pl.multiple_of(first - side * half, rows), rows)

    @pl.when(side == place_ref[2])
    def _():
        copy = pltpu.make_async_copy(source, keep_buf.at[side, at], sem)
        getattr(copy, back)()

    @pl.when(side != place_ref[2])
    def _():
        copy = pltpu.make_async_copy(source, send_buf.at[at], sem)
        getattr(copy, back)()


def local(
    tokens, cotangent, document_starts, pre_gain, pre_bias, project_weight, project_bias,
    head_scale, post_gain, post_bias, output_weight, expand_weight, expand_bias, middle_gain,
    middle_bias, reduce_weight, branch_bias,
):
    sections = lax.axis_size("section")
    section = lax.axis_index("section")
    parts = lax.axis_size("mp")
    part = lax.axis_index("mp")
    shard = lax.axis_index("batch")
    micro, rows_here, width = tokens.shape[1:]
    length = rows_here * parts
    chunk = CHUNK
    count = length // chunk
    head = width // (head_scale.shape[1] * parts)
    units = expand_bias.shape[1] * parts
    paired = parts == 2 and micro == 2
    by_links = paired and lax.axis_size("batch") == 4
    block = part * micro // parts
    copies = micro / parts

    def swapped(value):
        return lax.ppermute(value, "mp", [(0, 1), (1, 0)])

    def both(value, axis):
        if paired:
            return value, swapped(value)
        whole = lax.all_gather(value, "mp", axis=axis, tiled=True)
        return tuple(jnp.split(whole, 2, axis=axis))

    def row_source(value):
        if paired:
            theirs = lax.dynamic_index_in_dim(value, 1 - part, 0, keepdims=False)
            return value.reshape(micro * rows_here, width), swapped(theirs)
        whole = lax.all_gather(value, "mp", axis=1, tiled=True)
        whole = lax.dynamic_index_in_dim(whole, block, 0, keepdims=False)
        return whole[:length // 2], whole[length // 2:]

    def spread_rows(kept, sent, after):
        if paired:
            return with_other_half(kept, swapped(sent), place, after)
        whole = lax.all_gather(jnp.concatenate([kept[0], sent]), "mp", axis=0)[:: parts // micro]
        return lax.dynamic_slice_in_dim(whole, part * rows_here, rows_here, 1)

    near_tokens, far_tokens = row_source(tokens[0])
    place = jnp.stack(
        [
            section, jnp.int32(sections), part if paired else jnp.int32(0),
            part * rows_here if paired else jnp.int32(0), shard % 2, shard // 2,
        ]
    ).astype(jnp.int32)
    starts = lax.dynamic_index_in_dim(document_starts[0], block, 0, keepdims=False)[0]
    fields = (
        project_bias[0, 0], project_bias[0, 1], jnp.repeat(head_scale[0], head), post_gain[0],
        post_bias[0], expand_bias[0], middle_gain[0], middle_bias[0],
    )
    if paired:
        own = jnp.concatenate(fields)[None]
        other = swapped(own)
    else:
        sides = [both(field, 0) for field in fields]
        own = jnp.concatenate([a for a, _ in sides])[None]
        other = jnp.concatenate([b for _, b in sides])[None]
    gains, biases, branches = pre_gain[0], pre_bias[0], branch_bias[0]
    wp_a, wp_b = both(project_weight[0], 2)
    wo_a, wo_b = both(output_weight[0], 0)
    we_a, we_b = both(expand_weight[0], 1)
    wr_a, wr_b = both(reduce_weight[0], 0)
    wp_a = loaded(wp_a, place)
    wo_a = loaded(wo_a, wp_a)
    we_a = loaded(we_a, wo_a)
    wr_a = loaded(wr_a, we_a)
    wp_b = loaded(wp_b, wr_a)
    wo_b = loaded(wo_b, wp_b)
    we_b = loaded(we_b, wo_b)
    wr_b = loaded(wr_b, we_b)
    near_cotangent, far_cotangent = row_source(cotangent[0])

    def sized(columns, dtype):
        return ((length, columns), dtype)

    halves = (((2, length // 2, width), BF16), ((length // 2, width), BF16))

    (
        x_buf, h1_buf, q_buf, o_buf, lse_buf, post_buf, mid_buf,
        h2_buf, g_buf, gp_buf, m_buf, st_buf, hid_keep, hid_send,
        df_buf, dur_buf, dmr_buf, dq_buf, dkr_buf, dvr_buf, ig_keep, ig_send,
    ) = empty(
        [
            sized(width, BF16), sized(width, BF16), sized(width, BF16), sized(width, F32),
            ((count, 128, chunk), F32), sized(width, BF16), sized(width, F32),
            sized(width, BF16), sized(units, BF16), sized(units, BF16), sized(units, BF16),
            sized(128, F32), *halves,
            sized(width, BF16), sized(units, BF16), sized(width, BF16), sized(width, BF16),
            sized(width, BF16), sized(width, BF16), *halves,
        ],
        pltpu.HBM,
    )
    k_all = jnp.zeros((length, width), BF16)
    v_all = jnp.zeros((length, width), BF16)
    dma = pltpu.SemaphoreType.DMA
    dense = 2 * chunk * width

    def shifted(value, distance):
        route = [(i, i + distance) for i in range(sections) if 0 <= i + distance < sections]
        return lax.ppermute(value, "section", route)

    ticks = count + 2 * (sections - 1)
    blank = jnp.zeros((chunk, width), BF16)
    incoming = blank
    sent = None
    for tick in range(ticks):
        now = jnp.full((1,), tick, jnp.int32)
        arriving = shifted(sent, 1) if sent is not None and tick + 1 < ticks else blank
        (
            k_all, v_all, x_buf, h1_buf, q_buf, o_buf, lse_buf, post_buf, mid_buf, middle,
        ) = call(
            attend_kernel,
            (
                now, place, starts, near_tokens, far_tokens, incoming, wp_a, wp_b, wo_a, wo_b,
                own, other, gains, biases, branches,
            ),
            [SMEM, SMEM, SMEM, HBM, HBM] + [VMEM] * 10,
            (k_all, v_all, x_buf, h1_buf, q_buf, o_buf, lse_buf, post_buf, mid_buf),
            [VMEM, VMEM] + [HBM] * 7,
            [jax.ShapeDtypeStruct((chunk, width), F32)],
            [VMEM],
            [
                pltpu.VMEM((chunk, width), BF16), pltpu.VMEM((chunk, width), BF16),
                pltpu.VMEM((chunk, width), BF16), pltpu.VMEM((chunk, width), F32),
                pltpu.VMEM((128, chunk), F32), pltpu.VMEM((chunk, width), BF16),
                pltpu.VMEM((chunk, length), F32), dma((7,)),
            ],
            LIMITS[0],
            8 * dense * width,
        )
        h2_buf, g_buf, gp_buf, m_buf, st_buf, hid_keep, hid_send, sent = call(
            expand_kernel,
            (
                now, place, middle, we_a, we_b, wr_a, wr_b, own, other, gains, biases, branches,
            ),
            [SMEM, SMEM] + [VMEM] * 10,
            (h2_buf, g_buf, gp_buf, m_buf, st_buf, hid_keep, hid_send),
            [HBM] * 7,
            [jax.ShapeDtypeStruct((chunk, width), BF16)],
            [VMEM],
            [
                pltpu.VMEM((chunk, width), BF16), pltpu.VMEM((chunk, units), F32),
                pltpu.VMEM((chunk, units), BF16), pltpu.VMEM((chunk, units), BF16),
                pltpu.VMEM((chunk, units), BF16), pltpu.VMEM((chunk, 128), F32), dma((6,)),
            ],
            LIMITS[1],
            2 * dense * units,
        )
        incoming = arriving

    wrt_a, wrt_b = flipped(wr_a, wr_b, sent)
    wet_a, wet_b = flipped(we_a, we_b, wrt_a)
    wot_a, wot_b = flipped(wo_a, wo_b, wet_a)
    wpt_a, wpt_b = flipped(wp_a, wp_b, wot_a)
    dk_acc, dv_acc = empty([sized(width, F32)] * 2, pltpu.VMEM, wpt_a)
    sum_f = jnp.zeros((4, width), F32)
    sum_w = jnp.zeros((3, units), F32)
    sum_a = jnp.zeros((7, width), F32)
    incoming = blank
    sent = None

    def weight_gradient(left, right, axis):
        full = dot_tn(left, right).astype(BF16)
        total = lax.psum_scatter(full, "mp", scatter_dimension=axis, tiled=True)
        return (total.astype(F32) * copies).astype(BF16)

    def attend_back(now, after, grad_mid, carried, cost=10):
        return call(
            attend_back_kernel,
            (
                now, place, starts, after, grad_mid, wot_a, wot_b, wpt_a, wpt_b, own, other, gains,
                k_all, v_all, x_buf, q_buf, o_buf, lse_buf,
            ),
            [SMEM, SMEM, SMEM, HBM] + [VMEM] * 10 + [HBM] * 4,
            carried,
            [VMEM, VMEM, VMEM] + [HBM] * 5,
            [jax.ShapeDtypeStruct((chunk, width), BF16)],
            [VMEM],
            [
                pltpu.VMEM((chunk, width), BF16), pltpu.VMEM((chunk, width), BF16),
                pltpu.VMEM((chunk, width), F32), pltpu.VMEM((128, chunk), F32),
                pltpu.VMEM((chunk, width), BF16), pltpu.VMEM((chunk, width), F32),
                pltpu.VMEM((length, chunk), F32), pltpu.VMEM((chunk, width), BF16),
                pltpu.VMEM((chunk, width), BF16), pltpu.VMEM((chunk, width), BF16),
                dma((4,)), dma((4,)),
            ],
            LIMITS[3],
            cost * 11 * 10**8,
        )

    held = []
    carried = (sum_a, dk_acc, dv_acc, dq_buf, dkr_buf, dvr_buf, ig_keep, ig_send)
    for tick in range(ticks):
        now = jnp.full((1,), tick, jnp.int32)
        arriving = shifted(sent, -1) if sent is not None and tick + 1 < ticks else blank
        sum_f, sum_w, df_buf, dur_buf, dmr_buf, grad_mid = call(
            expand_back_kernel,
            (
                now, place, near_cotangent, far_cotangent, incoming, wrt_a, wrt_b, wet_a, wet_b,
                own, other, gains, g_buf, gp_buf, st_buf, mid_buf,
            ),
            [SMEM, SMEM, HBM, HBM] + [VMEM] * 8 + [HBM] * 4,
            (sum_f, sum_w, df_buf, dur_buf, dmr_buf),
            [VMEM, VMEM] + [HBM] * 3,
            [jax.ShapeDtypeStruct((chunk, width), F32)],
            [VMEM],
            [
                pltpu.VMEM((chunk, units), BF16), pltpu.VMEM((chunk, units), BF16),
                pltpu.VMEM((chunk, 128), F32), pltpu.VMEM((chunk, width), F32),
                pltpu.VMEM((chunk, width), BF16), pltpu.VMEM((chunk, units), F32),
                pltpu.VMEM((chunk, units), BF16), pltpu.VMEM((chunk, width), BF16),
                dma((4,)), dma((3,)),
            ],
            LIMITS[2],
            2 * dense * units,
        )
        held.append((now, grad_mid))
        if tick + 2 < ticks:
            held.clear()
            *carried, sent = attend_back(now, x_buf, grad_mid, carried)
        incoming = arriving
    def gathered(sum_a):
        shared = jnp.stack([sum_a[5], sum_f[1], sum_a[6], sum_f[2], sum_f[3], sum_f[0]])
        narrow = jnp.stack([sum_a[3], sum_a[4], sum_a[2], sum_a[0], sum_a[1]])
        broad = jnp.stack([sum_w[2], sum_w[0], sum_w[1]])
        return shared, narrow, broad

    def packed(side, sum_a):
        shared, narrow, broad = gathered(sum_a)
        cut, wide_cut = width // 2, units // 2
        return jnp.concatenate(
            [
                shared.reshape(-1),
                narrow[:, side * cut:(side + 1) * cut].reshape(-1),
                broad[:, side * wide_cut:(side + 1) * wide_cut].reshape(-1),
            ]
        )

    if by_links:
        reduce_sides = (m_buf,), (df_buf,), (0,)
        expand_sides = (h2_buf,), (dur_buf,), (0,)
        reduce_other = other_part(*reduce_sides, 0, df_buf)
        expand_other = other_part(*expand_sides, 1, reduce_other)
        pieces = own_part(*reduce_sides, swapped(reduce_other), place, expand_other)
        reduce_sum = BatchSum(pieces, place)
        pieces = own_part(*expand_sides, swapped(expand_other), place, pieces[3])
        expand_sum = BatchSum(pieces, place)
        after = pieces[3]
        for number, (now, grad_mid) in enumerate(held):
            *carried, sent = attend_back(now, after, grad_mid, carried, 1)
            after = reduce_sum.second(carried[-1], 1) if number == 0 else carried[-1]
        sum_a, _, _, dq_buf, dkr_buf, dvr_buf, ig_keep, ig_send = carried
        mixed_sides = (h1_buf, dmr_buf), (dq_buf, dkr_buf, dvr_buf, post_buf), (0, 0, 0, 1)
        mixed_other = other_part(*mixed_sides, 1, after)
        after = expand_sum.second(mixed_other, COSTS[0])
        pieces = own_part(*mixed_sides, swapped(mixed_other), place, after)
        mixed_sum = BatchSum(pieces, place)
        after = reduce_sum.third(pieces[3], COSTS[1])
        after = hidden = spread_rows(hid_keep, hid_send, after)
        small_one, small_two = (packed(side, sum_a).reshape(-1, 128) for side in (0, 1))
        small = plus(small_one, swapped(small_two), after)
        after = mixed_sum.second(after, COSTS[2])
        after = expand_sum.third(after, COSTS[3])
        after = mixed_sum.third(after, COSTS[4])
        input_gradient = spread_rows(ig_keep, ig_send, after)
        small = plus(small, crossed(small, 1), input_gradient)
        (reduce_grad,) = reduce_sum.result((reduce_weight.shape[1:],), input_gradient)
        small = plus(small, crossed(small, 2), reduce_grad)
        (expand_grad,) = expand_sum.result((expand_weight.shape[1:],), reduce_grad)
        project_grad, output_grad = mixed_sum.result(
            (project_weight.shape[1:], output_weight.shape[1:]), expand_grad
        )
        project_grad = project_grad[None]
    else:
        for now, grad_mid in held:
            *carried, sent = attend_back(now, x_buf, grad_mid, carried)
        sum_a, _, _, dq_buf, dkr_buf, dvr_buf, ig_keep, ig_send = carried
        hidden = spread_rows(hid_keep, hid_send, sent)
        input_gradient = spread_rows(ig_keep, ig_send, sent)
        reduce_grad, expand_grad, output_grad, *project_grad = (
            total.astype(F32)
            for total in lax.psum(
                (
                    weight_gradient(m_buf, df_buf, 0), weight_gradient(h2_buf, dur_buf, 1),
                    weight_gradient(post_buf, dmr_buf, 0), weight_gradient(h1_buf, dq_buf, 1),
                    weight_gradient(h1_buf, dkr_buf, 1), weight_gradient(h1_buf, dvr_buf, 1),
                ),
                "batch",
            )
        )
        project_grad = jnp.stack(project_grad)[None]

    if paired:
        if not by_links:
            small = lax.psum(packed(0, sum_a) + swapped(packed(1, sum_a)), "batch")
        small = small.reshape(-1)
        here, there = width // 2, units // 2
        shared = small[:6 * width].reshape(6, width)
        narrow = small[6 * width:6 * width + 5 * here].reshape(5, here)
        broad = small[6 * width + 5 * here:].reshape(3, there)
    else:
        shared, narrow, broad = gathered(sum_a)
        small = lax.psum(
            jnp.concatenate([shared.reshape(-1), narrow.reshape(-1), broad.reshape(-1)]),
            ("batch", "mp"),
        ) * copies
        shared = small[:6 * width].reshape(6, width)
        narrow = small[6 * width:11 * width].reshape(5, width)
        broad = small[11 * width:].reshape(3, units)
        narrow = lax.dynamic_slice_in_dim(narrow, part * (width // parts), width // parts, 1)
        broad = lax.dynamic_slice_in_dim(broad, part * (units // parts), units // parts, 1)

    return (
        hidden[None, None],
        input_gradient[None, None],
        shared[0:2][None],
        shared[2:4][None],
        project_grad,
        narrow[0:2][None],
        jnp.sum(narrow[2].reshape(-1, head), axis=1)[None],
        narrow[3][None],
        narrow[4][None],
        output_grad[None],
        expand_grad[None],
        broad[0][None],
        broad[1][None],
        broad[2][None],
        reduce_grad[None],
        shared[4:6][None],
    )


def solution(mesh):
    layered = P("section", None, None)
    split = P("section", "mp")
    rows = P("section", "mp", None)
    columns = P("section", None, "mp")
    projected = P("section", None, None, "mp")
    tokens = P("batch", None, "mp", None)
    states = P("section", "batch", None, "mp", None)
    return jax.shard_map(
        local,
        mesh=mesh,
        in_specs=(
            tokens, tokens, P("batch", None, None, None), layered, layered, projected, columns,
            split, split, split, rows, columns, split, split, split, rows, layered,
        ),
        out_specs=(
            states, states, layered, layered, projected, columns, split, split, split, rows,
            columns, split, split, split, rows, layered,
        ),
        check_vma=False,
    )
```

```python
from functools import partial

import jax
import jax.numpy as jnp
from jax import lax
from jax.experimental import pallas as pl
from jax.experimental.pallas import tpu as pltpu
from jax.sharding import PartitionSpec as P

EPSILON = 1e-05
CHUNK = 128
KEYS = 256
TILE = 512
STRIP = 256
HIDE = -1e30
COSTS = (100, 15, 10, 5, 5)
LIMITS = tuple(size * 2**20 for size in (7, 8, 11, 10))
F32 = jnp.float32
BF16 = jnp.bfloat16
VMEM = pl.BlockSpec(memory_space=pltpu.VMEM)
SMEM = pl.BlockSpec(memory_space=pltpu.SMEM)
HBM = pl.BlockSpec(memory_space=pltpu.HBM)
ANY = pl.BlockSpec(memory_space=pl.ANY)

DMA = pltpu.SemaphoreType.DMA
SCR = {
    "af": lambda chunk, width, units, length: [
        pltpu.VMEM((chunk, width), BF16), pltpu.VMEM((chunk, width), BF16),
        pltpu.VMEM((chunk, width), BF16), pltpu.VMEM((chunk, width), F32),
        pltpu.VMEM((128, chunk), F32), pltpu.VMEM((chunk, width), BF16),
        pltpu.VMEM((chunk, length), F32), pltpu.VMEM((3, chunk, width), BF16), DMA((7,)),
    ],
    "ff": lambda chunk, width, units, length: [
        pltpu.VMEM((chunk, width), BF16), pltpu.VMEM((chunk, units), F32),
        pltpu.VMEM((chunk, units), BF16), pltpu.VMEM((chunk, units), BF16),
        pltpu.VMEM((chunk, units), BF16), pltpu.VMEM((chunk, 128), F32), DMA((7,)),
    ],
    "fb": lambda chunk, width, units, length: [
        pltpu.VMEM((chunk, units), BF16), pltpu.VMEM((chunk, units), BF16),
        pltpu.VMEM((chunk, 128), F32), pltpu.VMEM((chunk, width), F32),
        pltpu.VMEM((chunk, width), BF16), pltpu.VMEM((chunk, units), F32),
        pltpu.VMEM((chunk, units), BF16), pltpu.VMEM((chunk, width), F32), DMA((4,)), DMA((2,)),
    ],
    "ab": lambda chunk, width, units, length: [
        pltpu.VMEM((chunk, width), BF16), pltpu.VMEM((chunk, width), BF16),
        pltpu.VMEM((chunk, width), F32), pltpu.VMEM((128, chunk), F32),
        pltpu.VMEM((chunk, width), BF16), pltpu.VMEM((chunk, width), F32),
        pltpu.VMEM((length, chunk), F32), pltpu.VMEM((chunk, width), BF16),
        pltpu.VMEM((chunk, width), BF16), pltpu.VMEM((chunk, width), BF16),
        pltpu.VMEM((chunk, width), BF16), pltpu.VMEM((chunk, width), F32),
        DMA((4,)), DMA((6,)),
    ],
}


def lasts(microseconds):
    flops = int(microseconds * 1.1e9)
    return pl.CostEstimate(flops=flops, bytes_accessed=1024, transcendentals=0)


def dot_nn(left, right):
    return jnp.dot(left, right, preferred_element_type=F32)


def dot_nt(left, right):
    return lax.dot_general(left, right, (((1,), (1,)), ((), ())), preferred_element_type=F32)


def dot_tn(left, right):
    return lax.dot_general(left, right, (((0,), (0,)), ((), ())), preferred_element_type=F32)


def norm_parts(values):
    centre = values - jnp.mean(values, axis=-1, keepdims=True)
    inv_std = lax.rsqrt(jnp.mean(centre * centre, axis=-1, keepdims=True) + EPSILON)
    return centre * inv_std, inv_std


def norm_back(scaled, normed, inv_std):
    mean_one = jnp.mean(scaled, axis=-1, keepdims=True)
    mean_two = jnp.mean(scaled * normed, axis=-1, keepdims=True)
    return inv_std * (scaled - mean_one - normed * mean_two)


def column_sum(values):
    return jnp.sum(values, axis=0, keepdims=True)


def document_start(starts_ref, place):
    first = jnp.zeros_like(place)
    for k in range(starts_ref.shape[0]):
        start = starts_ref[k]
        first = jnp.maximum(first, jnp.where(place >= start, start, 0))
    return first


def half_masks():
    lane = lax.broadcasted_iota(jnp.int32, (1, 128), 1)
    return (lane < 64).astype(BF16), (lane >= 64).astype(BF16)


def stack_heads(pair):
    even, odd = half_masks()
    return jnp.concatenate([pair * even, pair * odd], axis=0)


def pick_heads(stacked):
    rows = stacked.shape[0] // 2
    lane = lax.broadcasted_iota(jnp.int32, (1, 128), 1)
    return jnp.where(lane < 64, stacked[:rows], stacked[rows:])


def copies_of(pairs, sems):
    return [pltpu.make_async_copy(a, b, sems.at[i]) for i, (a, b) in enumerate(pairs)]


def in_hbm(values):
    return [pltpu.with_memory_space_constraint(value, pltpu.HBM) for value in values]


def chunk_rows(place_ref, near_ref, far_ref, first, into, sem, step):
    rows, half = into.shape[0], far_ref.shape[0]
    side = first // half
    inner = first - side * half

    @pl.when(side == place_ref[2])
    def _():
        at = pl.ds(pl.multiple_of(place_ref[3] + inner, rows), rows)
        getattr(pltpu.make_async_copy(near_ref.at[at], into, sem), step)()

    @pl.when(side != place_ref[2])
    def _():
        at = pl.ds(pl.multiple_of(inner, rows), rows)
        getattr(pltpu.make_async_copy(far_ref.at[at], into, sem), step)()


def first_rows(place, near, far, first, rows, after):
    def kernel(place_ref, near_ref, far_ref, after_ref, out_ref, sem):
        del after_ref
        for step in ("start", "wait"):
            chunk_rows(place_ref, near_ref, far_ref, jnp.int32(first), out_ref, sem, step)

    return pl.pallas_call(
        kernel,
        in_specs=[SMEM, HBM, HBM, ANY],
        out_specs=VMEM,
        out_shape=jax.ShapeDtypeStruct((rows, near.shape[1]), near.dtype),
        scratch_shapes=[pltpu.SemaphoreType.DMA],
        compiler_params=pltpu.CompilerParams(vmem_limit_bytes=2**20),
    )(place, *in_hbm([near, far]), after)


def last_rows(place, rows, chunk_of, count, keep, send):
    size = rows.shape[0]

    def kernel(place_ref, rows_ref, keep_in, send_in, keep_buf, send_buf, sem):
        del keep_in, send_in
        chunk = chunk_of(place_ref[0], place_ref[1] - 1)

        @pl.when((chunk >= 0) & (chunk < count))
        def _():
            for step in ("start", "wait"):
                store_rows(place_ref, keep_buf, send_buf, chunk * size, rows_ref, sem, step)

    return pl.pallas_call(
        kernel,
        in_specs=[SMEM, VMEM, HBM, HBM],
        out_specs=[HBM, HBM],
        out_shape=[pltpu.HBM(keep.shape, keep.dtype), pltpu.HBM(send.shape, send.dtype)],
        scratch_shapes=[pltpu.SemaphoreType.DMA],
        input_output_aliases={2: 0, 3: 1},
        compiler_params=pltpu.CompilerParams(vmem_limit_bytes=2**20),
        cost_estimate=lasts(1),
    )(place, rows, keep, send)


def row_of(vec_ref, first, size):
    return jnp.concatenate(
        [vec_ref[0, :, first:first + size], vec_ref[1, :, first:first + size]], axis=1
    )


def aligned(index, size):
    return pl.ds(pl.multiple_of(index * size, size), size)


def attend_kernel(
    tick_ref, section_ref, starts_ref, tok_ref, inc_ref, prev_ref, wp_ref, wo_ref,
    vec_ref, gain_ref, bias_ref, branch_ref,
    k_in, v_in, x_in, h1_in, q_in, o_in, lse_in, post_in, keep_in, send_in,
    k_ref, v_ref, x_buf, h1_buf, q_buf, o_buf, lse_buf, post_buf, keep_buf, send_buf, mid_ref,
    x_s, h1_s, q_s, o_s, lse_s, post_s, hide_s, qkv_s, sems,
):
    del k_in, v_in, x_in, h1_in, q_in, o_in, lse_in, post_in, keep_in, send_in
    rows = mid_ref.shape[0]
    length, width = k_ref.shape
    half = width // 2
    section = section_ref[0]
    chunk = tick_ref[0] - 2 * section
    live = (chunk >= 0) & (chunk < length // rows)
    state = (section_ref, keep_buf, send_buf, (chunk - 1) * rows, prev_ref, sems.at[6])

    @pl.when((chunk >= 1) & (chunk <= length // rows))
    def _():
        store_rows(*state, "start")

    @pl.when(live)
    def _():
        first = pl.multiple_of(chunk * rows, rows)
        here = pl.ds(first, rows)

        @pl.when(section == 0)
        def _():
            x_s[...] = tok_ref[...]

        @pl.when(section != 0)
        def _():
            x_s[...] = inc_ref[...]

        sent = []

        def send(source, target):
            copy = pltpu.make_async_copy(source, target, sems.at[len(sent)])
            copy.start()
            sent.append(copy)

        layer_in = x_s[...].astype(F32)
        send(x_s, x_buf.at[here])
        normed, _ = norm_parts(layer_in)
        h1 = (normed * gain_ref[0:1].astype(F32) + bias_ref[0:1].astype(F32)).astype(BF16)
        h1_s[...] = h1
        send(h1_s, h1_buf.at[here])

        def project(number, carry):
            side, which = number // 3, number % 3
            shift = vec_ref[side, :, aligned(which, half)]
            value = dot_nn(h1_s[...], wp_ref[side, which]) + shift
            qkv_s[which, :, aligned(side, half)] = value.astype(BF16)
            return carry

        lax.fori_loop(0, 6, project, 0, unroll=6)
        q_s[...] = qkv_s[0] * jnp.asarray(0.125, BF16)
        k_ref[here, :] = qkv_s[1]
        v_ref[here, :] = qkv_s[2]
        send(q_s, q_buf.at[here])

        def attend(keys):
            place = first + lax.broadcasted_iota(jnp.int32, (rows, 1), 0)
            start = document_start(starts_ref, place)
            key_at = lax.broadcasted_iota(jnp.int32, (rows, keys), 1)
            hide_s[:, :keys] = jnp.where((key_at <= place) & (key_at >= start), 0.0, HIDE)
            lane = lax.broadcasted_iota(jnp.int32, (rows, 128), 1)

            def one_pair(pair, lse):
                at = pl.ds(pl.multiple_of(pair * 128, 128), 128)
                queries = stack_heads(q_s[:, at])
                hide = hide_s[:, :keys]
                scores = dot_nt(queries, k_ref[0:keys, at]) + jnp.concatenate([hide, hide], axis=0)
                top = jnp.max(scores, axis=-1, keepdims=True)
                raised = jnp.exp(scores - top)
                total = jnp.sum(raised, axis=-1, keepdims=True)
                out = dot_nn(raised.astype(BF16), v_ref[0:keys, at]) / total
                o_s[:, at] = pick_heads(out)
                now = top + jnp.log(total)
                lse = jnp.where(lane == 2 * pair, now[:rows], lse)
                return jnp.where(lane == 2 * pair + 1, now[rows:], lse)

            lse = lax.fori_loop(0, width // 128, one_pair, jnp.zeros((rows, 128), F32))
            lse_s[...] = lse.T

        for count in range(length // KEYS):

            @pl.when(first // KEYS == count)
            def _():
                attend((count + 1) * KEYS)

        send(o_s, o_buf.at[here])
        send(lse_s, lse_buf.at[chunk])
        post_normed, _ = norm_parts(o_s[...] * row_of(vec_ref, 3 * half, half))
        post = post_normed * row_of(vec_ref, 4 * half, half) + row_of(vec_ref, 5 * half, half)
        post_s[...] = post.astype(BF16)
        send(post_s, post_buf.at[here])

        def mix(number, carry):
            at = aligned(number, STRIP)
            total = dot_nn(post_s[:, :half], wo_ref[0, :, at])
            total += dot_nn(post_s[:, half:], wo_ref[1, :, at])
            mid_ref[:, at] = x_s[:, at].astype(F32) + total + branch_ref[0:1, at].astype(F32)
            return carry

        lax.fori_loop(0, width // STRIP, mix, 0, unroll=4)
        for copy in sent:
            copy.wait()

    @pl.when((chunk >= 1) & (chunk <= length // rows))
    def _():
        store_rows(*state, "wait")


def gelu_parts(pre):
    phi = 0.5 + 0.5 * lax.erf(pre * 0.7071067811865476)
    density = jnp.exp(pre * pre * -0.5) * 0.3989422804014327
    return pre * phi, phi + pre * density


def expand_kernel(
    tick_ref, section_ref, near_ref, far_ref, mid_ref, we_ref, wr_ref, vec_ref, gain_ref,
    bias_ref, branch_ref,
    h2_in, g_in, gp_in, m_in, st_in, mid_in,
    h2_buf, g_buf, gp_buf, m_buf, st_buf, mid_buf, out_ref, next_ref,
    h2_s, gf_s, g_s, gp_s, m_s, st_s, sems,
):
    del h2_in, g_in, gp_in, m_in, st_in, mid_in
    rows = mid_ref.shape[0]
    width = mid_ref.shape[1]
    half = we_ref.shape[2]
    units = 2 * half
    tiles = half // TILE
    length = h2_buf.shape[0]
    chunk = tick_ref[0] - 2 * section_ref[0]

    @pl.when((chunk >= 0) & (chunk < length // rows))
    def _():
        here = pl.ds(pl.multiple_of(chunk * rows, rows), rows)
        sent = []

        def send(source, target):
            copy = pltpu.make_async_copy(source, target, sems.at[len(sent)])
            copy.start()
            sent.append(copy)

        send(mid_ref, mid_buf.at[here])
        more = (section_ref[0] == 0) & (chunk + 1 < length // rows)
        fetch = (section_ref, near_ref, far_ref, (chunk + 1) * rows, next_ref, sems.at[6])

        @pl.when(more)
        def _():
            chunk_rows(*fetch, "start")

        def wide(tile, which):
            first = 3 * width + which * half + tile % tiles * TILE
            return vec_ref[tile // tiles, :, pl.ds(pl.multiple_of(first, TILE), TILE)]

        normed, _ = norm_parts(mid_ref[...])
        h2 = (normed * gain_ref[1:2].astype(F32) + bias_ref[1:2].astype(F32)).astype(BF16)
        h2_s[...] = h2
        send(h2_s, h2_buf.at[here])
        def expand(tile, total):
            at = aligned(tile, TILE)
            weight = we_ref[tile // tiles, :, aligned(tile % tiles, TILE)]
            active, slope = gelu_parts(dot_nn(h2_s[...], weight) + wide(tile, 0))
            gf_s[:, at] = active
            g_s[:, at] = active.astype(BF16)
            gp_s[:, at] = slope.astype(BF16)
            return total + jnp.sum(active, axis=-1, keepdims=True)

        nothing = jnp.zeros((rows, 1), F32)
        mean = lax.fori_loop(0, 2 * tiles, expand, nothing, unroll=4) / units
        send(g_s, g_buf.at[here])
        send(gp_s, gp_buf.at[here])

        def spread(tile, total):
            centre = gf_s[:, aligned(tile, TILE)] - mean
            return total + jnp.sum(centre * centre, axis=-1, keepdims=True)

        inv_std = lax.rsqrt(lax.fori_loop(0, 2 * tiles, spread, nothing, unroll=8) / units + EPSILON)
        lane = lax.broadcasted_iota(jnp.int32, (rows, 128), 1)
        st_s[...] = jnp.where(lane == 0, mean, inv_std)
        send(st_s, st_buf.at[here])

        def normalise(tile, carry):
            at = aligned(tile, TILE)
            active = (gf_s[:, at] - mean) * inv_std * wide(tile, 1) + wide(tile, 2)
            m_s[:, at] = active.astype(BF16)
            return carry

        lax.fori_loop(0, 2 * tiles, normalise, 0, unroll=4)
        send(m_s, m_buf.at[here])

        def reduce(number, carry):
            at = aligned(number, STRIP)
            total = dot_nn(m_s[:, :half], wr_ref[0, :, at])
            total += dot_nn(m_s[:, half:], wr_ref[1, :, at])
            total += mid_ref[:, at] + branch_ref[1:2, at].astype(F32)
            out_ref[:, at] = total.astype(BF16)
            return carry

        lax.fori_loop(0, width // STRIP, reduce, 0, unroll=2)
        for copy in sent:
            copy.wait()

        @pl.when(more)
        def _():
            chunk_rows(*fetch, "wait")


def expand_back_kernel(
    tick_ref, section_ref, cot_ref, inc_ref, wr_ref, we_ref, vec_ref, gain_ref,
    g_buf, gp_buf, st_buf, mid_buf,
    sum_in, wsum_in, df_in, dur_in,
    sum_ref, wsum_ref, df_buf, dur_buf, dmid_ref,
    g_s, gp_s, st_s, mid_s, df_s, z_s, dur_s, dh_s, in_sems, out_sems,
):
    del sum_in, wsum_in, df_in, dur_in
    rows = dmid_ref.shape[0]
    width = dmid_ref.shape[1]
    half = wr_ref.shape[2]
    units = 2 * half
    tiles = half // TILE
    length = g_buf.shape[0]
    count = length // rows
    section = section_ref[0]
    last = section_ref[1] - 1
    chunk = count - 1 - (tick_ref[0] - 2 * (last - section))

    @pl.when((chunk >= 0) & (chunk < count))
    def _():
        here = pl.ds(pl.multiple_of(chunk * rows, rows), rows)
        loads = copies_of(
            (
                (g_buf.at[here], g_s), (gp_buf.at[here], gp_s), (st_buf.at[here], st_s),
                (mid_buf.at[here], mid_s),
            ),
            in_sems,
        )
        for copy in loads:
            copy.start()

        @pl.when(section == last)
        def _():
            df_s[...] = cot_ref[...]

        @pl.when(section != last)
        def _():
            df_s[...] = inc_ref[...]

        sent = []

        def send(source, target):
            copy = pltpu.make_async_copy(source, target, out_sems.at[len(sent)])
            copy.start()
            sent.append(copy)

        def gain_of(tile):
            first = 3 * width + half + tile % tiles * TILE
            return vec_ref[tile // tiles, :, pl.ds(pl.multiple_of(first, TILE), TILE)]

        grad_low = df_s[...]
        send(df_s, df_buf.at[here])
        sum_ref[0:1] += column_sum(grad_low.astype(F32))
        loads[0].wait()
        loads[2].wait()
        mean = st_s[:, 0:1]
        inv_std = st_s[:, 1:2]
        def reduce_back(tile, sums):
            at = aligned(tile, TILE)
            weight = wr_ref[tile // tiles, :, aligned(tile % tiles, TILE)]
            grad = dot_nn(df_s[...], weight)
            normed = (g_s[:, at].astype(F32) - mean) * inv_std
            wsum_ref[0:1, at] += column_sum(grad * normed)
            wsum_ref[1:2, at] += column_sum(grad)
            scaled = grad * gain_of(tile)
            z_s[:, at] = scaled
            return (
                sums[0] + jnp.sum(scaled, axis=-1, keepdims=True),
                sums[1] + jnp.sum(scaled * normed, axis=-1, keepdims=True),
            )

        nothing = jnp.zeros((rows, 1), F32)
        one, two = lax.fori_loop(0, 2 * tiles, reduce_back, (nothing, nothing), unroll=4)
        one = one / units
        two = two / units

        def active_back(tile, carry):
            at = aligned(tile, TILE)
            normed = (g_s[:, at].astype(F32) - mean) * inv_std
            grad = inv_std * (z_s[:, at] - one - normed * two) * gp_s[:, at].astype(F32)
            wsum_ref[2:3, at] += column_sum(grad)
            dur_s[:, at] = grad.astype(BF16)
            return carry

        loads[1].wait()
        lax.fori_loop(0, 2 * tiles, active_back, 0, unroll=8)
        send(dur_s, dur_buf.at[here])

        def expand_back(number, carry):
            at = aligned(number, STRIP)
            total = dot_nn(dur_s[:, :half], we_ref[0, :, at])
            dh_s[:, at] = total + dot_nn(dur_s[:, half:], we_ref[1, :, at])
            return carry

        lax.fori_loop(0, width // STRIP, expand_back, 0, unroll=4)
        grad_second = dh_s[...]
        loads[3].wait()
        normed, inv_std = norm_parts(mid_s[...])
        sum_ref[1:2] += column_sum(grad_second * normed)
        sum_ref[2:3] += column_sum(grad_second)
        grad_mid = grad_low.astype(F32) + norm_back(
            grad_second * gain_ref[1:2].astype(F32), normed, inv_std
        )
        sum_ref[3:4] += column_sum(grad_mid)
        dmid_ref[...] = grad_mid
        for copy in sent:
            copy.wait()


def attend_back_kernel(
    tick_ref, section_ref, starts_ref, after, near_ref, far_ref, prev_ref, dmid_ref, wo_ref,
    wp_ref, vec_ref, gain_ref, k_ref, v_ref,
    x_buf, q_buf, o_buf, lse_buf,
    sum_in, dk_in, dv_in, dq_in, dkr_in, dvr_in, dmr_in, keep_in, send_in,
    sum_ref, dk_ref, dv_ref, dq_buf, dkr_buf, dvr_buf, dmr_buf, keep_buf, send_buf, out_ref,
    next_ref,
    x_s, q_s, o_s, lse_s, do_s, dqf_s, hide_s, dq_s, dkr_s, dvr_s, low_s, wide_s, in_sems,
    out_sems,
):
    del after, sum_in, dk_in, dv_in, dq_in, dkr_in, dvr_in, dmr_in, keep_in, send_in
    rows = dmid_ref.shape[0]
    length, width = k_ref.shape
    half = width // 2
    count = length // rows
    section = section_ref[0]
    last = section_ref[1] - 1
    chunk = count - 1 - (tick_ref[0] - 2 * (last - section))

    state = (section_ref, keep_buf, send_buf, (chunk + 1) * rows, prev_ref, out_sems.at[4])

    @pl.when((chunk >= -1) & (chunk < count - 1))
    def _():
        store_rows(*state, "start")

    @pl.when((chunk >= 0) & (chunk < count))
    def _():
        first = pl.multiple_of(chunk * rows, rows)
        here = pl.ds(first, rows)
        loads = copies_of(
            (
                (x_buf.at[here], x_s), (q_buf.at[here], q_s), (o_buf.at[here], o_s),
                (lse_buf.at[chunk], lse_s),
            ),
            in_sems,
        )
        for copy in loads:
            copy.start()

        @pl.when(chunk == count - 1)
        def _():
            dk_ref[...] = jnp.zeros_like(dk_ref)
            dv_ref[...] = jnp.zeros_like(dv_ref)

        more = (section == last) & (chunk >= 1)
        fetch = (section_ref, near_ref, far_ref, (chunk - 1) * rows, next_ref, out_sems.at[5])

        @pl.when(more)
        def _():
            chunk_rows(*fetch, "start")

        sent = []

        def send(source, target):
            copy = pltpu.make_async_copy(source, target, out_sems.at[len(sent)])
            copy.start()
            sent.append(copy)

        low_s[...] = dmid_ref[...].astype(BF16)
        send(low_s, dmr_buf.at[here])

        def mix_back(side, carry):
            wide_s[:, aligned(side, half)] = dot_nn(low_s[...], wo_ref[side])
            return carry

        lax.fori_loop(0, 2, mix_back, 0, unroll=2)
        grad_post = wide_s[...]
        loads[2].wait()
        attended = o_s[...]
        scale = row_of(vec_ref, 3 * half, half)
        normed, inv_std = norm_parts(attended * scale)
        sum_ref[0:1] += column_sum(grad_post * normed)
        sum_ref[1:2] += column_sum(grad_post)
        grad_mixed = norm_back(grad_post * row_of(vec_ref, 4 * half, half), normed, inv_std)
        sum_ref[2:3] += column_sum(grad_mixed * attended)
        do_s[...] = (grad_mixed * scale).astype(BF16)

        loads[1].wait()
        loads[3].wait()

        def attend(keys):
            place = first + lax.broadcasted_iota(jnp.int32, (1, rows), 1)
            start = document_start(starts_ref, place)
            key_at = lax.broadcasted_iota(jnp.int32, (keys, rows), 0)
            hide_s[:keys, :] = jnp.where((key_at <= place) & (key_at >= start), 0.0, HIDE)

            def one_pair(pair, carry):
                at = pl.ds(pl.multiple_of(pair * 128, 128), 128)
                queries = stack_heads(q_s[:, at])
                grad_pair = do_s[:, at]
                grads = stack_heads(grad_pair)
                product = (grad_pair.astype(F32) * o_s[:, at]).T
                delta = jnp.concatenate(
                    [column_sum(product[:64]), column_sum(product[64:])], axis=1
                )
                lse = jnp.concatenate(
                    [lse_s[pl.ds(2 * pair, 1), :], lse_s[pl.ds(2 * pair + 1, 1), :]], axis=1
                )
                hide = hide_s[:keys, :]
                key_pair = k_ref[0:keys, at]
                scores = dot_nt(key_pair, queries) + jnp.concatenate([hide, hide], axis=1)
                probs = jnp.exp(scores - lse)
                grad_probs = dot_nt(v_ref[0:keys, at], grads)
                grad_scores = (probs * (grad_probs - delta)).astype(BF16)
                dk_ref[0:keys, at] += dot_nn(grad_scores, queries)
                dv_ref[0:keys, at] += dot_nn(probs.astype(BF16), grads)
                dqf_s[:, at] = pick_heads(dot_tn(grad_scores, key_pair)) * 0.125
                return carry

            lax.fori_loop(0, width // 128, one_pair, 0)

        for number in range(length // KEYS):

            @pl.when(first // KEYS == number)
            def _():
                attend((number + 1) * KEYS)

        grad_query = dqf_s[...]
        grad_value = dv_ref[here, :]
        sum_ref[3:4] += column_sum(grad_query)
        sum_ref[4:5] += column_sum(grad_value)
        dq_s[...] = grad_query.astype(BF16)
        dkr_s[...] = dk_ref[here, :].astype(BF16)
        dvr_s[...] = grad_value.astype(BF16)
        send(dq_s, dq_buf.at[here])
        send(dkr_s, dkr_buf.at[here])
        send(dvr_s, dvr_buf.at[here])

        def project_back(number, carry):
            at = aligned(number, STRIP)
            total = jnp.zeros((rows, STRIP), F32)
            for which, part in enumerate((dq_s, dkr_s, dvr_s)):
                total += dot_nn(part[:, :half], wp_ref[0, which, :, at])
                total += dot_nn(part[:, half:], wp_ref[1, which, :, at])
            wide_s[:, at] = total
            return carry

        lax.fori_loop(0, width // STRIP, project_back, 0, unroll=4)
        grad_first = wide_s[...]
        loads[0].wait()
        normed, inv_std = norm_parts(x_s[...].astype(F32))
        sum_ref[5:6] += column_sum(grad_first * normed)
        sum_ref[6:7] += column_sum(grad_first)
        out = dmid_ref[...] + norm_back(
            grad_first * gain_ref[0:1].astype(F32), normed, inv_std
        )
        out_ref[...] = out.astype(BF16)
        for copy in sent:
            copy.wait()

        @pl.when(more)
        def _():
            chunk_rows(*fetch, "wait")

    @pl.when((chunk >= -1) & (chunk < count - 1))
    def _():
        store_rows(*state, "wait")


def flip_kernel(source, after, target):
    del after
    size = 256

    def flip(one, two):
        def body(step, carry):
            at = aligned(step, size)
            two[:, at] = one[at, :].T
            return carry

        lax.fori_loop(0, one.shape[0] // size, body, 0)

    def each(index, carry):
        if len(source.shape) == 3:
            flip(source.at[index], target.at[index])
        else:
            deep = source.shape[1]
            flip(source.at[index // deep, index % deep], target.at[index // deep, index % deep])
        return carry

    count = source.shape[0] * (source.shape[1] if len(source.shape) == 4 else 1)
    lax.fori_loop(0, count, each, 0)


def flipped(weight, after):
    shape = weight.shape[:-2] + (weight.shape[-1], weight.shape[-2])
    return pl.pallas_call(
        flip_kernel,
        in_specs=[VMEM, ANY],
        out_specs=VMEM,
        out_shape=pltpu.VMEM(shape, BF16),
        compiler_params=pltpu.CompilerParams(vmem_limit_bytes=2 * 2**20),
    )(weight, after)


def load_kernel(side, source, after, *refs):
    del after
    copy = pltpu.make_async_copy(source, refs[-2].at[side], refs[-1])
    copy.start()
    copy.wait()


def loaded(side, value, both, after):
    known = [] if both is None else [both]
    return pl.pallas_call(
        partial(load_kernel, side),
        in_specs=[HBM, ANY] + [VMEM] * len(known),
        out_specs=VMEM,
        out_shape=pltpu.VMEM((2, *value.shape), value.dtype),
        scratch_shapes=[pltpu.SemaphoreType.DMA],
        input_output_aliases={2: 0} if known else {},
        compiler_params=pltpu.CompilerParams(vmem_limit_bytes=2**20),
    )(*in_hbm([value]), after, *known)


def empty_kernel(*refs):
    del refs


def empty(shapes, space, *after):
    return pl.pallas_call(
        empty_kernel,
        in_specs=[ANY] * len(after),
        out_specs=[pl.BlockSpec(memory_space=space)] * len(shapes),
        out_shape=[space(shape, dtype) for shape, dtype in shapes],
        compiler_params=pltpu.CompilerParams(vmem_limit_bytes=2**20),
    )(*after)


def call(kernel, inputs, specs, carried, carried_specs, fresh, fresh_specs, scratch, limit, flops):
    first = len(inputs)
    inputs = [
        pltpu.with_memory_space_constraint(a, pltpu.HBM) if spec is HBM else a
        for a, spec in zip(inputs, specs)
    ]
    shapes = [
        pltpu.HBM(a.shape, a.dtype) if spec is HBM else jax.ShapeDtypeStruct(a.shape, a.dtype)
        for a, spec in zip(carried, carried_specs)
    ] + fresh
    return pl.pallas_call(
        kernel,
        in_specs=specs + carried_specs,
        out_specs=carried_specs + fresh_specs,
        out_shape=shapes,
        scratch_shapes=scratch,
        input_output_aliases={first + i: i for i in range(len(carried))},
        compiler_params=pltpu.CompilerParams(vmem_limit_bytes=limit),
        cost_estimate=pl.CostEstimate(flops=flops, bytes_accessed=2**22, transcendentals=0),
    )(*inputs, *carried)


def settle_kernel(place_ref, *refs):
    pieces, (*outs, wide_s, turn_s, sems) = refs[:8], refs[8:]
    rows = pieces[0].shape[0]
    low, high = place_ref[4], place_ref[5]
    copies = []
    for number, piece in enumerate(pieces):
        half, flips = number // 4, number % 4
        first = (low, high)[half] ^ (flips // 2)
        second = (high, low)[half] ^ (flips % 2)
        slot = number % 2
        if number >= 2:
            for copy in copies[number - 2]:
                copy.wait()
        wide_s[slot] = piece[...].astype(F32)
        at = pl.ds(pl.multiple_of((half * 4 + first * 2 + second) * rows, rows), rows)
        moves = []
        if len(outs) == 1:
            moves.append((wide_s.at[slot], outs[0].at[at]))
        else:
            layers, _, columns = outs[0].shape
            for layer in range(layers):
                source = wide_s.at[slot, :, layer * columns:(layer + 1) * columns]
                moves.append((source, outs[0].at[layer, at]))
            turn_s[slot] = wide_s[slot, :, layers * columns:].T
            moves.append((turn_s.at[slot], outs[1].at[:, at]))
        started = [
            pltpu.make_async_copy(source, target, sems.at[slot, i])
            for i, (source, target) in enumerate(moves)
        ]
        for copy in started:
            copy.start()
        copies.append(started)
    for copy in copies[6] + copies[7]:
        copy.wait()


def settle(place, pieces, shapes, after, cost):
    rows, columns = pieces[0].shape
    turn = (2, shapes[1][0], rows) if len(shapes) > 1 else (2, 8, 128)

    def kernel(place_ref, *refs):
        settle_kernel(place_ref, *refs[:8], *refs[9:])

    return pl.pallas_call(
        kernel,
        grid=(1,),
        in_specs=[SMEM]
        + [pl.BlockSpec((rows, columns), lambda i: (0, 0), pipeline_mode=pl.Buffered(1))] * 8
        + [HBM],
        out_specs=[HBM] * len(shapes),
        out_shape=[pltpu.HBM(shape, F32) for shape in shapes],
        scratch_shapes=[
            pltpu.VMEM((2, rows, columns), F32), pltpu.VMEM(turn, F32),
            pltpu.SemaphoreType.DMA((2, 4)),
        ],
        compiler_params=pltpu.CompilerParams(vmem_limit_bytes=12 * 2**20),
        cost_estimate=lasts(cost),
    )(place, *pieces, *in_hbm([after]))


def crossed(value, bit):
    route = [(i, i ^ bit) for i in range(lax.axis_size("batch"))]
    return lax.ppermute(value, "batch", route)


def product(lefts, rights, pairs, columns, number):
    left = lefts[pairs[number]][...]
    return slice(number * columns, (number + 1) * columns), dot_tn(left, rights[number][...])


def other_part(lefts, rights, pairs, axis, after, cost=1):
    length = lefts[0].shape[0]
    rows = lefts[0].shape[1] // (2 if axis == 0 else 1)
    columns = rights[0].shape[1] // (1 if axis == 0 else 2)
    tile = rows // 4
    skip = 4 if axis == 0 else 0
    side = 0 if axis == 0 else 1

    def kernel(*refs):
        for number in range(len(rights)):
            at, value = product(
                refs[:len(lefts)], refs[len(lefts):], pairs, columns, number
            )
            refs[-1][:, at] = value.astype(BF16)

    return pl.pallas_call(
        kernel,
        grid=(rows // tile,),
        in_specs=[pl.BlockSpec((length, tile), lambda i: (0, skip + i))] * len(lefts)
        + [pl.BlockSpec((length, columns), lambda i: (0, side), pipeline_mode=pl.Buffered(1))]
        * len(rights)
        + [HBM],
        out_specs=pl.BlockSpec((tile, columns * len(rights)), lambda i: (i, 0)),
        out_shape=pltpu.HBM((rows, columns * len(rights)), BF16),
        compiler_params=pltpu.CompilerParams(vmem_limit_bytes=12 * 2**20),
        cost_estimate=lasts(cost),
    )(*in_hbm(lefts), *in_hbm(rights), *in_hbm([after]))


def own_part(lefts, rights, pairs, come, place, after, cost=1):
    length = lefts[0].shape[0]
    rows, whole = come.shape
    columns = whole // len(rights)
    tile = rows // 4

    def at(i, place):
        low, high = place[4], place[5]
        first = jnp.where(i == 0, 1 - low, 3 - high)
        return jnp.where(i < 2, first, jnp.where(i == 2, low, 2 + high))

    def kernel(place_ref, *refs):
        del place_ref
        come_ref = refs[len(lefts) + len(rights)]
        *outs, low_s, sems = refs[-6:]
        step = pl.program_id(0)
        slot = step % 2

        def store(number):
            return pltpu.make_async_copy(
                low_s.at[number % 2], outs[number], sems.at[number % 2]
            )

        for number in (2, 3):

            @pl.when(step == number)
            def _():
                store(number - 2).wait()

        for number in range(len(rights)):
            where, value = product(
                refs[:len(lefts)], refs[len(lefts):], pairs, columns, number
            )
            low_s[slot, :, where] = (value + come_ref[:, where].astype(F32)).astype(BF16)
        for number in range(4):

            @pl.when(step == number)
            def _():
                store(number).start()

        @pl.when(step == 3)
        def _():
            store(2).wait()
            store(3).wait()

    return pl.pallas_call(
        kernel,
        grid_spec=pltpu.PrefetchScalarGridSpec(
            num_scalar_prefetch=1,
            grid=(4,),
            in_specs=[pl.BlockSpec((length, tile), lambda i, place: (0, at(i, place)))]
            * len(lefts)
            + [
                pl.BlockSpec(
                    (length, columns), lambda i, place: (0, 0), pipeline_mode=pl.Buffered(1)
                )
            ]
            * len(rights)
            + [pl.BlockSpec((tile, whole), lambda i, place: (at(i, place), 0)), HBM],
            out_specs=[HBM] * 4,
            scratch_shapes=[
                pltpu.VMEM((2, tile, whole), BF16), pltpu.SemaphoreType.DMA((2,))
            ],
        ),
        out_shape=[pltpu.HBM((tile, whole), BF16)] * 4,
        compiler_params=pltpu.CompilerParams(vmem_limit_bytes=12 * 2**20),
        cost_estimate=lasts(cost),
    )(place, *in_hbm(lefts), *in_hbm(rights), come, *in_hbm([after]))


def add_kernel(split, place_ref, *refs):
    keeps, comes = (refs[0], refs[2]), (refs[1], refs[3])
    outs = refs[5:]
    for half, bit in ((0, 5), (1, 4)):
        keep, come = keeps[half], comes[half]
        if split:
            rows = keep.shape[0] // 2
            side = place_ref[bit]
            for number, where in ((0, 1 - side), (1, side)):
                at = pl.ds(pl.multiple_of(where * rows, rows), rows)
                outs[2 * half + number][...] = (
                    keep[at, :].astype(F32) + come[at, :].astype(F32)
                ).astype(BF16)
        else:
            outs[half][...] = (keep[...].astype(F32) + come[...].astype(F32)).astype(BF16)


def added(keeps, comes, place, split, after, cost):
    rows, columns = keeps[0].shape
    kept = rows // 2 if split else rows
    count = 4 if split else 2
    return pl.pallas_call(
        partial(add_kernel, split),
        grid=(1,),
        in_specs=[SMEM]
        + [pl.BlockSpec((rows, columns), lambda i: (0, 0), pipeline_mode=pl.Buffered(1))] * 4
        + [HBM],
        out_specs=[
            pl.BlockSpec((kept, columns), lambda i: (0, 0), pipeline_mode=pl.Buffered(1))
        ]
        * count,
        out_shape=[pltpu.HBM((kept, columns), BF16)] * count,
        compiler_params=pltpu.CompilerParams(vmem_limit_bytes=12 * 2**20),
        cost_estimate=lasts(cost),
    )(place, keeps[0], comes[0], keeps[1], comes[1], *in_hbm([after]))


class BatchSum:
    def __init__(self, pieces, place):
        send_a, send_b, keep_a, keep_b = pieces
        self.place = place
        self.keeps = keep_a, keep_b
        self.comes = crossed(send_a, 1), crossed(send_b, 2)

    def second(self, after, cost):
        send_a, keep_a, send_b, keep_b = added(self.keeps, self.comes, self.place, True, after, cost)
        self.keeps = keep_a, keep_b
        self.comes = crossed(send_a, 2), crossed(send_b, 1)
        return keep_a

    def third(self, after, cost):
        a, b = added(self.keeps, self.comes, self.place, False, after, cost)
        across_a, across_b = crossed(a, 2), crossed(b, 1)
        self.pieces = [
            a, across_a, crossed(a, 1), crossed(across_a, 1),
            b, across_b, crossed(b, 2), crossed(across_b, 2),
        ]
        return a

    def result(self, shapes, after, cost=1):
        return settle(self.place, self.pieces, shapes, after, cost)


def keep_kernel(place_ref, come_ref, in_ref, out_ref, sem):
    del in_ref
    copy = pltpu.make_async_copy(come_ref, out_ref.at[1 - place_ref[2]], sem)
    copy.start()
    copy.wait()


def with_other_half(kept, come, place, after):
    def kernel(place_ref, come_ref, after_ref, *refs):
        keep_kernel(place_ref, come_ref, *refs)

    return pl.pallas_call(
        kernel,
        in_specs=[SMEM, VMEM, HBM, HBM],
        out_specs=HBM,
        out_shape=pltpu.HBM(kept.shape, kept.dtype),
        scratch_shapes=[pltpu.SemaphoreType.DMA],
        compiler_params=pltpu.CompilerParams(vmem_limit_bytes=4 * 2**20),
        input_output_aliases={3: 0},
        cost_estimate=lasts(3),
    )(place, come, *in_hbm([after]), kept)


def plus_kernel(one, two, after, out):
    del after
    out[...] = one[...] + two[...]


def plus(one, two, after):
    return pl.pallas_call(
        plus_kernel,
        in_specs=[VMEM, VMEM, HBM],
        out_specs=VMEM,
        out_shape=jax.ShapeDtypeStruct(one.shape, one.dtype),
        compiler_params=pltpu.CompilerParams(vmem_limit_bytes=2**20),
        cost_estimate=lasts(1),
    )(one, two, *in_hbm([after]))


def store_rows(place_ref, keep_buf, send_buf, first, source, sem, back):
    rows = source.shape[0]
    half = send_buf.shape[0]
    side = first // half
    at = pl.ds(pl.multiple_of(first - side * half, rows), rows)

    @pl.when(side == place_ref[2])
    def _():
        copy = pltpu.make_async_copy(source, keep_buf.at[side, at], sem)
        getattr(copy, back)()

    @pl.when(side != place_ref[2])
    def _():
        copy = pltpu.make_async_copy(source, send_buf.at[at], sem)
        getattr(copy, back)()


def local(
    tokens, cotangent, document_starts, pre_gain, pre_bias, project_weight, project_bias,
    head_scale, post_gain, post_bias, output_weight, expand_weight, expand_bias, middle_gain,
    middle_bias, reduce_weight, branch_bias,
):
    sections = lax.axis_size("section")
    section = lax.axis_index("section")
    parts = lax.axis_size("mp")
    part = lax.axis_index("mp")
    shard = lax.axis_index("batch")
    micro, rows_here, width = tokens.shape[1:]
    length = rows_here * parts
    chunk = CHUNK
    count = length // chunk
    head = width // (head_scale.shape[1] * parts)
    units = expand_bias.shape[1] * parts
    paired = parts == 2 and micro == 2
    by_links = paired and lax.axis_size("batch") == 4
    block = part * micro // parts
    copies = micro / parts

    def swapped(value):
        return lax.ppermute(value, "mp", [(0, 1), (1, 0)])

    def both(value, axis):
        if paired:
            return value, swapped(value)
        whole = lax.all_gather(value, "mp", axis=axis, tiled=True)
        return tuple(jnp.split(whole, 2, axis=axis))

    def row_source(value):
        if paired:
            theirs = lax.dynamic_index_in_dim(value, 1 - part, 0, keepdims=False)
            return value.reshape(micro * rows_here, width), swapped(theirs)
        whole = lax.all_gather(value, "mp", axis=1, tiled=True)
        whole = lax.dynamic_index_in_dim(whole, block, 0, keepdims=False)
        return whole[:length // 2], whole[length // 2:]

    def spread_rows(kept, sent, after):
        if paired:
            return with_other_half(kept, swapped(sent), place, after)
        whole = lax.all_gather(jnp.concatenate([kept[0], sent]), "mp", axis=0)[:: parts // micro]
        return lax.dynamic_slice_in_dim(whole, part * rows_here, rows_here, 1)

    near_tokens, far_tokens = row_source(tokens[0])
    place = jnp.stack(
        [
            section, jnp.int32(sections), part if paired else jnp.int32(0),
            part * rows_here if paired else jnp.int32(0), shard % 2, shard // 2,
        ]
    ).astype(jnp.int32)
    starts = lax.dynamic_index_in_dim(document_starts[0], block, 0, keepdims=False)[0]
    fields = (
        project_bias[0, 0], jnp.zeros_like(project_bias[0, 0]), project_bias[0, 1],
        jnp.repeat(head_scale[0], head), post_gain[0],
        post_bias[0], expand_bias[0], middle_gain[0], middle_bias[0],
    )
    if paired:
        own = jnp.concatenate(fields)[None]
        other = swapped(own)
    else:
        sides = [both(field, 0) for field in fields]
        own = jnp.concatenate([a for a, _ in sides])[None]
        other = jnp.concatenate([b for _, b in sides])[None]
    gains, biases, branches = pre_gain[0], pre_bias[0], branch_bias[0]
    wp_a, wp_b = both(project_weight[0], 2)
    wo_a, wo_b = both(output_weight[0], 0)
    we_a, we_b = both(expand_weight[0], 1)
    wr_a, wr_b = both(reduce_weight[0], 0)
    wp = loaded(0, wp_a, None, place)
    wo = loaded(0, wo_a, None, wp)
    we = loaded(0, we_a, None, wo)
    wr = loaded(0, wr_a, None, we)
    wr_own = wr
    wp = loaded(1, wp_b, wp, wr)
    wo = loaded(1, wo_b, wo, wp)
    we = loaded(1, we_b, we, wo)
    wr = loaded(1, wr_b, wr, we)
    vectors = jnp.stack([own, other]).astype(F32)
    near_cotangent, far_cotangent = row_source(cotangent[0])

    def sized(columns, dtype):
        return ((length, columns), dtype)

    halves = (((2, length // 2, width), BF16), ((length // 2, width), BF16))

    (
        x_buf, h1_buf, q_buf, o_buf, lse_buf, post_buf, mid_buf,
        h2_buf, g_buf, gp_buf, m_buf, st_buf, hid_keep, hid_send,
        df_buf, dur_buf, dmr_buf, dq_buf, dkr_buf, dvr_buf, ig_keep, ig_send,
    ) = empty(
        [
            sized(width, BF16), sized(width, BF16), sized(width, BF16), sized(width, F32),
            ((count, 128, chunk), F32), sized(width, BF16), sized(width, F32),
            sized(width, BF16), sized(units, BF16), sized(units, BF16), sized(units, BF16),
            sized(128, F32), *halves,
            sized(width, BF16), sized(units, BF16), sized(width, BF16), sized(width, BF16),
            sized(width, BF16), sized(width, BF16), *halves,
        ],
        pltpu.HBM,
    )
    k_all = jnp.zeros((length, width), BF16)
    v_all = jnp.zeros((length, width), BF16)
    dense = 2 * chunk * width

    def shifted(value, distance):
        route = [(i, i + distance) for i in range(sections) if 0 <= i + distance < sections]
        return lax.ppermute(value, "section", route)

    ticks = count + 2 * (sections - 1)
    blank = jnp.zeros((chunk, width), BF16)
    incoming = blank
    sent = None
    rows_in = first_rows(place, near_tokens, far_tokens, 0, chunk, wr_own)
    for tick in range(ticks):
        now = jnp.full((1,), tick, jnp.int32)
        arriving = shifted(sent, 1) if sent is not None and tick + 1 < ticks else blank
        (
            k_all, v_all, x_buf, h1_buf, q_buf, o_buf, lse_buf, post_buf, hid_keep, hid_send,
            middle,
        ) = call(
            attend_kernel,
            (
                now, place, starts, rows_in, incoming, blank if sent is None else sent, wp, wo,
                vectors, gains, biases, branches,
            ),
            [SMEM] * 3 + [VMEM] * 9,
            (
                k_all, v_all, x_buf, h1_buf, q_buf, o_buf, lse_buf, post_buf, hid_keep, hid_send,
            ),
            [VMEM, VMEM] + [HBM] * 8,
            [jax.ShapeDtypeStruct((chunk, width), F32)],
            [VMEM],
            SCR["af"](chunk, width, units, length),
            LIMITS[0],
            8 * dense * width,
        )
        h2_buf, g_buf, gp_buf, m_buf, st_buf, mid_buf, sent, rows_in = call(
            expand_kernel,
            (now, place, near_tokens, far_tokens, middle, we, wr, vectors, gains, biases, branches),
            [SMEM, SMEM, HBM, HBM] + [VMEM] * 7,
            (h2_buf, g_buf, gp_buf, m_buf, st_buf, mid_buf),
            [HBM] * 6,
            [jax.ShapeDtypeStruct((chunk, width), BF16)] * 2,
            [VMEM] * 2,
            SCR["ff"](chunk, width, units, length),
            LIMITS[1],
            2 * dense * units,
        )
        incoming = arriving

    last_out = sent
    wrt = flipped(wr, sent)
    wet = flipped(we, wrt)
    wot = flipped(wo, wet)
    wpt = flipped(wp, wot)
    dk_acc, dv_acc = empty([sized(width, F32)] * 2, pltpu.VMEM, wpt)
    sum_f = jnp.zeros((4, width), F32)
    sum_w = jnp.zeros((3, units), F32)
    sum_a = jnp.zeros((7, width), F32)
    incoming = blank
    sent = None

    def weight_gradient(left, right, axis):
        full = dot_tn(left, right).astype(BF16)
        total = lax.psum_scatter(full, "mp", scatter_dimension=axis, tiled=True)
        return (total.astype(F32) * copies).astype(BF16)

    def attend_back(now, after, prev, grad_mid, carried, cost=10):
        return call(
            attend_back_kernel,
            (
                now, place, starts, after, near_cotangent, far_cotangent, prev, grad_mid, wot,
                wpt, vectors, gains, k_all, v_all, x_buf, q_buf, o_buf, lse_buf,
            ),
            [SMEM, SMEM, SMEM, HBM, HBM, HBM] + [VMEM] * 8 + [HBM] * 4,
            carried,
            [VMEM, VMEM, VMEM] + [HBM] * 6,
            [jax.ShapeDtypeStruct((chunk, width), BF16)] * 2,
            [VMEM] * 2,
            SCR["ab"](chunk, width, units, length),
            LIMITS[3],
            cost * 11 * 10**8,
        )

    held = []
    carried = (sum_a, dk_acc, dv_acc, dq_buf, dkr_buf, dvr_buf, dmr_buf, ig_keep, ig_send)
    rows_in = first_rows(place, near_cotangent, far_cotangent, length - chunk, chunk, wpt)
    for tick in range(ticks):
        now = jnp.full((1,), tick, jnp.int32)
        arriving = shifted(sent, -1) if sent is not None and tick + 1 < ticks else blank
        sum_f, sum_w, df_buf, dur_buf, grad_mid = call(
            expand_back_kernel,
            (
                now, place, rows_in, incoming, wrt, wet, vectors, gains, g_buf, gp_buf, st_buf,
                mid_buf,
            ),
            [SMEM, SMEM] + [VMEM] * 6 + [HBM] * 4,
            (sum_f, sum_w, df_buf, dur_buf),
            [VMEM, VMEM] + [HBM] * 2,
            [jax.ShapeDtypeStruct((chunk, width), F32)],
            [VMEM],
            SCR["fb"](chunk, width, units, length),
            LIMITS[2],
            2 * dense * units,
        )
        held.append((now, grad_mid))
        if tick + 2 < ticks:
            held.clear()
            prev = blank if sent is None else sent
            *carried, sent, rows_in = attend_back(now, x_buf, prev, grad_mid, carried)
        incoming = arriving

    def gathered(sum_a):
        shared = jnp.stack([sum_a[5], sum_f[1], sum_a[6], sum_f[2], sum_f[3], sum_f[0]])
        narrow = jnp.stack([sum_a[3], sum_a[4], sum_a[2], sum_a[0], sum_a[1]])
        broad = jnp.stack([sum_w[2], sum_w[0], sum_w[1]])
        return shared, narrow, broad

    def packed(side, sum_a):
        shared, narrow, broad = gathered(sum_a)
        cut, wide_cut = width // 2, units // 2
        return jnp.concatenate(
            [
                shared.reshape(-1),
                narrow[:, side * cut:(side + 1) * cut].reshape(-1),
                broad[:, side * wide_cut:(side + 1) * wide_cut].reshape(-1),
            ]
        )

    def forward_chunk(section, last):
        return ticks - 1 - 2 * section

    def backward_chunk(section, last):
        return count - 1 - (ticks - 1 - 2 * (last - section))

    def finished(rows, chunk_of, keep, send):
        return last_rows(place, rows, chunk_of, count, keep, send)

    if by_links:
        reduce_sides = (m_buf,), (df_buf,), (0,)
        expand_sides = (h2_buf,), (dur_buf,), (0,)
        reduce_other = other_part(*reduce_sides, 0, df_buf)
        expand_other = other_part(*expand_sides, 1, reduce_other)
        pieces = own_part(*reduce_sides, swapped(reduce_other), place, expand_other)
        reduce_sum = BatchSum(pieces, place)
        pieces = own_part(*expand_sides, swapped(expand_other), place, pieces[3])
        expand_sum = BatchSum(pieces, place)
        after = pieces[3]
        for number, (now, grad_mid) in enumerate(held):
            *carried, sent, _ = attend_back(now, after, sent, grad_mid, carried, 1)
            after = reduce_sum.second(carried[-1], 1) if number == 0 else carried[-1]
        sum_a, _, _, dq_buf, dkr_buf, dvr_buf, dmr_buf, ig_keep, ig_send = carried
        mixed_sides = (h1_buf, dmr_buf), (dq_buf, dkr_buf, dvr_buf, post_buf), (0, 0, 0, 1)
        mixed_other = other_part(*mixed_sides, 1, after)
        after = expand_sum.second(mixed_other, COSTS[0])
        pieces = own_part(*mixed_sides, swapped(mixed_other), place, after)
        mixed_sum = BatchSum(pieces, place)
        after = reduce_sum.third(pieces[3], COSTS[1])
        kept = finished(last_out, forward_chunk, hid_keep, hid_send)
        after = hidden = spread_rows(*kept, after)
        small_one, small_two = (packed(side, sum_a).reshape(-1, 128) for side in (0, 1))
        small = plus(small_one, swapped(small_two), after)
        after = mixed_sum.second(after, COSTS[2])
        after = expand_sum.third(after, COSTS[3])
        after = mixed_sum.third(after, COSTS[4])
        kept = finished(sent, backward_chunk, ig_keep, ig_send)
        input_gradient = spread_rows(*kept, after)
        small = plus(small, crossed(small, 1), input_gradient)
        (reduce_grad,) = reduce_sum.result((reduce_weight.shape[1:],), input_gradient)
        small = plus(small, crossed(small, 2), reduce_grad)
        (expand_grad,) = expand_sum.result((expand_weight.shape[1:],), reduce_grad)
        project_grad, output_grad = mixed_sum.result(
            (project_weight.shape[1:], output_weight.shape[1:]), expand_grad
        )
        project_grad = project_grad[None]
    else:
        for now, grad_mid in held:
            *carried, sent, _ = attend_back(now, x_buf, sent, grad_mid, carried)
        sum_a, _, _, dq_buf, dkr_buf, dvr_buf, dmr_buf, ig_keep, ig_send = carried
        kept = finished(last_out, forward_chunk, hid_keep, hid_send)
        hidden = spread_rows(*kept, sent)
        kept = finished(sent, backward_chunk, ig_keep, ig_send)
        input_gradient = spread_rows(*kept, sent)
        reduce_grad, expand_grad, output_grad, *project_grad = (
            total.astype(F32)
            for total in lax.psum(
                (
                    weight_gradient(m_buf, df_buf, 0), weight_gradient(h2_buf, dur_buf, 1),
                    weight_gradient(post_buf, dmr_buf, 0), weight_gradient(h1_buf, dq_buf, 1),
                    weight_gradient(h1_buf, dkr_buf, 1), weight_gradient(h1_buf, dvr_buf, 1),
                ),
                "batch",
            )
        )
        project_grad = jnp.stack(project_grad)[None]

    if paired:
        if not by_links:
            small = lax.psum(packed(0, sum_a) + swapped(packed(1, sum_a)), "batch")
        small = small.reshape(-1)
        here, there = width // 2, units // 2
        shared = small[:6 * width].reshape(6, width)
        narrow = small[6 * width:6 * width + 5 * here].reshape(5, here)
        broad = small[6 * width + 5 * here:].reshape(3, there)
    else:
        shared, narrow, broad = gathered(sum_a)
        small = lax.psum(
            jnp.concatenate([shared.reshape(-1), narrow.reshape(-1), broad.reshape(-1)]),
            ("batch", "mp"),
        ) * copies
        shared = small[:6 * width].reshape(6, width)
        narrow = small[6 * width:11 * width].reshape(5, width)
        broad = small[11 * width:].reshape(3, units)
        narrow = lax.dynamic_slice_in_dim(narrow, part * (width // parts), width // parts, 1)
        broad = lax.dynamic_slice_in_dim(broad, part * (units // parts), units // parts, 1)

    return (
        hidden[None, None],
        input_gradient[None, None],
        shared[0:2][None],
        shared[2:4][None],
        project_grad,
        narrow[0:2][None],
        jnp.sum(narrow[2].reshape(-1, head), axis=1)[None],
        narrow[3][None],
        narrow[4][None],
        output_grad[None],
        expand_grad[None],
        broad[0][None],
        broad[1][None],
        broad[2][None],
        reduce_grad[None],
        shared[4:6][None],
    )


def solution(mesh):
    layered = P("section", None, None)
    split = P("section", "mp")
    rows = P("section", "mp", None)
    columns = P("section", None, "mp")
    projected = P("section", None, None, "mp")
    tokens = P("batch", None, "mp", None)
    states = P("section", "batch", None, "mp", None)
    return jax.shard_map(
        local,
        mesh=mesh,
        in_specs=(
            tokens, tokens, P("batch", None, None, None), layered, layered, projected, columns,
            split, split, split, rows, columns, split, split, split, rows, layered,
        ),
        out_specs=(
            states, states, layered, layered, projected, columns, split, split, split, rows,
            columns, split, split, split, rows, layered,
        ),
        check_vma=False,
    )
```

```python
from functools import partial

import jax
import jax.numpy as jnp
from jax import lax
from jax.experimental import pallas as pl
from jax.experimental.pallas import tpu as pltpu
from jax.sharding import PartitionSpec as P

EPSILON = 1e-05
CHUNK = 128
KEYS = 512
TILE = 512
STRIP = 256
PART = 512
HIDE = -1e30
COSTS = (100, 15, 10, 5, 5)
LIMITS = tuple(size * 2**20 for size in (14, 11, 10))
F32 = jnp.float32
BF16 = jnp.bfloat16
VMEM = pl.BlockSpec(memory_space=pltpu.VMEM)
SMEM = pl.BlockSpec(memory_space=pltpu.SMEM)
HBM = pl.BlockSpec(memory_space=pltpu.HBM)
ANY = pl.BlockSpec(memory_space=pl.ANY)

DMA = pltpu.SemaphoreType.DMA
SCR = {
    "af": lambda chunk, width, units, length: [
        pltpu.VMEM((chunk, width), BF16), pltpu.VMEM((chunk, width), BF16),
        pltpu.VMEM((chunk, width), BF16), pltpu.VMEM((chunk, width), F32),
        pltpu.VMEM((128, chunk), F32), pltpu.VMEM((chunk, width), BF16),
        pltpu.VMEM((chunk, length), F32), pltpu.VMEM((3, chunk, width), BF16), DMA((7,)),
    ],
    "ff": lambda chunk, width, units, length: [
        pltpu.VMEM((chunk, width), BF16), pltpu.VMEM((chunk, units), F32),
        pltpu.VMEM((chunk, units), BF16), pltpu.VMEM((chunk, units), BF16),
        pltpu.VMEM((chunk, units), BF16), pltpu.VMEM((chunk, 128), F32), DMA((7,)),
    ],
    "fb": lambda chunk, width, units, length: [
        pltpu.VMEM((chunk, units), BF16), pltpu.VMEM((chunk, units), BF16),
        pltpu.VMEM((chunk, 128), F32), pltpu.VMEM((chunk, width), F32),
        pltpu.VMEM((chunk, width), BF16), pltpu.VMEM((chunk, units), F32),
        pltpu.VMEM((chunk, units), BF16), pltpu.VMEM((chunk, width), F32),
        DMA((4,)), DMA((2,)),
    ],
    "ab": lambda chunk, width, units, length: [
        pltpu.VMEM((chunk, width), BF16), pltpu.VMEM((chunk, width), BF16),
        pltpu.VMEM((chunk, width), F32), pltpu.VMEM((128, chunk), F32),
        pltpu.VMEM((chunk, width), BF16), pltpu.VMEM((chunk, width), F32),
        pltpu.VMEM((length, chunk), F32), pltpu.VMEM((chunk, width), BF16),
        pltpu.VMEM((chunk, width), BF16), pltpu.VMEM((chunk, width), BF16),
        pltpu.VMEM((chunk, width), BF16), pltpu.VMEM((chunk, width), F32),
        DMA((4,)), DMA((6,)),
    ],
}


def lasts(microseconds):
    flops = int(microseconds * 1.1e9)
    return pl.CostEstimate(flops=flops, bytes_accessed=1024, transcendentals=0)


def dot_nn(left, right):
    return jnp.dot(left, right, preferred_element_type=F32)


def dot_nt(left, right):
    return lax.dot_general(left, right, (((1,), (1,)), ((), ())), preferred_element_type=F32)


def dot_tn(left, right):
    return lax.dot_general(left, right, (((0,), (0,)), ((), ())), preferred_element_type=F32)


def norm_parts(values):
    centre = values - jnp.mean(values, axis=-1, keepdims=True)
    inv_std = lax.rsqrt(jnp.mean(centre * centre, axis=-1, keepdims=True) + EPSILON)
    return centre * inv_std, inv_std


def norm_back(scaled, normed, inv_std):
    mean_one = jnp.mean(scaled, axis=-1, keepdims=True)
    mean_two = jnp.mean(scaled * normed, axis=-1, keepdims=True)
    return inv_std * (scaled - mean_one - normed * mean_two)


def column_sum(values):
    return jnp.sum(values, axis=0, keepdims=True)


def document_start(starts_ref, place):
    first = jnp.zeros_like(place)
    for k in range(starts_ref.shape[0]):
        start = starts_ref[k]
        first = jnp.maximum(first, jnp.where(place >= start, start, 0))
    return first


def half_masks():
    lane = lax.broadcasted_iota(jnp.int32, (1, 128), 1)
    return (lane < 64).astype(BF16), (lane >= 64).astype(BF16)


def stack_heads(pair):
    even, odd = half_masks()
    return jnp.concatenate([pair * even, pair * odd], axis=0)


def pick_heads(stacked):
    rows = stacked.shape[0] // 2
    lane = lax.broadcasted_iota(jnp.int32, (1, 128), 1)
    return jnp.where(lane < 64, stacked[:rows], stacked[rows:])


def copies_of(pairs, sems):
    return [pltpu.make_async_copy(a, b, sems.at[i]) for i, (a, b) in enumerate(pairs)]


def in_hbm(values):
    return [pltpu.with_memory_space_constraint(value, pltpu.HBM) for value in values]


def chunk_rows(place_ref, near_ref, far_ref, first, into, sem, step):
    rows, half = into.shape[0], far_ref.shape[0]
    side = first // half
    inner = first - side * half

    @pl.when(side == place_ref[2])
    def _():
        at = pl.ds(pl.multiple_of(place_ref[3] + inner, rows), rows)
        getattr(pltpu.make_async_copy(near_ref.at[at], into, sem), step)()

    @pl.when(side != place_ref[2])
    def _():
        at = pl.ds(pl.multiple_of(inner, rows), rows)
        getattr(pltpu.make_async_copy(far_ref.at[at], into, sem), step)()


def first_rows(place, near, far, first, rows, after):
    def kernel(place_ref, near_ref, far_ref, after_ref, out_ref, sem):
        del after_ref
        for step in ("start", "wait"):
            chunk_rows(place_ref, near_ref, far_ref, jnp.int32(first), out_ref, sem, step)

    return pl.pallas_call(
        kernel,
        in_specs=[SMEM, HBM, HBM, ANY],
        out_specs=VMEM,
        out_shape=jax.ShapeDtypeStruct((rows, near.shape[1]), near.dtype),
        scratch_shapes=[pltpu.SemaphoreType.DMA],
        compiler_params=pltpu.CompilerParams(vmem_limit_bytes=2**20),
    )(place, *in_hbm([near, far]), after)


def last_rows(place, rows, chunk_of, count, keep, send):
    size = rows.shape[0]

    def kernel(place_ref, rows_ref, keep_in, send_in, keep_buf, send_buf, sem):
        del keep_in, send_in
        chunk = chunk_of(place_ref[0], place_ref[1] - 1)

        @pl.when((chunk >= 0) & (chunk < count))
        def _():
            for step in ("start", "wait"):
                store_rows(place_ref, keep_buf, send_buf, chunk * size, rows_ref, sem, step)

    return pl.pallas_call(
        kernel,
        in_specs=[SMEM, VMEM, HBM, HBM],
        out_specs=[HBM, HBM],
        out_shape=[pltpu.HBM(keep.shape, keep.dtype), pltpu.HBM(send.shape, send.dtype)],
        scratch_shapes=[pltpu.SemaphoreType.DMA],
        input_output_aliases={2: 0, 3: 1},
        compiler_params=pltpu.CompilerParams(vmem_limit_bytes=2**20),
        cost_estimate=lasts(1),
    )(place, rows, keep, send)


def row_of(vec_ref, first, size):
    return jnp.concatenate(
        [vec_ref[0, :, first:first + size], vec_ref[1, :, first:first + size]], axis=1
    )


def aligned(index, size):
    return pl.ds(pl.multiple_of(index * size, size), size)


def attend_kernel(
    tick_ref, section_ref, starts_ref, tok_ref, inc_ref, prev_ref, wp_ref, wo_ref,
    vec_ref, gain_ref, bias_ref, branch_ref,
    k_in, v_in, x_in, h1_in, q_in, o_in, lse_in, post_in, keep_in, send_in,
    k_ref, v_ref, x_buf, h1_buf, q_buf, o_buf, lse_buf, post_buf, keep_buf, send_buf, mid_ref,
    x_s, h1_s, q_s, o_s, lse_s, post_s, hide_s, qkv_s, sems, finish=True,
):
    del k_in, v_in, x_in, h1_in, q_in, o_in, lse_in, post_in, keep_in, send_in
    rows = mid_ref.shape[0]
    length, width = k_ref.shape
    half = width // 2
    section = section_ref[0]
    chunk = tick_ref[0] - 2 * section
    live = (chunk >= 0) & (chunk < length // rows)
    state = (section_ref, keep_buf, send_buf, (chunk - 1) * rows, prev_ref, sems.at[6])

    @pl.when((chunk >= 1) & (chunk <= length // rows))
    def _():
        store_rows(*state, "start")

    def saves():
        here = pl.ds(pl.multiple_of(chunk * rows, rows), rows)
        return copies_of(
            (
                (x_s, x_buf.at[here]), (h1_s, h1_buf.at[here]), (q_s, q_buf.at[here]),
                (o_s, o_buf.at[here]), (lse_s, lse_buf.at[chunk]), (post_s, post_buf.at[here]),
            ),
            sems,
        )

    @pl.when(live)
    def _():
        first = pl.multiple_of(chunk * rows, rows)
        here = pl.ds(first, rows)

        @pl.when(section == 0)
        def _():
            x_s[...] = tok_ref[...]

        @pl.when(section != 0)
        def _():
            x_s[...] = inc_ref[...]

        stores = saves()
        layer_in = x_s[...].astype(F32)
        stores[0].start()
        normed, _ = norm_parts(layer_in)
        h1 = (normed * gain_ref[0:1].astype(F32) + bias_ref[0:1].astype(F32)).astype(BF16)
        h1_s[...] = h1
        stores[1].start()

        def project(number, carry):
            side, which = number // 3, number % 3
            shift = vec_ref[side, :, aligned(which, half)]
            value = dot_nn(h1_s[...], wp_ref[side, which]) + shift
            qkv_s[which, :, aligned(side, half)] = value.astype(BF16)
            return carry

        lax.fori_loop(0, 6, project, 0, unroll=6)
        q_s[...] = qkv_s[0] * jnp.asarray(0.125, BF16)
        k_ref[here, :] = qkv_s[1]
        v_ref[here, :] = qkv_s[2]
        stores[2].start()

        def attend(keys):
            place = first + lax.broadcasted_iota(jnp.int32, (rows, 1), 0)
            start = document_start(starts_ref, place)
            key_at = lax.broadcasted_iota(jnp.int32, (rows, keys), 1)
            hide_s[:, :keys] = jnp.where((key_at <= place) & (key_at >= start), 0.0, HIDE)
            lane = lax.broadcasted_iota(jnp.int32, (rows, 128), 1)

            def one_pair(pair, lse):
                at = pl.ds(pl.multiple_of(pair * 128, 128), 128)
                queries = stack_heads(q_s[:, at])
                hide = hide_s[:, :keys]
                scores = dot_nt(queries, k_ref[0:keys, at]) + jnp.concatenate([hide, hide], axis=0)
                top = jnp.max(scores, axis=-1, keepdims=True)
                raised = jnp.exp(scores - top)
                total = jnp.sum(raised, axis=-1, keepdims=True)
                out = dot_nn(raised.astype(BF16), v_ref[0:keys, at]) / total
                o_s[:, at] = pick_heads(out)
                now = top + jnp.log(total)
                lse = jnp.where(lane == 2 * pair, now[:rows], lse)
                return jnp.where(lane == 2 * pair + 1, now[rows:], lse)

            nothing = jnp.zeros((rows, 128), F32)
            lse = lax.fori_loop(0, width // 128, one_pair, nothing, unroll=2)
            lse_s[...] = lse.T

        for count in range(length // KEYS):

            @pl.when(first // KEYS == count)
            def _():
                attend((count + 1) * KEYS)

        stores[3].start()
        stores[4].start()
        post_normed, _ = norm_parts(o_s[...] * row_of(vec_ref, 3 * half, half))
        post = post_normed * row_of(vec_ref, 4 * half, half) + row_of(vec_ref, 5 * half, half)
        post_s[...] = post.astype(BF16)
        stores[5].start()

        def mix(number, carry):
            at = aligned(number, STRIP)
            total = dot_nn(post_s[:, :half], wo_ref[0, :, at])
            total += dot_nn(post_s[:, half:], wo_ref[1, :, at])
            mid_ref[:, at] = x_s[:, at].astype(F32) + total + branch_ref[0:1, at].astype(F32)
            return carry

        lax.fori_loop(0, width // STRIP, mix, 0, unroll=4)

    def done():
        @pl.when(live)
        def _():
            for copy in saves():
                copy.wait()

        @pl.when((chunk >= 1) & (chunk <= length // rows))
        def _():
            store_rows(*state, "wait")

    if finish:
        done()
    return done


def gelu_parts(pre):
    phi = 0.5 + 0.5 * lax.erf(pre * 0.7071067811865476)
    density = jnp.exp(pre * pre * -0.5) * 0.3989422804014327
    return pre * phi, phi + pre * density


def expand_kernel(
    tick_ref, section_ref, near_ref, far_ref, near_back, far_back, mid_ref, we_ref, wr_ref,
    vec_ref, gain_ref, bias_ref, branch_ref,
    h2_in, g_in, gp_in, m_in, st_in, mid_in,
    h2_buf, g_buf, gp_buf, m_buf, st_buf, mid_buf, out_ref, next_ref,
    h2_s, gf_s, g_s, gp_s, m_s, st_s, sems,
):
    del h2_in, g_in, gp_in, m_in, st_in, mid_in
    rows = mid_ref.shape[0]
    width = mid_ref.shape[1]
    half = we_ref.shape[2]
    units = 2 * half
    tiles = half // TILE
    length = h2_buf.shape[0]
    chunk = tick_ref[0] - 2 * section_ref[0]

    @pl.when((chunk >= 0) & (chunk < length // rows))
    def _():
        here = pl.ds(pl.multiple_of(chunk * rows, rows), rows)
        sent = []

        def send(source, target):
            copy = pltpu.make_async_copy(source, target, sems.at[len(sent)])
            copy.start()
            sent.append(copy)

        send(mid_ref, mid_buf.at[here])
        more = (section_ref[0] == 0) & (chunk + 1 < length // rows)
        fetch = (section_ref, near_ref, far_ref, (chunk + 1) * rows, next_ref, sems.at[6])

        turn = (section_ref[0] == section_ref[1] - 1) & (chunk == length // rows - 1)
        back = (section_ref, near_back, far_back, chunk * rows, next_ref, sems.at[6])

        @pl.when(more)
        def _():
            chunk_rows(*fetch, "start")

        @pl.when(turn)
        def _():
            chunk_rows(*back, "start")

        def wide(tile, which):
            first = 3 * width + which * half + tile % tiles * TILE
            return vec_ref[tile // tiles, :, pl.ds(pl.multiple_of(first, TILE), TILE)]

        normed, _ = norm_parts(mid_ref[...])
        h2 = (normed * gain_ref[1:2].astype(F32) + bias_ref[1:2].astype(F32)).astype(BF16)
        h2_s[...] = h2
        send(h2_s, h2_buf.at[here])
        def expand(tile, total):
            at = aligned(tile, TILE)
            weight = we_ref[tile // tiles, :, aligned(tile % tiles, TILE)]
            active, slope = gelu_parts(dot_nn(h2_s[...], weight) + wide(tile, 0))
            gf_s[:, at] = active
            g_s[:, at] = active.astype(BF16)
            gp_s[:, at] = slope.astype(BF16)
            return total + jnp.sum(active, axis=-1, keepdims=True)

        nothing = jnp.zeros((rows, 1), F32)
        mean = lax.fori_loop(0, 2 * tiles, expand, nothing, unroll=4) / units
        send(g_s, g_buf.at[here])
        send(gp_s, gp_buf.at[here])

        def spread(tile, total):
            centre = gf_s[:, aligned(tile, TILE)] - mean
            return total + jnp.sum(centre * centre, axis=-1, keepdims=True)

        inv_std = lax.rsqrt(lax.fori_loop(0, 2 * tiles, spread, nothing, unroll=8) / units + EPSILON)
        lane = lax.broadcasted_iota(jnp.int32, (rows, 128), 1)
        st_s[...] = jnp.where(lane == 0, mean, inv_std)
        send(st_s, st_buf.at[here])

        def normalise(tile, carry):
            at = aligned(tile, TILE)
            active = (gf_s[:, at] - mean) * inv_std * wide(tile, 1) + wide(tile, 2)
            m_s[:, at] = active.astype(BF16)
            return carry

        lax.fori_loop(0, 2 * tiles, normalise, 0, unroll=4)
        send(m_s, m_buf.at[here])

        def reduce(number, carry):
            at = aligned(number, STRIP)
            total = dot_nn(m_s[:, :half], wr_ref[0, :, at])
            total += dot_nn(m_s[:, half:], wr_ref[1, :, at])
            total += mid_ref[:, at] + branch_ref[1:2, at].astype(F32)
            out_ref[:, at] = total.astype(BF16)
            return carry

        lax.fori_loop(0, width // STRIP, reduce, 0, unroll=2)
        for copy in sent:
            copy.wait()

        @pl.when(more)
        def _():
            chunk_rows(*fetch, "wait")

        @pl.when(turn)
        def _():
            chunk_rows(*back, "wait")


def expand_back_kernel(
    tick_ref, section_ref, cot_ref, inc_ref, wr_ref, we_ref, vec_ref, gain_ref,
    g_buf, gp_buf, st_buf, mid_buf,
    sum_in, wsum_in, df_in, dur_in,
    sum_ref, wsum_ref, df_buf, dur_buf, dmid_ref,
    g_s, gp_s, st_s, mid_s, df_s, z_s, dur_s, dh_s, in_sems, out_sems,
):
    del sum_in, wsum_in, df_in, dur_in
    rows = dmid_ref.shape[0]
    width = dmid_ref.shape[1]
    half = wr_ref.shape[2]
    units = 2 * half
    tiles = half // TILE
    length = g_buf.shape[0]
    count = length // rows
    section = section_ref[0]
    last = section_ref[1] - 1
    chunk = count - 1 - (tick_ref[0] - 2 * (last - section))

    @pl.when((chunk >= 0) & (chunk < count))
    def _():
        here = pl.ds(pl.multiple_of(chunk * rows, rows), rows)
        loads = copies_of(
            (
                (g_buf.at[here], g_s), (st_buf.at[here], st_s), (gp_buf.at[here], gp_s),
                (mid_buf.at[here], mid_s),
            ),
            in_sems,
        )
        loads[0].start()
        loads[1].start()

        @pl.when(section == last)
        def _():
            df_s[...] = cot_ref[...]

        @pl.when(section != last)
        def _():
            df_s[...] = inc_ref[...]

        sent = []

        def send(source, target):
            copy = pltpu.make_async_copy(source, target, out_sems.at[len(sent)])
            copy.start()
            sent.append(copy)

        def gain_of(tile):
            first = 3 * width + half + tile % tiles * TILE
            return vec_ref[tile // tiles, :, pl.ds(pl.multiple_of(first, TILE), TILE)]

        grad_low = df_s[...]
        send(df_s, df_buf.at[here])
        sum_ref[0:1] += column_sum(grad_low.astype(F32))
        loads[0].wait()
        loads[1].wait()
        loads[2].start()
        loads[3].start()
        mean = st_s[:, 0:1]
        inv_std = st_s[:, 1:2]
        def reduce_back(tile, sums):
            at = aligned(tile, TILE)
            weight = wr_ref[tile // tiles, :, aligned(tile % tiles, TILE)]
            grad = dot_nn(df_s[...], weight)
            normed = (g_s[:, at].astype(F32) - mean) * inv_std
            wsum_ref[0:1, at] += column_sum(grad * normed)
            wsum_ref[1:2, at] += column_sum(grad)
            scaled = grad * gain_of(tile)
            z_s[:, at] = scaled
            return (
                sums[0] + jnp.sum(scaled, axis=-1, keepdims=True),
                sums[1] + jnp.sum(scaled * normed, axis=-1, keepdims=True),
            )

        nothing = jnp.zeros((rows, 1), F32)
        one, two = lax.fori_loop(0, 2 * tiles, reduce_back, (nothing, nothing), unroll=4)
        one = one / units
        two = two / units

        def active_back(tile, carry):
            at = aligned(tile, TILE)
            normed = (g_s[:, at].astype(F32) - mean) * inv_std
            grad = inv_std * (z_s[:, at] - one - normed * two) * gp_s[:, at].astype(F32)
            wsum_ref[2:3, at] += column_sum(grad)
            dur_s[:, at] = grad.astype(BF16)
            return carry

        loads[2].wait()
        lax.fori_loop(0, 2 * tiles, active_back, 0, unroll=8)
        send(dur_s, dur_buf.at[here])

        def expand_back(number, carry):
            at = aligned(number, STRIP)
            total = dot_nn(dur_s[:, :half], we_ref[0, :, at])
            dh_s[:, at] = total + dot_nn(dur_s[:, half:], we_ref[1, :, at])
            return carry

        lax.fori_loop(0, width // STRIP, expand_back, 0, unroll=4)
        grad_second = dh_s[...]
        loads[3].wait()
        normed, inv_std = norm_parts(mid_s[...])
        sum_ref[1:2] += column_sum(grad_second * normed)
        sum_ref[2:3] += column_sum(grad_second)
        grad_mid = grad_low.astype(F32) + norm_back(
            grad_second * gain_ref[1:2].astype(F32), normed, inv_std
        )
        sum_ref[3:4] += column_sum(grad_mid)
        dmid_ref[...] = grad_mid
        for copy in sent:
            copy.wait()


def attend_back_kernel(
    tick_ref, section_ref, starts_ref, after, near_ref, far_ref, prev_ref, dmid_ref, wo_ref,
    wp_ref, vec_ref, gain_ref, k_ref, v_ref,
    x_buf, q_buf, o_buf, lse_buf,
    sum_in, dk_in, dv_in, dq_in, dkr_in, dvr_in, dmr_in, keep_in, send_in,
    sum_ref, dk_ref, dv_ref, dq_buf, dkr_buf, dvr_buf, dmr_buf, keep_buf, send_buf, out_ref,
    next_ref,
    x_s, q_s, o_s, lse_s, do_s, dqf_s, hide_s, dq_s, dkr_s, dvr_s, low_s, wide_s, in_sems,
    out_sems,
):
    del after, sum_in, dk_in, dv_in, dq_in, dkr_in, dvr_in, dmr_in, keep_in, send_in
    rows = dmid_ref.shape[0]
    length, width = k_ref.shape
    half = width // 2
    count = length // rows
    section = section_ref[0]
    last = section_ref[1] - 1
    chunk = count - 1 - (tick_ref[0] - 2 * (last - section))

    def fetches():
        here = pl.ds(pl.multiple_of(chunk * rows, rows), rows)
        return copies_of(
            (
                (o_buf.at[here], o_s), (q_buf.at[here], q_s), (lse_buf.at[chunk], lse_s),
                (x_buf.at[here], x_s),
            ),
            in_sems,
        )

    @pl.when((chunk >= 0) & (chunk < count))
    def _():
        for copy in fetches():
            copy.start()

    state = (section_ref, keep_buf, send_buf, (chunk + 1) * rows, prev_ref, out_sems.at[4])

    @pl.when((chunk >= -1) & (chunk < count - 1))
    def _():
        store_rows(*state, "start")

    @pl.when((chunk >= 0) & (chunk < count))
    def _():
        first = pl.multiple_of(chunk * rows, rows)
        here = pl.ds(first, rows)
        loads = fetches()

        @pl.when(chunk == count - 1)
        def _():
            dk_ref[...] = jnp.zeros_like(dk_ref)
            dv_ref[...] = jnp.zeros_like(dv_ref)

        more = (section == last) & (chunk >= 1)
        fetch = (section_ref, near_ref, far_ref, (chunk - 1) * rows, next_ref, out_sems.at[5])

        @pl.when(more)
        def _():
            chunk_rows(*fetch, "start")

        sent = []

        def send(source, target):
            copy = pltpu.make_async_copy(source, target, out_sems.at[len(sent)])
            copy.start()
            sent.append(copy)

        low_s[...] = dmid_ref[...].astype(BF16)
        send(low_s, dmr_buf.at[here])

        def mix_back(side, carry):
            wide_s[:, aligned(side, half)] = dot_nn(low_s[...], wo_ref[side])
            return carry

        lax.fori_loop(0, 2, mix_back, 0, unroll=2)
        grad_post = wide_s[...]
        loads[0].wait()
        attended = o_s[...]
        scale = row_of(vec_ref, 3 * half, half)
        normed, inv_std = norm_parts(attended * scale)
        sum_ref[0:1] += column_sum(grad_post * normed)
        sum_ref[1:2] += column_sum(grad_post)
        grad_mixed = norm_back(grad_post * row_of(vec_ref, 4 * half, half), normed, inv_std)
        sum_ref[2:3] += column_sum(grad_mixed * attended)
        do_s[...] = (grad_mixed * scale).astype(BF16)

        loads[1].wait()
        loads[2].wait()

        def attend(keys):
            place = first + lax.broadcasted_iota(jnp.int32, (1, rows), 1)
            start = document_start(starts_ref, place)
            key_at = lax.broadcasted_iota(jnp.int32, (keys, rows), 0)
            hide_s[:keys, :] = jnp.where((key_at <= place) & (key_at >= start), 0.0, HIDE)

            def one_pair(pair, carry):
                at = pl.ds(pl.multiple_of(pair * 128, 128), 128)
                queries = stack_heads(q_s[:, at])
                grad_pair = do_s[:, at]
                grads = stack_heads(grad_pair)
                product = (grad_pair.astype(F32) * o_s[:, at]).T
                delta = jnp.concatenate(
                    [column_sum(product[:64]), column_sum(product[64:])], axis=1
                )
                lse = jnp.concatenate(
                    [lse_s[pl.ds(2 * pair, 1), :], lse_s[pl.ds(2 * pair + 1, 1), :]], axis=1
                )
                hide = hide_s[:keys, :]
                key_pair = k_ref[0:keys, at]
                scores = dot_nt(key_pair, queries) + jnp.concatenate([hide, hide], axis=1)
                probs = jnp.exp(scores - lse)
                grad_probs = dot_nt(v_ref[0:keys, at], grads)
                grad_scores = (probs * (grad_probs - delta)).astype(BF16)
                dk_ref[0:keys, at] += dot_nn(grad_scores, queries)
                dv_ref[0:keys, at] += dot_nn(probs.astype(BF16), grads)
                dqf_s[:, at] = pick_heads(dot_tn(grad_scores, key_pair)) * 0.125
                return carry

            lax.fori_loop(0, width // 128, one_pair, 0, unroll=2)

        for number in range(length // KEYS):

            @pl.when(first // KEYS == number)
            def _():
                attend((number + 1) * KEYS)

        grad_query = dqf_s[...]
        grad_value = dv_ref[here, :]
        sum_ref[3:4] += column_sum(grad_query)
        sum_ref[4:5] += column_sum(grad_value)
        dq_s[...] = grad_query.astype(BF16)
        dkr_s[...] = dk_ref[here, :].astype(BF16)
        dvr_s[...] = grad_value.astype(BF16)
        send(dq_s, dq_buf.at[here])
        send(dkr_s, dkr_buf.at[here])
        send(dvr_s, dvr_buf.at[here])

        def project_back(number, carry):
            at = aligned(number, STRIP)
            total = jnp.zeros((rows, STRIP), F32)
            for which, part in enumerate((dq_s, dkr_s, dvr_s)):
                total += dot_nn(part[:, :half], wp_ref[0, which, :, at])
                total += dot_nn(part[:, half:], wp_ref[1, which, :, at])
            wide_s[:, at] = total
            return carry

        lax.fori_loop(0, width // STRIP, project_back, 0, unroll=4)
        grad_first = wide_s[...]
        loads[3].wait()
        normed, inv_std = norm_parts(x_s[...].astype(F32))
        sum_ref[5:6] += column_sum(grad_first * normed)
        sum_ref[6:7] += column_sum(grad_first)
        out = dmid_ref[...] + norm_back(
            grad_first * gain_ref[0:1].astype(F32), normed, inv_std
        )
        out_ref[...] = out.astype(BF16)
        for copy in sent:
            copy.wait()

        @pl.when(more)
        def _():
            chunk_rows(*fetch, "wait")

    @pl.when((chunk >= -1) & (chunk < count - 1))
    def _():
        store_rows(*state, "wait")


def forward_kernel(
    tick_ref, section_ref, starts_ref, near_ref, far_ref, near_back, far_back, tok_ref, inc_ref,
    prev_ref, wp_ref, wo_ref, we_ref, wr_ref, vec_ref, gain_ref, bias_ref, branch_ref, *refs,
):
    ins, outs, (out_ref, next_ref, mid_s), scratch = refs[:16], refs[16:32], refs[32:35], refs[35:]
    shared = vec_ref, gain_ref, bias_ref, branch_ref
    done = attend_kernel(
        tick_ref, section_ref, starts_ref, tok_ref, inc_ref, prev_ref, wp_ref, wo_ref, *shared,
        *ins[:10], *outs[:10], mid_s, *scratch[:9], finish=False,
    )
    expand_kernel(
        tick_ref, section_ref, near_ref, far_ref, near_back, far_back, mid_s, we_ref, wr_ref,
        *shared,
        *ins[10:], *outs[10:], out_ref, next_ref, *scratch[9:],
    )
    done()


def flip_kernel(source, after, target):
    del after
    size = 256

    def flip(one, two):
        def body(step, carry):
            at = aligned(step, size)
            two[:, at] = one[at, :].T
            return carry

        lax.fori_loop(0, one.shape[0] // size, body, 0)

    def each(index, carry):
        if len(source.shape) == 3:
            flip(source.at[index], target.at[index])
        else:
            deep = source.shape[1]
            flip(source.at[index // deep, index % deep], target.at[index // deep, index % deep])
        return carry

    count = source.shape[0] * (source.shape[1] if len(source.shape) == 4 else 1)
    lax.fori_loop(0, count, each, 0)


def flipped(weight, after):
    shape = weight.shape[:-2] + (weight.shape[-1], weight.shape[-2])
    return pl.pallas_call(
        flip_kernel,
        in_specs=[VMEM, ANY],
        out_specs=VMEM,
        out_shape=pltpu.VMEM(shape, BF16),
        compiler_params=pltpu.CompilerParams(vmem_limit_bytes=2 * 2**20),
    )(weight, after)


def load_kernel(side, source, after, *refs):
    del after
    copy = pltpu.make_async_copy(source, refs[-2].at[side], refs[-1])
    copy.start()
    copy.wait()


def loaded(side, value, both, after):
    known = [] if both is None else [both]
    return pl.pallas_call(
        partial(load_kernel, side),
        in_specs=[HBM, ANY] + [VMEM] * len(known),
        out_specs=VMEM,
        out_shape=pltpu.VMEM((2, *value.shape), value.dtype),
        scratch_shapes=[pltpu.SemaphoreType.DMA],
        input_output_aliases={2: 0} if known else {},
        compiler_params=pltpu.CompilerParams(vmem_limit_bytes=2**20),
    )(*in_hbm([value]), after, *known)


def empty_kernel(*refs):
    del refs


def empty(shapes, space, *after):
    return pl.pallas_call(
        empty_kernel,
        in_specs=[ANY] * len(after),
        out_specs=[pl.BlockSpec(memory_space=space)] * len(shapes),
        out_shape=[space(shape, dtype) for shape, dtype in shapes],
        compiler_params=pltpu.CompilerParams(vmem_limit_bytes=2**20),
    )(*after)


def call(kernel, inputs, specs, carried, carried_specs, fresh, fresh_specs, scratch, limit, flops):
    first = len(inputs)
    inputs = [
        pltpu.with_memory_space_constraint(a, pltpu.HBM) if spec is HBM else a
        for a, spec in zip(inputs, specs)
    ]
    shapes = [
        pltpu.HBM(a.shape, a.dtype) if spec is HBM else jax.ShapeDtypeStruct(a.shape, a.dtype)
        for a, spec in zip(carried, carried_specs)
    ] + fresh
    return pl.pallas_call(
        kernel,
        in_specs=specs + carried_specs,
        out_specs=carried_specs + fresh_specs,
        out_shape=shapes,
        scratch_shapes=scratch,
        input_output_aliases={first + i: i for i in range(len(carried))},
        compiler_params=pltpu.CompilerParams(vmem_limit_bytes=limit),
        cost_estimate=pl.CostEstimate(flops=flops, bytes_accessed=2**22, transcendentals=0),
    )(*inputs, *carried)


def settle_kernel(place_ref, *refs):
    pieces, (*outs, wide_s, turn_s, sems) = refs[:8], refs[8:]
    rows = pieces[0].shape[0]
    low, high = place_ref[4], place_ref[5]
    copies = []
    for number, piece in enumerate(pieces):
        half, flips = number // 4, number % 4
        first = (low, high)[half] ^ (flips // 2)
        second = (high, low)[half] ^ (flips % 2)
        slot = number % 2
        if number >= 2:
            for copy in copies[number - 2]:
                copy.wait()
        wide_s[slot] = piece[...].astype(F32)
        at = pl.ds(pl.multiple_of((half * 4 + first * 2 + second) * rows, rows), rows)
        moves = []
        if len(outs) == 1:
            moves.append((wide_s.at[slot], outs[0].at[at]))
        else:
            layers, _, columns = outs[0].shape
            for layer in range(layers):
                source = wide_s.at[slot, :, layer * columns:(layer + 1) * columns]
                moves.append((source, outs[0].at[layer, at]))
            turn_s[slot] = wide_s[slot, :, layers * columns:].T
            moves.append((turn_s.at[slot], outs[1].at[:, at]))
        started = [
            pltpu.make_async_copy(source, target, sems.at[slot, i])
            for i, (source, target) in enumerate(moves)
        ]
        for copy in started:
            copy.start()
        copies.append(started)
    for copy in copies[6] + copies[7]:
        copy.wait()


def settle(place, pieces, shapes, after, cost):
    rows, columns = pieces[0].shape
    turn = (2, shapes[1][0], rows) if len(shapes) > 1 else (2, 8, 128)

    def kernel(place_ref, *refs):
        settle_kernel(place_ref, *refs[:8], *refs[9:])

    return pl.pallas_call(
        kernel,
        grid=(1,),
        in_specs=[SMEM]
        + [pl.BlockSpec((rows, columns), lambda i: (0, 0), pipeline_mode=pl.Buffered(1))] * 8
        + [HBM],
        out_specs=[HBM] * len(shapes),
        out_shape=[pltpu.HBM(shape, F32) for shape in shapes],
        scratch_shapes=[
            pltpu.VMEM((2, rows, columns), F32), pltpu.VMEM(turn, F32),
            pltpu.SemaphoreType.DMA((2, 4)),
        ],
        compiler_params=pltpu.CompilerParams(vmem_limit_bytes=12 * 2**20),
        cost_estimate=lasts(cost),
    )(place, *pieces, *in_hbm([after]))


def crossed(value, bit):
    route = [(i, i ^ bit) for i in range(lax.axis_size("batch"))]
    return lax.ppermute(value, "batch", route)


def products(lefts, rights, pairs, columns, tile, store):
    part = min(tile, PART)

    def body(index, carry):
        at = aligned(index, part)
        for number, right in enumerate(rights):
            where = slice(number * columns, (number + 1) * columns)
            store(at, where, dot_tn(lefts[pairs[number]][:, at], right[...]))
        return carry

    if tile == part:
        body(0, 0)
    else:
        lax.fori_loop(0, tile // part, body, 0)


def other_part(lefts, rights, pairs, axis, after, cost=1):
    length = lefts[0].shape[0]
    rows = lefts[0].shape[1] // (2 if axis == 0 else 1)
    columns = rights[0].shape[1] // (1 if axis == 0 else 2)
    tile = rows // 4
    skip = 4 if axis == 0 else 0
    side = 0 if axis == 0 else 1

    def kernel(*refs):
        def store(at, where, value):
            refs[-1][at, where] = value.astype(BF16)

        inputs = refs[:len(lefts)], refs[len(lefts):len(lefts) + len(rights)]
        products(*inputs, pairs, columns, tile, store)

    return pl.pallas_call(
        kernel,
        grid=(rows // tile,),
        in_specs=[pl.BlockSpec((length, tile), lambda i: (0, skip + i))] * len(lefts)
        + [pl.BlockSpec((length, columns), lambda i: (0, side), pipeline_mode=pl.Buffered(1))]
        * len(rights)
        + [HBM],
        out_specs=pl.BlockSpec((tile, columns * len(rights)), lambda i: (i, 0)),
        out_shape=pltpu.HBM((rows, columns * len(rights)), BF16),
        compiler_params=pltpu.CompilerParams(vmem_limit_bytes=12 * 2**20),
        cost_estimate=lasts(cost),
    )(*in_hbm(lefts), *in_hbm(rights), *in_hbm([after]))


def own_part(lefts, rights, pairs, come, place, after, cost=1):
    length = lefts[0].shape[0]
    rows, whole = come.shape
    columns = whole // len(rights)
    tile = rows // 4

    def at(i, place):
        low, high = place[4], place[5]
        first = jnp.where(i == 0, 1 - low, 3 - high)
        return jnp.where(i < 2, first, jnp.where(i == 2, low, 2 + high))

    def kernel(place_ref, *refs):
        del place_ref
        come_ref = refs[len(lefts) + len(rights)]
        *outs, low_s, sems = refs[-6:]
        step = pl.program_id(0)
        slot = step % 2

        def store(number):
            return pltpu.make_async_copy(
                low_s.at[number % 2], outs[number], sems.at[number % 2]
            )

        for number in (2, 3):

            @pl.when(step == number)
            def _():
                store(number - 2).wait()

        def keep(at, where, value):
            low_s[slot, at, where] = (value + come_ref[at, where].astype(F32)).astype(BF16)

        inputs = refs[:len(lefts)], refs[len(lefts):len(lefts) + len(rights)]
        products(*inputs, pairs, columns, tile, keep)
        for number in range(4):

            @pl.when(step == number)
            def _():
                store(number).start()

        @pl.when(step == 3)
        def _():
            store(2).wait()
            store(3).wait()

    return pl.pallas_call(
        kernel,
        grid_spec=pltpu.PrefetchScalarGridSpec(
            num_scalar_prefetch=1,
            grid=(4,),
            in_specs=[pl.BlockSpec((length, tile), lambda i, place: (0, at(i, place)))]
            * len(lefts)
            + [
                pl.BlockSpec(
                    (length, columns), lambda i, place: (0, 0), pipeline_mode=pl.Buffered(1)
                )
            ]
            * len(rights)
            + [pl.BlockSpec((tile, whole), lambda i, place: (at(i, place), 0)), HBM],
            out_specs=[HBM] * 4,
            scratch_shapes=[
                pltpu.VMEM((2, tile, whole), BF16), pltpu.SemaphoreType.DMA((2,))
            ],
        ),
        out_shape=[pltpu.HBM((tile, whole), BF16)] * 4,
        compiler_params=pltpu.CompilerParams(vmem_limit_bytes=12 * 2**20),
        cost_estimate=lasts(cost),
    )(place, *in_hbm(lefts), *in_hbm(rights), come, *in_hbm([after]))


def add_kernel(split, place_ref, *refs):
    keeps, comes = (refs[0], refs[2]), (refs[1], refs[3])
    outs = refs[5:]
    for half, bit in ((0, 5), (1, 4)):
        keep, come = keeps[half], comes[half]
        if split:
            rows = keep.shape[0] // 2
            side = place_ref[bit]
            for number, where in ((0, 1 - side), (1, side)):
                at = pl.ds(pl.multiple_of(where * rows, rows), rows)
                outs[2 * half + number][...] = (
                    keep[at, :].astype(F32) + come[at, :].astype(F32)
                ).astype(BF16)
        else:
            outs[half][...] = (keep[...].astype(F32) + come[...].astype(F32)).astype(BF16)


def added(keeps, comes, place, split, after, cost):
    rows, columns = keeps[0].shape
    kept = rows // 2 if split else rows
    count = 4 if split else 2
    return pl.pallas_call(
        partial(add_kernel, split),
        grid=(1,),
        in_specs=[SMEM]
        + [pl.BlockSpec((rows, columns), lambda i: (0, 0), pipeline_mode=pl.Buffered(1))] * 4
        + [HBM],
        out_specs=[
            pl.BlockSpec((kept, columns), lambda i: (0, 0), pipeline_mode=pl.Buffered(1))
        ]
        * count,
        out_shape=[pltpu.HBM((kept, columns), BF16)] * count,
        compiler_params=pltpu.CompilerParams(vmem_limit_bytes=12 * 2**20),
        cost_estimate=lasts(cost),
    )(place, keeps[0], comes[0], keeps[1], comes[1], *in_hbm([after]))


class BatchSum:
    def __init__(self, pieces, place):
        send_a, send_b, keep_a, keep_b = pieces
        self.place = place
        self.keeps = keep_a, keep_b
        self.comes = crossed(send_a, 1), crossed(send_b, 2)

    def second(self, after, cost):
        send_a, keep_a, send_b, keep_b = added(self.keeps, self.comes, self.place, True, after, cost)
        self.keeps = keep_a, keep_b
        self.comes = crossed(send_a, 2), crossed(send_b, 1)
        return keep_a

    def third(self, after, cost):
        a, b = added(self.keeps, self.comes, self.place, False, after, cost)
        across_a, across_b = crossed(a, 2), crossed(b, 1)
        self.pieces = [
            a, across_a, crossed(a, 1), crossed(across_a, 1),
            b, across_b, crossed(b, 2), crossed(across_b, 2),
        ]
        return a

    def result(self, shapes, after, cost=1):
        return settle(self.place, self.pieces, shapes, after, cost)


def keep_kernel(place_ref, come_ref, in_ref, out_ref, sem):
    del in_ref
    copy = pltpu.make_async_copy(come_ref, out_ref.at[1 - place_ref[2]], sem)
    copy.start()
    copy.wait()


def with_other_half(kept, come, place, after):
    def kernel(place_ref, come_ref, after_ref, *refs):
        keep_kernel(place_ref, come_ref, *refs)

    return pl.pallas_call(
        kernel,
        in_specs=[SMEM, VMEM, HBM, HBM],
        out_specs=HBM,
        out_shape=pltpu.HBM(kept.shape, kept.dtype),
        scratch_shapes=[pltpu.SemaphoreType.DMA],
        compiler_params=pltpu.CompilerParams(vmem_limit_bytes=4 * 2**20),
        input_output_aliases={3: 0},
        cost_estimate=lasts(3),
    )(place, come, *in_hbm([after]), kept)


def plus_kernel(one, two, after, out):
    del after
    out[...] = one[...] + two[...]


def plus(one, two, after):
    return pl.pallas_call(
        plus_kernel,
        in_specs=[VMEM, VMEM, HBM],
        out_specs=VMEM,
        out_shape=jax.ShapeDtypeStruct(one.shape, one.dtype),
        compiler_params=pltpu.CompilerParams(vmem_limit_bytes=2**20),
        cost_estimate=lasts(1),
    )(one, two, *in_hbm([after]))


def store_rows(place_ref, keep_buf, send_buf, first, source, sem, back):
    rows = source.shape[0]
    half = send_buf.shape[0]
    side = first // half
    at = pl.ds(pl.multiple_of(first - side * half, rows), rows)

    @pl.when(side == place_ref[2])
    def _():
        copy = pltpu.make_async_copy(source, keep_buf.at[side, at], sem)
        getattr(copy, back)()

    @pl.when(side != place_ref[2])
    def _():
        copy = pltpu.make_async_copy(source, send_buf.at[at], sem)
        getattr(copy, back)()


def local(
    tokens, cotangent, document_starts, pre_gain, pre_bias, project_weight, project_bias,
    head_scale, post_gain, post_bias, output_weight, expand_weight, expand_bias, middle_gain,
    middle_bias, reduce_weight, branch_bias,
):
    sections = lax.axis_size("section")
    section = lax.axis_index("section")
    parts = lax.axis_size("mp")
    part = lax.axis_index("mp")
    shard = lax.axis_index("batch")
    micro, rows_here, width = tokens.shape[1:]
    length = rows_here * parts
    chunk = CHUNK
    count = length // chunk
    head = width // (head_scale.shape[1] * parts)
    units = expand_bias.shape[1] * parts
    paired = parts == 2 and micro == 2
    by_links = paired and lax.axis_size("batch") == 4
    block = part * micro // parts
    copies = micro / parts

    def swapped(value):
        return lax.ppermute(value, "mp", [(0, 1), (1, 0)])

    def both(value, axis):
        if paired:
            return value, swapped(value)
        whole = lax.all_gather(value, "mp", axis=axis, tiled=True)
        return tuple(jnp.split(whole, 2, axis=axis))

    def row_source(value):
        if paired:
            theirs = lax.dynamic_index_in_dim(value, 1 - part, 0, keepdims=False)
            return value.reshape(micro * rows_here, width), swapped(theirs)
        whole = lax.all_gather(value, "mp", axis=1, tiled=True)
        whole = lax.dynamic_index_in_dim(whole, block, 0, keepdims=False)
        return whole[:length // 2], whole[length // 2:]

    def spread_rows(kept, sent, after):
        if paired:
            return with_other_half(kept, swapped(sent), place, after)
        whole = lax.all_gather(jnp.concatenate([kept[0], sent]), "mp", axis=0)[:: parts // micro]
        return lax.dynamic_slice_in_dim(whole, part * rows_here, rows_here, 1)

    near_tokens, far_tokens = row_source(tokens[0])
    place = jnp.stack(
        [
            section, jnp.int32(sections), part if paired else jnp.int32(0),
            part * rows_here if paired else jnp.int32(0), shard % 2, shard // 2,
        ]
    ).astype(jnp.int32)
    starts = lax.dynamic_index_in_dim(document_starts[0], block, 0, keepdims=False)[0]
    fields = (
        project_bias[0, 0], jnp.zeros_like(project_bias[0, 0]), project_bias[0, 1],
        jnp.repeat(head_scale[0], head), post_gain[0],
        post_bias[0], expand_bias[0], middle_gain[0], middle_bias[0],
    )
    if paired:
        own = jnp.concatenate(fields)[None]
        other = swapped(own)
    else:
        sides = [both(field, 0) for field in fields]
        own = jnp.concatenate([a for a, _ in sides])[None]
        other = jnp.concatenate([b for _, b in sides])[None]
    gains, biases, branches = pre_gain[0], pre_bias[0], branch_bias[0]
    wp_a, wp_b = both(project_weight[0], 2)
    wo_a, wo_b = both(output_weight[0], 0)
    we_a, we_b = both(expand_weight[0], 1)
    wr_a, wr_b = both(reduce_weight[0], 0)
    wp = loaded(0, wp_a, None, place)
    wo = loaded(0, wo_a, None, wp)
    we = loaded(0, we_a, None, wo)
    wr = loaded(0, wr_a, None, we)
    wr_own = wr
    wp = loaded(1, wp_b, wp, wr)
    wo = loaded(1, wo_b, wo, wp)
    we = loaded(1, we_b, we, wo)
    wr = loaded(1, wr_b, wr, we)
    vectors = jnp.stack([own, other]).astype(F32)
    near_cotangent, far_cotangent = row_source(cotangent[0])

    def sized(columns, dtype):
        return ((length, columns), dtype)

    halves = (((2, length // 2, width), BF16), ((length // 2, width), BF16))

    (
        x_buf, h1_buf, q_buf, o_buf, lse_buf, post_buf, mid_buf,
        h2_buf, g_buf, gp_buf, m_buf, st_buf, hid_keep, hid_send,
        df_buf, dur_buf, dmr_buf, dq_buf, dkr_buf, dvr_buf, ig_keep, ig_send,
    ) = empty(
        [
            sized(width, BF16), sized(width, BF16), sized(width, BF16), sized(width, F32),
            ((count, 128, chunk), F32), sized(width, BF16), sized(width, F32),
            sized(width, BF16), sized(units, BF16), sized(units, BF16), sized(units, BF16),
            sized(128, F32), *halves,
            sized(width, BF16), sized(units, BF16), sized(width, BF16), sized(width, BF16),
            sized(width, BF16), sized(width, BF16), *halves,
        ],
        pltpu.HBM,
    )
    k_all = jnp.zeros((length, width), BF16)
    v_all = jnp.zeros((length, width), BF16)
    dense = 2 * chunk * width

    def shifted(value, distance):
        route = [(i, i + distance) for i in range(sections) if 0 <= i + distance < sections]
        return lax.ppermute(value, "section", route)

    ticks = count + 2 * (sections - 1)
    blank = jnp.zeros((chunk, width), BF16)
    incoming = blank
    sent = None
    rows_in = first_rows(place, near_tokens, far_tokens, 0, chunk, wr_own)
    kept = (
        k_all, v_all, x_buf, h1_buf, q_buf, o_buf, lse_buf, post_buf, hid_keep, hid_send,
        h2_buf, g_buf, gp_buf, m_buf, st_buf, mid_buf,
    )
    for tick in range(ticks):
        now = jnp.full((1,), tick, jnp.int32)
        arriving = shifted(sent, 1) if sent is not None and tick + 1 < ticks else blank
        *kept, sent, rows_in = call(
            forward_kernel,
            (
                now, place, starts, near_tokens, far_tokens, near_cotangent, far_cotangent,
                rows_in, incoming, blank if sent is None else sent, wp, wo, we, wr, vectors, gains, biases, branches,
            ),
            [SMEM, SMEM, SMEM] + [HBM] * 4 + [VMEM] * 11,
            kept,
            [VMEM, VMEM] + [HBM] * 14,
            [jax.ShapeDtypeStruct((chunk, width), BF16)] * 2,
            [VMEM] * 2,
            [
                pltpu.VMEM((chunk, width), F32), *SCR["af"](chunk, width, units, length),
                *SCR["ff"](chunk, width, units, length),
            ],
            LIMITS[0],
            4 * dense * units,
        )
        incoming = arriving

    (
        k_all, v_all, x_buf, h1_buf, q_buf, o_buf, lse_buf, post_buf, hid_keep, hid_send,
        h2_buf, g_buf, gp_buf, m_buf, st_buf, mid_buf,
    ) = kept
    last_out = sent
    wrt = flipped(wr, sent)
    wpt = flipped(wp, wrt)
    wet = flipped(we, wpt)
    wot = flipped(wo, wet)
    dk_acc, dv_acc = empty([sized(width, F32)] * 2, pltpu.VMEM, wpt)
    sum_f = jnp.zeros((4, width), F32)
    sum_w = jnp.zeros((3, units), F32)
    sum_a = jnp.zeros((7, width), F32)
    incoming = blank
    sent = None

    def weight_gradient(left, right, axis):
        full = dot_tn(left, right).astype(BF16)
        total = lax.psum_scatter(full, "mp", scatter_dimension=axis, tiled=True)
        return (total.astype(F32) * copies).astype(BF16)

    def attend_back(now, after, prev, grad_mid, carried, cost=10):
        return call(
            attend_back_kernel,
            (
                now, place, starts, after, near_cotangent, far_cotangent, prev, grad_mid, wot,
                wpt, vectors, gains, k_all, v_all, x_buf, q_buf, o_buf, lse_buf,
            ),
            [SMEM, SMEM, SMEM, HBM, HBM, HBM] + [VMEM] * 8 + [HBM] * 4,
            carried,
            [VMEM, VMEM, VMEM] + [HBM] * 6,
            [jax.ShapeDtypeStruct((chunk, width), BF16)] * 2,
            [VMEM] * 2,
            SCR["ab"](chunk, width, units, length),
            LIMITS[2],
            cost * 11 * 10**8,
        )

    held = []
    carried = (sum_a, dk_acc, dv_acc, dq_buf, dkr_buf, dvr_buf, dmr_buf, ig_keep, ig_send)
    for tick in range(ticks):
        now = jnp.full((1,), tick, jnp.int32)
        arriving = shifted(sent, -1) if sent is not None and tick + 1 < ticks else blank
        sum_f, sum_w, df_buf, dur_buf, grad_mid = call(
            expand_back_kernel,
            (
                now, place, rows_in, incoming, wrt, wet, vectors, gains, g_buf, gp_buf, st_buf,
                mid_buf,
            ),
            [SMEM, SMEM] + [VMEM] * 6 + [HBM] * 4,
            (sum_f, sum_w, df_buf, dur_buf),
            [VMEM, VMEM] + [HBM] * 2,
            [jax.ShapeDtypeStruct((chunk, width), F32)],
            [VMEM],
            SCR["fb"](chunk, width, units, length),
            LIMITS[1],
            2 * dense * units,
        )
        held.append((now, grad_mid))
        if tick + 2 < ticks:
            held.clear()
            prev = blank if sent is None else sent
            *carried, sent, rows_in = attend_back(now, x_buf, prev, grad_mid, carried)
        incoming = arriving

    def gathered(sum_a):
        shared = jnp.stack([sum_a[5], sum_f[1], sum_a[6], sum_f[2], sum_f[3], sum_f[0]])
        narrow = jnp.stack([sum_a[3], sum_a[4], sum_a[2], sum_a[0], sum_a[1]])
        broad = jnp.stack([sum_w[2], sum_w[0], sum_w[1]])
        return shared, narrow, broad

    def packed(side, sum_a):
        shared, narrow, broad = gathered(sum_a)
        cut, wide_cut = width // 2, units // 2
        return jnp.concatenate(
            [
                shared.reshape(-1),
                narrow[:, side * cut:(side + 1) * cut].reshape(-1),
                broad[:, side * wide_cut:(side + 1) * wide_cut].reshape(-1),
            ]
        )

    def forward_chunk(section, last):
        return ticks - 1 - 2 * section

    def backward_chunk(section, last):
        return count - 1 - (ticks - 1 - 2 * (last - section))

    def finished(rows, chunk_of, keep, send):
        return last_rows(place, rows, chunk_of, count, keep, send)

    if by_links:
        reduce_sides = (m_buf,), (df_buf,), (0,)
        expand_sides = (h2_buf,), (dur_buf,), (0,)
        reduce_other = other_part(*reduce_sides, 0, df_buf)
        expand_other = other_part(*expand_sides, 1, reduce_other)
        pieces = own_part(*reduce_sides, swapped(reduce_other), place, expand_other)
        reduce_sum = BatchSum(pieces, place)
        pieces = own_part(*expand_sides, swapped(expand_other), place, pieces[3])
        expand_sum = BatchSum(pieces, place)
        after = pieces[3]
        for number, (now, grad_mid) in enumerate(held):
            *carried, sent, _ = attend_back(now, after, sent, grad_mid, carried, 1)
            after = reduce_sum.second(carried[-1], 1) if number == 0 else carried[-1]
        sum_a, _, _, dq_buf, dkr_buf, dvr_buf, dmr_buf, ig_keep, ig_send = carried
        mixed_sides = (h1_buf, dmr_buf), (dq_buf, dkr_buf, dvr_buf, post_buf), (0, 0, 0, 1)
        mixed_other = other_part(*mixed_sides, 1, after)
        after = expand_sum.second(mixed_other, COSTS[0])
        pieces = own_part(*mixed_sides, swapped(mixed_other), place, after)
        mixed_sum = BatchSum(pieces, place)
        after = reduce_sum.third(pieces[3], COSTS[1])
        kept = finished(last_out, forward_chunk, hid_keep, hid_send)
        after = hidden = spread_rows(*kept, after)
        small_one, small_two = (packed(side, sum_a).reshape(-1, 128) for side in (0, 1))
        small = plus(small_one, swapped(small_two), after)
        after = mixed_sum.second(after, COSTS[2])
        after = expand_sum.third(after, COSTS[3])
        after = mixed_sum.third(after, COSTS[4])
        kept = finished(sent, backward_chunk, ig_keep, ig_send)
        input_gradient = spread_rows(*kept, after)
        small = plus(small, crossed(small, 1), input_gradient)
        (reduce_grad,) = reduce_sum.result((reduce_weight.shape[1:],), input_gradient)
        small = plus(small, crossed(small, 2), reduce_grad)
        (expand_grad,) = expand_sum.result((expand_weight.shape[1:],), reduce_grad)
        project_grad, output_grad = mixed_sum.result(
            (project_weight.shape[1:], output_weight.shape[1:]), expand_grad
        )
        project_grad = project_grad[None]
    else:
        for now, grad_mid in held:
            *carried, sent, _ = attend_back(now, x_buf, sent, grad_mid, carried)
        sum_a, _, _, dq_buf, dkr_buf, dvr_buf, dmr_buf, ig_keep, ig_send = carried
        kept = finished(last_out, forward_chunk, hid_keep, hid_send)
        hidden = spread_rows(*kept, sent)
        kept = finished(sent, backward_chunk, ig_keep, ig_send)
        input_gradient = spread_rows(*kept, sent)
        reduce_grad, expand_grad, output_grad, *project_grad = (
            total.astype(F32)
            for total in lax.psum(
                (
                    weight_gradient(m_buf, df_buf, 0), weight_gradient(h2_buf, dur_buf, 1),
                    weight_gradient(post_buf, dmr_buf, 0), weight_gradient(h1_buf, dq_buf, 1),
                    weight_gradient(h1_buf, dkr_buf, 1), weight_gradient(h1_buf, dvr_buf, 1),
                ),
                "batch",
            )
        )
        project_grad = jnp.stack(project_grad)[None]

    if paired:
        if not by_links:
            small = lax.psum(packed(0, sum_a) + swapped(packed(1, sum_a)), "batch")
        small = small.reshape(-1)
        here, there = width // 2, units // 2
        shared = small[:6 * width].reshape(6, width)
        narrow = small[6 * width:6 * width + 5 * here].reshape(5, here)
        broad = small[6 * width + 5 * here:].reshape(3, there)
    else:
        shared, narrow, broad = gathered(sum_a)
        small = lax.psum(
            jnp.concatenate([shared.reshape(-1), narrow.reshape(-1), broad.reshape(-1)]),
            ("batch", "mp"),
        ) * copies
        shared = small[:6 * width].reshape(6, width)
        narrow = small[6 * width:11 * width].reshape(5, width)
        broad = small[11 * width:].reshape(3, units)
        narrow = lax.dynamic_slice_in_dim(narrow, part * (width // parts), width // parts, 1)
        broad = lax.dynamic_slice_in_dim(broad, part * (units // parts), units // parts, 1)

    return (
        hidden[None, None],
        input_gradient[None, None],
        shared[0:2][None],
        shared[2:4][None],
        project_grad,
        narrow[0:2][None],
        jnp.sum(narrow[2].reshape(-1, head), axis=1)[None],
        narrow[3][None],
        narrow[4][None],
        output_grad[None],
        expand_grad[None],
        broad[0][None],
        broad[1][None],
        broad[2][None],
        reduce_grad[None],
        shared[4:6][None],
    )


def solution(mesh):
    layered = P("section", None, None)
    split = P("section", "mp")
    rows = P("section", "mp", None)
    columns = P("section", None, "mp")
    projected = P("section", None, None, "mp")
    tokens = P("batch", None, "mp", None)
    states = P("section", "batch", None, "mp", None)
    return jax.shard_map(
        local,
        mesh=mesh,
        in_specs=(
            tokens, tokens, P("batch", None, None, None), layered, layered, projected, columns,
            split, split, split, rows, columns, split, split, split, rows, layered,
        ),
        out_specs=(
            states, states, layered, layered, projected, columns, split, split, split, rows,
            columns, split, split, split, rows, layered,
        ),
        check_vma=False,
    )
```

```python
from functools import partial

import jax
import jax.numpy as jnp
from jax import lax
from jax.experimental import pallas as pl
from jax.experimental.pallas import tpu as pltpu
from jax.sharding import PartitionSpec as P

EPSILON = 1e-05
CHUNK = 128
KEYS = 512
TILE = 512
STRIP = 256
PART = 512
HIDE = -1e30
COSTS = (100, 15, 10, 5, 5)
LIMITS = tuple(size * 2**20 for size in (14, 11, 10))
F32 = jnp.float32
BF16 = jnp.bfloat16
VMEM = pl.BlockSpec(memory_space=pltpu.VMEM)
SMEM = pl.BlockSpec(memory_space=pltpu.SMEM)
HBM = pl.BlockSpec(memory_space=pltpu.HBM)
ANY = pl.BlockSpec(memory_space=pl.ANY)

DMA = pltpu.SemaphoreType.DMA
SCR = {
    "af": lambda chunk, width, units, length: [
        pltpu.VMEM((chunk, width), BF16), pltpu.VMEM((chunk, width), BF16),
        pltpu.VMEM((chunk, width), BF16), pltpu.VMEM((chunk, width), F32),
        pltpu.VMEM((128, chunk), F32), pltpu.VMEM((chunk, width), BF16),
        pltpu.VMEM((chunk, length), F32), pltpu.VMEM((3, chunk, width), BF16), DMA((7,)),
    ],
    "ff": lambda chunk, width, units, length: [
        pltpu.VMEM((chunk, width), BF16), pltpu.VMEM((chunk, units), F32),
        pltpu.VMEM((chunk, units), BF16), pltpu.VMEM((chunk, units), BF16),
        pltpu.VMEM((chunk, units), BF16), pltpu.VMEM((chunk, 128), F32), DMA((7,)),
    ],
    "fb": lambda chunk, width, units, length: [
        pltpu.VMEM((chunk, units), BF16), pltpu.VMEM((chunk, units), BF16),
        pltpu.VMEM((chunk, 128), F32), pltpu.VMEM((chunk, width), F32),
        pltpu.VMEM((chunk, width), BF16), pltpu.VMEM((chunk, units), F32),
        pltpu.VMEM((chunk, units), BF16), pltpu.VMEM((chunk, width), F32),
        DMA((4,)), DMA((2,)),
    ],
    "ab": lambda chunk, width, units, length: [
        pltpu.VMEM((chunk, width), BF16), pltpu.VMEM((chunk, width), BF16),
        pltpu.VMEM((chunk, width), F32), pltpu.VMEM((128, chunk), F32),
        pltpu.VMEM((chunk, width), BF16), pltpu.VMEM((chunk, width), F32),
        pltpu.VMEM((length, chunk), F32), pltpu.VMEM((chunk, width), BF16),
        pltpu.VMEM((chunk, width), BF16), pltpu.VMEM((chunk, width), BF16),
        pltpu.VMEM((chunk, width), BF16), pltpu.VMEM((chunk, width), F32),
        DMA((4,)), DMA((6,)),
    ],
}


def lasts(microseconds):
    flops = int(microseconds * 1.1e9)
    return pl.CostEstimate(flops=flops, bytes_accessed=1024, transcendentals=0)


def dot_nn(left, right):
    return jnp.dot(left, right, preferred_element_type=F32)


def dot_nt(left, right):
    return lax.dot_general(left, right, (((1,), (1,)), ((), ())), preferred_element_type=F32)


def dot_tn(left, right):
    return lax.dot_general(left, right, (((0,), (0,)), ((), ())), preferred_element_type=F32)


def norm_parts(values):
    centre = values - jnp.mean(values, axis=-1, keepdims=True)
    inv_std = lax.rsqrt(jnp.mean(centre * centre, axis=-1, keepdims=True) + EPSILON)
    return centre * inv_std, inv_std


def norm_back(scaled, normed, inv_std):
    mean_one = jnp.mean(scaled, axis=-1, keepdims=True)
    mean_two = jnp.mean(scaled * normed, axis=-1, keepdims=True)
    return inv_std * (scaled - mean_one - normed * mean_two)


def column_sum(values):
    return jnp.sum(values, axis=0, keepdims=True)


def document_start(starts_ref, place):
    first = jnp.zeros_like(place)
    for k in range(starts_ref.shape[0]):
        start = starts_ref[k]
        first = jnp.maximum(first, jnp.where(place >= start, start, 0))
    return first


def half_masks():
    lane = lax.broadcasted_iota(jnp.int32, (1, 128), 1)
    return (lane < 64).astype(BF16), (lane >= 64).astype(BF16)


def stack_heads(pair):
    even, odd = half_masks()
    return jnp.concatenate([pair * even, pair * odd], axis=0)


def pick_heads(stacked):
    rows = stacked.shape[0] // 2
    lane = lax.broadcasted_iota(jnp.int32, (1, 128), 1)
    return jnp.where(lane < 64, stacked[:rows], stacked[rows:])


def copies_of(pairs, sems):
    return [pltpu.make_async_copy(a, b, sems.at[i]) for i, (a, b) in enumerate(pairs)]


def in_hbm(values):
    return [pltpu.with_memory_space_constraint(value, pltpu.HBM) for value in values]


def chunk_rows(place_ref, near_ref, far_ref, first, into, sem, step):
    rows, half = into.shape[0], far_ref.shape[0]
    side = first // half
    inner = first - side * half

    @pl.when(side == place_ref[2])
    def _():
        at = pl.ds(pl.multiple_of(place_ref[3] + inner, rows), rows)
        getattr(pltpu.make_async_copy(near_ref.at[at], into, sem), step)()

    @pl.when(side != place_ref[2])
    def _():
        at = pl.ds(pl.multiple_of(inner, rows), rows)
        getattr(pltpu.make_async_copy(far_ref.at[at], into, sem), step)()


def first_rows(place, near, far, first, rows, after):
    def kernel(place_ref, near_ref, far_ref, after_ref, out_ref, sem):
        del after_ref
        for step in ("start", "wait"):
            chunk_rows(place_ref, near_ref, far_ref, jnp.int32(first), out_ref, sem, step)

    return pl.pallas_call(
        kernel,
        in_specs=[SMEM, HBM, HBM, ANY],
        out_specs=VMEM,
        out_shape=jax.ShapeDtypeStruct((rows, near.shape[1]), near.dtype),
        scratch_shapes=[pltpu.SemaphoreType.DMA],
        compiler_params=pltpu.CompilerParams(vmem_limit_bytes=2**20),
    )(place, *in_hbm([near, far]), after)


def last_rows(place, rows, chunk_of, count, keep, send):
    size = rows.shape[0]

    def kernel(place_ref, rows_ref, keep_in, send_in, keep_buf, send_buf, sem):
        del keep_in, send_in
        chunk = chunk_of(place_ref[0], place_ref[1] - 1)

        @pl.when((chunk >= 0) & (chunk < count))
        def _():
            for step in ("start", "wait"):
                store_rows(place_ref, keep_buf, send_buf, chunk * size, rows_ref, sem, step)

    return pl.pallas_call(
        kernel,
        in_specs=[SMEM, VMEM, HBM, HBM],
        out_specs=[HBM, HBM],
        out_shape=[pltpu.HBM(keep.shape, keep.dtype), pltpu.HBM(send.shape, send.dtype)],
        scratch_shapes=[pltpu.SemaphoreType.DMA],
        input_output_aliases={2: 0, 3: 1},
        compiler_params=pltpu.CompilerParams(vmem_limit_bytes=2**20),
        cost_estimate=lasts(1),
    )(place, rows, keep, send)


def row_of(vec_ref, first, size):
    return jnp.concatenate(
        [vec_ref[0, :, first:first + size], vec_ref[1, :, first:first + size]], axis=1
    )


def aligned(index, size):
    return pl.ds(pl.multiple_of(index * size, size), size)


def attend_kernel(
    tick_ref, section_ref, starts_ref, tok_ref, inc_ref, prev_ref, wp_ref, wo_ref,
    vec_ref, gain_ref, bias_ref, branch_ref,
    k_in, v_in, x_in, h1_in, q_in, o_in, lse_in, post_in, keep_in, send_in,
    k_ref, v_ref, x_buf, h1_buf, q_buf, o_buf, lse_buf, post_buf, keep_buf, send_buf, mid_ref,
    x_s, h1_s, q_s, o_s, lse_s, post_s, hide_s, qkv_s, sems, finish=True,
):
    del k_in, v_in, x_in, h1_in, q_in, o_in, lse_in, post_in, keep_in, send_in
    rows = mid_ref.shape[0]
    length, width = k_ref.shape
    half = width // 2
    section = section_ref[0]
    chunk = tick_ref[0] - 2 * section
    live = (chunk >= 0) & (chunk < length // rows)
    state = (section_ref, keep_buf, send_buf, (chunk - 1) * rows, prev_ref, sems.at[6])

    @pl.when((chunk >= 1) & (chunk <= length // rows))
    def _():
        store_rows(*state, "start")

    def saves():
        here = pl.ds(pl.multiple_of(chunk * rows, rows), rows)
        return copies_of(
            (
                (x_s, x_buf.at[here]), (h1_s, h1_buf.at[here]), (q_s, q_buf.at[here]),
                (o_s, o_buf.at[here]), (lse_s, lse_buf.at[chunk]), (post_s, post_buf.at[here]),
            ),
            sems,
        )

    @pl.when(live)
    def _():
        first = pl.multiple_of(chunk * rows, rows)
        here = pl.ds(first, rows)

        @pl.when(section == 0)
        def _():
            x_s[...] = tok_ref[...]

        @pl.when(section != 0)
        def _():
            x_s[...] = inc_ref[...]

        stores = saves()
        layer_in = x_s[...].astype(F32)
        stores[0].start()
        normed, _ = norm_parts(layer_in)
        h1 = (normed * gain_ref[0:1].astype(F32) + bias_ref[0:1].astype(F32)).astype(BF16)
        h1_s[...] = h1
        stores[1].start()

        def project(number, carry):
            side, which = number // 3, number % 3
            shift = vec_ref[side, :, aligned(which, half)]
            value = dot_nn(h1_s[...], wp_ref[side, which]) + shift
            qkv_s[which, :, aligned(side, half)] = value.astype(BF16)
            return carry

        lax.fori_loop(0, 6, project, 0, unroll=6)
        q_s[...] = qkv_s[0] * jnp.asarray(0.125, BF16)
        k_ref[here, :] = qkv_s[1]
        v_ref[here, :] = qkv_s[2]
        stores[2].start()

        def attend(keys):
            place = first + lax.broadcasted_iota(jnp.int32, (rows, 1), 0)
            start = document_start(starts_ref, place)
            key_at = lax.broadcasted_iota(jnp.int32, (rows, keys), 1)
            hide_s[:, :keys] = jnp.where((key_at <= place) & (key_at >= start), 0.0, HIDE)
            lane = lax.broadcasted_iota(jnp.int32, (rows, 128), 1)

            def one_pair(pair, lse):
                at = pl.ds(pl.multiple_of(pair * 128, 128), 128)
                queries = stack_heads(q_s[:, at])
                hide = hide_s[:, :keys]
                scores = dot_nt(queries, k_ref[0:keys, at]) + jnp.concatenate([hide, hide], axis=0)
                top = jnp.max(scores, axis=-1, keepdims=True)
                raised = jnp.exp(scores - top)
                total = jnp.sum(raised, axis=-1, keepdims=True)
                out = dot_nn(raised.astype(BF16), v_ref[0:keys, at]) / total
                o_s[:, at] = pick_heads(out)
                now = top + jnp.log(total)
                lse = jnp.where(lane == 2 * pair, now[:rows], lse)
                return jnp.where(lane == 2 * pair + 1, now[rows:], lse)

            nothing = jnp.zeros((rows, 128), F32)
            lse = lax.fori_loop(0, width // 128, one_pair, nothing, unroll=2)
            lse_s[...] = lse.T

        for count in range(length // KEYS):

            @pl.when(first // KEYS == count)
            def _():
                attend((count + 1) * KEYS)

        stores[3].start()
        stores[4].start()
        post_normed, _ = norm_parts(o_s[...] * row_of(vec_ref, 3 * half, half))
        post = post_normed * row_of(vec_ref, 4 * half, half) + row_of(vec_ref, 5 * half, half)
        post_s[...] = post.astype(BF16)
        stores[5].start()

        def mix(number, carry):
            at = aligned(number, STRIP)
            total = dot_nn(post_s[:, :half], wo_ref[0, :, at])
            total += dot_nn(post_s[:, half:], wo_ref[1, :, at])
            mid_ref[:, at] = x_s[:, at].astype(F32) + total + branch_ref[0:1, at].astype(F32)
            return carry

        lax.fori_loop(0, width // STRIP, mix, 0, unroll=4)

    def done():
        @pl.when(live)
        def _():
            for copy in saves():
                copy.wait()

        @pl.when((chunk >= 1) & (chunk <= length // rows))
        def _():
            store_rows(*state, "wait")

    if finish:
        done()
    return done


def gelu_parts(pre):
    phi = 0.5 + 0.5 * lax.erf(pre * 0.7071067811865476)
    density = jnp.exp(pre * pre * -0.5) * 0.3989422804014327
    return pre * phi, phi + pre * density


def expand_kernel(
    tick_ref, section_ref, near_ref, far_ref, near_back, far_back, mid_ref, we_ref, wr_ref,
    vec_ref, gain_ref, bias_ref, branch_ref,
    h2_in, g_in, gp_in, m_in, st_in, mid_in,
    h2_buf, g_buf, gp_buf, m_buf, st_buf, mid_buf, out_ref, next_ref,
    h2_s, gf_s, g_s, gp_s, m_s, st_s, sems,
):
    del h2_in, g_in, gp_in, m_in, st_in, mid_in
    rows = mid_ref.shape[0]
    width = mid_ref.shape[1]
    half = we_ref.shape[2]
    units = 2 * half
    tiles = half // TILE
    length = h2_buf.shape[0]
    chunk = tick_ref[0] - 2 * section_ref[0]

    @pl.when((chunk >= 0) & (chunk < length // rows))
    def _():
        here = pl.ds(pl.multiple_of(chunk * rows, rows), rows)
        sent = []

        def send(source, target):
            copy = pltpu.make_async_copy(source, target, sems.at[len(sent)])
            copy.start()
            sent.append(copy)

        send(mid_ref, mid_buf.at[here])
        more = (section_ref[0] == 0) & (chunk + 1 < length // rows)
        fetch = (section_ref, near_ref, far_ref, (chunk + 1) * rows, next_ref, sems.at[6])

        turn = (section_ref[0] == section_ref[1] - 1) & (chunk == length // rows - 1)
        back = (section_ref, near_back, far_back, chunk * rows, next_ref, sems.at[6])

        @pl.when(more)
        def _():
            chunk_rows(*fetch, "start")

        @pl.when(turn)
        def _():
            chunk_rows(*back, "start")

        def wide(tile, which):
            first = 3 * width + which * half + tile % tiles * TILE
            return vec_ref[tile // tiles, :, pl.ds(pl.multiple_of(first, TILE), TILE)]

        normed, _ = norm_parts(mid_ref[...])
        h2 = (normed * gain_ref[1:2].astype(F32) + bias_ref[1:2].astype(F32)).astype(BF16)
        h2_s[...] = h2
        send(h2_s, h2_buf.at[here])
        def expand(tile, total):
            at = aligned(tile, TILE)
            weight = we_ref[tile // tiles, :, aligned(tile % tiles, TILE)]
            active, slope = gelu_parts(dot_nn(h2_s[...], weight) + wide(tile, 0))
            gf_s[:, at] = active
            g_s[:, at] = active.astype(BF16)
            gp_s[:, at] = slope.astype(BF16)
            return total + jnp.sum(active, axis=-1, keepdims=True)

        nothing = jnp.zeros((rows, 1), F32)
        mean = lax.fori_loop(0, 2 * tiles, expand, nothing, unroll=4) / units
        send(g_s, g_buf.at[here])
        send(gp_s, gp_buf.at[here])

        def spread(tile, total):
            centre = gf_s[:, aligned(tile, TILE)] - mean
            return total + jnp.sum(centre * centre, axis=-1, keepdims=True)

        inv_std = lax.rsqrt(lax.fori_loop(0, 2 * tiles, spread, nothing, unroll=8) / units + EPSILON)
        lane = lax.broadcasted_iota(jnp.int32, (rows, 128), 1)
        st_s[...] = jnp.where(lane == 0, mean, inv_std)
        send(st_s, st_buf.at[here])

        def normalise(tile, carry):
            at = aligned(tile, TILE)
            active = (gf_s[:, at] - mean) * inv_std * wide(tile, 1) + wide(tile, 2)
            m_s[:, at] = active.astype(BF16)
            return carry

        lax.fori_loop(0, 2 * tiles, normalise, 0, unroll=4)
        send(m_s, m_buf.at[here])

        def reduce(number, carry):
            at = aligned(number, STRIP)
            total = dot_nn(m_s[:, :half], wr_ref[0, :, at])
            total += dot_nn(m_s[:, half:], wr_ref[1, :, at])
            total += mid_ref[:, at] + branch_ref[1:2, at].astype(F32)
            out_ref[:, at] = total.astype(BF16)
            return carry

        lax.fori_loop(0, width // STRIP, reduce, 0, unroll=2)
        for copy in sent:
            copy.wait()

        @pl.when(more)
        def _():
            chunk_rows(*fetch, "wait")

        @pl.when(turn)
        def _():
            chunk_rows(*back, "wait")


def expand_back_kernel(
    tick_ref, section_ref, cot_ref, inc_ref, wr_ref, we_ref, vec_ref, gain_ref,
    g_buf, gp_buf, st_buf, mid_buf,
    sum_in, wsum_in, df_in, dur_in,
    sum_ref, wsum_ref, df_buf, dur_buf, dmid_ref,
    g_s, gp_s, st_s, mid_s, df_s, z_s, dur_s, dh_s, in_sems, out_sems,
):
    del sum_in, wsum_in, df_in, dur_in
    rows = dmid_ref.shape[0]
    width = dmid_ref.shape[1]
    half = wr_ref.shape[2]
    units = 2 * half
    tiles = half // TILE
    length = g_buf.shape[0]
    count = length // rows
    section = section_ref[0]
    last = section_ref[1] - 1
    chunk = count - 1 - (tick_ref[0] - 2 * (last - section))

    @pl.when((chunk >= 0) & (chunk < count))
    def _():
        here = pl.ds(pl.multiple_of(chunk * rows, rows), rows)
        loads = copies_of(
            (
                (g_buf.at[here], g_s), (st_buf.at[here], st_s), (gp_buf.at[here], gp_s),
                (mid_buf.at[here], mid_s),
            ),
            in_sems,
        )
        loads[0].start()
        loads[1].start()

        @pl.when(section == last)
        def _():
            df_s[...] = cot_ref[...]

        @pl.when(section != last)
        def _():
            df_s[...] = inc_ref[...]

        sent = []

        def send(source, target):
            copy = pltpu.make_async_copy(source, target, out_sems.at[len(sent)])
            copy.start()
            sent.append(copy)

        def gain_of(tile):
            first = 3 * width + half + tile % tiles * TILE
            return vec_ref[tile // tiles, :, pl.ds(pl.multiple_of(first, TILE), TILE)]

        grad_low = df_s[...]
        send(df_s, df_buf.at[here])
        sum_ref[0:1] += column_sum(grad_low.astype(F32))
        loads[0].wait()
        loads[1].wait()
        loads[2].start()
        loads[3].start()
        mean = st_s[:, 0:1]
        inv_std = st_s[:, 1:2]
        def reduce_back(tile, sums):
            at = aligned(tile, TILE)
            weight = wr_ref[tile // tiles, :, aligned(tile % tiles, TILE)]
            grad = dot_nn(df_s[...], weight)
            normed = (g_s[:, at].astype(F32) - mean) * inv_std
            wsum_ref[0:1, at] += column_sum(grad * normed)
            wsum_ref[1:2, at] += column_sum(grad)
            scaled = grad * gain_of(tile)
            z_s[:, at] = scaled
            return (
                sums[0] + jnp.sum(scaled, axis=-1, keepdims=True),
                sums[1] + jnp.sum(scaled * normed, axis=-1, keepdims=True),
            )

        nothing = jnp.zeros((rows, 1), F32)
        one, two = lax.fori_loop(0, 2 * tiles, reduce_back, (nothing, nothing), unroll=4)
        one = one / units
        two = two / units

        def active_back(tile, carry):
            at = aligned(tile, TILE)
            normed = (g_s[:, at].astype(F32) - mean) * inv_std
            grad = inv_std * (z_s[:, at] - one - normed * two) * gp_s[:, at].astype(F32)
            wsum_ref[2:3, at] += column_sum(grad)
            dur_s[:, at] = grad.astype(BF16)
            return carry

        loads[2].wait()
        lax.fori_loop(0, 2 * tiles, active_back, 0, unroll=2)
        send(dur_s, dur_buf.at[here])

        def expand_back(number, carry):
            at = aligned(number, STRIP)
            total = dot_nn(dur_s[:, :half], we_ref[0, :, at])
            dh_s[:, at] = total + dot_nn(dur_s[:, half:], we_ref[1, :, at])
            return carry

        lax.fori_loop(0, width // STRIP, expand_back, 0, unroll=4)
        grad_second = dh_s[...]
        loads[3].wait()
        normed, inv_std = norm_parts(mid_s[...])
        sum_ref[1:2] += column_sum(grad_second * normed)
        sum_ref[2:3] += column_sum(grad_second)
        grad_mid = grad_low.astype(F32) + norm_back(
            grad_second * gain_ref[1:2].astype(F32), normed, inv_std
        )
        sum_ref[3:4] += column_sum(grad_mid)
        dmid_ref[...] = grad_mid
        for copy in sent:
            copy.wait()


def attend_back_kernel(
    tick_ref, section_ref, starts_ref, after, near_ref, far_ref, prev_ref, dmid_ref, wo_ref,
    wp_ref, vec_ref, gain_ref, k_ref, v_ref,
    x_buf, q_buf, o_buf, lse_buf,
    sum_in, dk_in, dv_in, dq_in, dkr_in, dvr_in, dmr_in, keep_in, send_in,
    sum_ref, dk_ref, dv_ref, dq_buf, dkr_buf, dvr_buf, dmr_buf, keep_buf, send_buf, out_ref,
    next_ref,
    x_s, q_s, o_s, lse_s, do_s, dqf_s, hide_s, dq_s, dkr_s, dvr_s, low_s, wide_s, in_sems,
    out_sems,
):
    del after, sum_in, dk_in, dv_in, dq_in, dkr_in, dvr_in, dmr_in, keep_in, send_in
    rows = dmid_ref.shape[0]
    length, width = k_ref.shape
    half = width // 2
    count = length // rows
    section = section_ref[0]
    last = section_ref[1] - 1
    chunk = count - 1 - (tick_ref[0] - 2 * (last - section))

    def fetches():
        here = pl.ds(pl.multiple_of(chunk * rows, rows), rows)
        return copies_of(
            (
                (o_buf.at[here], o_s), (q_buf.at[here], q_s), (lse_buf.at[chunk], lse_s),
                (x_buf.at[here], x_s),
            ),
            in_sems,
        )

    @pl.when((chunk >= 0) & (chunk < count))
    def _():
        for copy in fetches():
            copy.start()

    state = (section_ref, keep_buf, send_buf, (chunk + 1) * rows, prev_ref, out_sems.at[4])

    @pl.when((chunk >= -1) & (chunk < count - 1))
    def _():
        store_rows(*state, "start")

    @pl.when((chunk >= 0) & (chunk < count))
    def _():
        first = pl.multiple_of(chunk * rows, rows)
        here = pl.ds(first, rows)
        loads = fetches()

        @pl.when(chunk == count - 1)
        def _():
            dk_ref[...] = jnp.zeros_like(dk_ref)
            dv_ref[...] = jnp.zeros_like(dv_ref)

        more = (section == last) & (chunk >= 1)
        fetch = (section_ref, near_ref, far_ref, (chunk - 1) * rows, next_ref, out_sems.at[5])

        @pl.when(more)
        def _():
            chunk_rows(*fetch, "start")

        sent = []

        def send(source, target):
            copy = pltpu.make_async_copy(source, target, out_sems.at[len(sent)])
            copy.start()
            sent.append(copy)

        low_s[...] = dmid_ref[...].astype(BF16)
        send(low_s, dmr_buf.at[here])

        def mix_back(side, carry):
            wide_s[:, aligned(side, half)] = dot_nn(low_s[...], wo_ref[side])
            return carry

        lax.fori_loop(0, 2, mix_back, 0, unroll=2)
        grad_post = wide_s[...]
        loads[0].wait()
        attended = o_s[...]
        scale = row_of(vec_ref, 3 * half, half)
        normed, inv_std = norm_parts(attended * scale)
        sum_ref[0:1] += column_sum(grad_post * normed)
        sum_ref[1:2] += column_sum(grad_post)
        grad_mixed = norm_back(grad_post * row_of(vec_ref, 4 * half, half), normed, inv_std)
        sum_ref[2:3] += column_sum(grad_mixed * attended)
        do_s[...] = (grad_mixed * scale).astype(BF16)

        loads[1].wait()
        loads[2].wait()

        def attend(keys):
            place = first + lax.broadcasted_iota(jnp.int32, (1, rows), 1)
            start = document_start(starts_ref, place)
            key_at = lax.broadcasted_iota(jnp.int32, (keys, rows), 0)
            hide_s[:keys, :] = jnp.where((key_at <= place) & (key_at >= start), 0.0, HIDE)

            def one_pair(pair, carry):
                at = pl.ds(pl.multiple_of(pair * 128, 128), 128)
                queries = stack_heads(q_s[:, at])
                grad_pair = do_s[:, at]
                grads = stack_heads(grad_pair)
                product = (grad_pair.astype(F32) * o_s[:, at]).T
                delta = jnp.concatenate(
                    [column_sum(product[:64]), column_sum(product[64:])], axis=1
                )
                lse = jnp.concatenate(
                    [lse_s[pl.ds(2 * pair, 1), :], lse_s[pl.ds(2 * pair + 1, 1), :]], axis=1
                )
                hide = hide_s[:keys, :]
                key_pair = k_ref[0:keys, at]
                scores = dot_nt(key_pair, queries) + jnp.concatenate([hide, hide], axis=1)
                probs = jnp.exp(scores - lse)
                grad_probs = dot_nt(v_ref[0:keys, at], grads)
                grad_scores = (probs * (grad_probs - delta)).astype(BF16)
                dk_ref[0:keys, at] += dot_nn(grad_scores, queries)
                dv_ref[0:keys, at] += dot_nn(probs.astype(BF16), grads)
                dqf_s[:, at] = pick_heads(dot_tn(grad_scores, key_pair)) * 0.125
                return carry

            lax.fori_loop(0, width // 128, one_pair, 0, unroll=2)

        for number in range(length // KEYS):

            @pl.when(first // KEYS == number)
            def _():
                attend((number + 1) * KEYS)

        grad_query = dqf_s[...]
        grad_value = dv_ref[here, :]
        sum_ref[3:4] += column_sum(grad_query)
        sum_ref[4:5] += column_sum(grad_value)
        dq_s[...] = grad_query.astype(BF16)
        dkr_s[...] = dk_ref[here, :].astype(BF16)
        dvr_s[...] = grad_value.astype(BF16)
        send(dq_s, dq_buf.at[here])
        send(dkr_s, dkr_buf.at[here])
        send(dvr_s, dvr_buf.at[here])

        def project_back(number, carry):
            at = aligned(number, STRIP)
            total = jnp.zeros((rows, STRIP), F32)
            for which, part in enumerate((dq_s, dkr_s, dvr_s)):
                total += dot_nn(part[:, :half], wp_ref[0, which, :, at])
                total += dot_nn(part[:, half:], wp_ref[1, which, :, at])
            wide_s[:, at] = total
            return carry

        lax.fori_loop(0, width // STRIP, project_back, 0, unroll=4)
        grad_first = wide_s[...]
        loads[3].wait()
        normed, inv_std = norm_parts(x_s[...].astype(F32))
        sum_ref[5:6] += column_sum(grad_first * normed)
        sum_ref[6:7] += column_sum(grad_first)
        out = dmid_ref[...] + norm_back(
            grad_first * gain_ref[0:1].astype(F32), normed, inv_std
        )
        out_ref[...] = out.astype(BF16)
        for copy in sent:
            copy.wait()

        @pl.when(more)
        def _():
            chunk_rows(*fetch, "wait")

    @pl.when((chunk >= -1) & (chunk < count - 1))
    def _():
        store_rows(*state, "wait")


def forward_kernel(
    tick_ref, section_ref, starts_ref, near_ref, far_ref, near_back, far_back, tok_ref, inc_ref,
    prev_ref, wp_ref, wo_ref, we_ref, wr_ref, vec_ref, gain_ref, bias_ref, branch_ref, *refs,
):
    ins, outs, (out_ref, next_ref, mid_s), scratch = refs[:16], refs[16:32], refs[32:35], refs[35:]
    shared = vec_ref, gain_ref, bias_ref, branch_ref
    done = attend_kernel(
        tick_ref, section_ref, starts_ref, tok_ref, inc_ref, prev_ref, wp_ref, wo_ref, *shared,
        *ins[:10], *outs[:10], mid_s, *scratch[:9], finish=False,
    )
    expand_kernel(
        tick_ref, section_ref, near_ref, far_ref, near_back, far_back, mid_s, we_ref, wr_ref,
        *shared,
        *ins[10:], *outs[10:], out_ref, next_ref, *scratch[9:],
    )
    done()


def flip_kernel(source, after, target):
    del after
    size = 256

    def flip(one, two):
        def body(step, carry):
            at = aligned(step, size)
            two[:, at] = one[at, :].T
            return carry

        lax.fori_loop(0, one.shape[0] // size, body, 0)

    def each(index, carry):
        if len(source.shape) == 3:
            flip(source.at[index], target.at[index])
        else:
            deep = source.shape[1]
            flip(source.at[index // deep, index % deep], target.at[index // deep, index % deep])
        return carry

    count = source.shape[0] * (source.shape[1] if len(source.shape) == 4 else 1)
    lax.fori_loop(0, count, each, 0)


def flipped(weight, after):
    shape = weight.shape[:-2] + (weight.shape[-1], weight.shape[-2])
    return pl.pallas_call(
        flip_kernel,
        in_specs=[VMEM, ANY],
        out_specs=VMEM,
        out_shape=pltpu.VMEM(shape, BF16),
        compiler_params=pltpu.CompilerParams(vmem_limit_bytes=2 * 2**20),
    )(weight, after)


def load_kernel(side, source, after, *refs):
    del after
    copy = pltpu.make_async_copy(source, refs[-2].at[side], refs[-1])
    copy.start()
    copy.wait()


def loaded(side, value, both, after):
    known = [] if both is None else [both]
    return pl.pallas_call(
        partial(load_kernel, side),
        in_specs=[HBM, ANY] + [VMEM] * len(known),
        out_specs=VMEM,
        out_shape=pltpu.VMEM((2, *value.shape), value.dtype),
        scratch_shapes=[pltpu.SemaphoreType.DMA],
        input_output_aliases={2: 0} if known else {},
        compiler_params=pltpu.CompilerParams(vmem_limit_bytes=2**20),
    )(*in_hbm([value]), after, *known)


def empty_kernel(*refs):
    del refs


def empty(shapes, space, *after):
    return pl.pallas_call(
        empty_kernel,
        in_specs=[ANY] * len(after),
        out_specs=[pl.BlockSpec(memory_space=space)] * len(shapes),
        out_shape=[space(shape, dtype) for shape, dtype in shapes],
        compiler_params=pltpu.CompilerParams(vmem_limit_bytes=2**20),
    )(*after)


def call(kernel, inputs, specs, carried, carried_specs, fresh, fresh_specs, scratch, limit, flops):
    first = len(inputs)
    inputs = [
        pltpu.with_memory_space_constraint(a, pltpu.HBM) if spec is HBM else a
        for a, spec in zip(inputs, specs)
    ]
    shapes = [
        pltpu.HBM(a.shape, a.dtype) if spec is HBM else jax.ShapeDtypeStruct(a.shape, a.dtype)
        for a, spec in zip(carried, carried_specs)
    ] + fresh
    return pl.pallas_call(
        kernel,
        in_specs=specs + carried_specs,
        out_specs=carried_specs + fresh_specs,
        out_shape=shapes,
        scratch_shapes=scratch,
        input_output_aliases={first + i: i for i in range(len(carried))},
        compiler_params=pltpu.CompilerParams(vmem_limit_bytes=limit),
        cost_estimate=pl.CostEstimate(flops=flops, bytes_accessed=2**22, transcendentals=0),
    )(*inputs, *carried)


def settle_kernel(place_ref, *refs):
    pieces, (*outs, wide_s, turn_s, sems) = refs[:8], refs[8:]
    rows = pieces[0].shape[0]
    low, high = place_ref[4], place_ref[5]
    copies = []
    for number, piece in enumerate(pieces):
        half, flips = number // 4, number % 4
        first = (low, high)[half] ^ (flips // 2)
        second = (high, low)[half] ^ (flips % 2)
        slot = number % 2
        if number >= 2:
            for copy in copies[number - 2]:
                copy.wait()
        wide_s[slot] = piece[...].astype(F32)
        at = pl.ds(pl.multiple_of((half * 4 + first * 2 + second) * rows, rows), rows)
        moves = []
        if len(outs) == 1:
            moves.append((wide_s.at[slot], outs[0].at[at]))
        else:
            layers, _, columns = outs[0].shape
            for layer in range(layers):
                source = wide_s.at[slot, :, layer * columns:(layer + 1) * columns]
                moves.append((source, outs[0].at[layer, at]))
            turn_s[slot] = wide_s[slot, :, layers * columns:].T
            moves.append((turn_s.at[slot], outs[1].at[:, at]))
        started = [
            pltpu.make_async_copy(source, target, sems.at[slot, i])
            for i, (source, target) in enumerate(moves)
        ]
        for copy in started:
            copy.start()
        copies.append(started)
    for copy in copies[6] + copies[7]:
        copy.wait()


def settle(place, pieces, shapes, after, cost):
    rows, columns = pieces[0].shape
    turn = (2, shapes[1][0], rows) if len(shapes) > 1 else (2, 8, 128)

    def kernel(place_ref, *refs):
        settle_kernel(place_ref, *refs[:8], *refs[9:])

    return pl.pallas_call(
        kernel,
        grid=(1,),
        in_specs=[SMEM]
        + [pl.BlockSpec((rows, columns), lambda i: (0, 0), pipeline_mode=pl.Buffered(1))] * 8
        + [HBM],
        out_specs=[HBM] * len(shapes),
        out_shape=[pltpu.HBM(shape, F32) for shape in shapes],
        scratch_shapes=[
            pltpu.VMEM((2, rows, columns), F32), pltpu.VMEM(turn, F32),
            pltpu.SemaphoreType.DMA((2, 4)),
        ],
        compiler_params=pltpu.CompilerParams(vmem_limit_bytes=12 * 2**20),
        cost_estimate=lasts(cost),
    )(place, *pieces, *in_hbm([after]))


def crossed(value, bit):
    route = [(i, i ^ bit) for i in range(lax.axis_size("batch"))]
    return lax.ppermute(value, "batch", route)


def products(lefts, rights, pairs, columns, tile, store):
    part = min(tile, PART)

    def body(index, carry):
        at = aligned(index, part)
        for number, right in enumerate(rights):
            where = slice(number * columns, (number + 1) * columns)
            store(at, where, dot_tn(lefts[pairs[number]][:, at], right[...]))
        return carry

    if tile == part:
        body(0, 0)
    else:
        lax.fori_loop(0, tile // part, body, 0)


def other_part(lefts, rights, pairs, axis, after, cost=1):
    length = lefts[0].shape[0]
    rows = lefts[0].shape[1] // (2 if axis == 0 else 1)
    columns = rights[0].shape[1] // (1 if axis == 0 else 2)
    tile = rows // 4
    skip = 4 if axis == 0 else 0
    side = 0 if axis == 0 else 1

    def kernel(*refs):
        def store(at, where, value):
            refs[-1][at, where] = value.astype(BF16)

        inputs = refs[:len(lefts)], refs[len(lefts):len(lefts) + len(rights)]
        products(*inputs, pairs, columns, tile, store)

    return pl.pallas_call(
        kernel,
        grid=(rows // tile,),
        in_specs=[pl.BlockSpec((length, tile), lambda i: (0, skip + i))] * len(lefts)
        + [pl.BlockSpec((length, columns), lambda i: (0, side), pipeline_mode=pl.Buffered(1))]
        * len(rights)
        + [HBM],
        out_specs=pl.BlockSpec((tile, columns * len(rights)), lambda i: (i, 0)),
        out_shape=pltpu.HBM((rows, columns * len(rights)), BF16),
        compiler_params=pltpu.CompilerParams(vmem_limit_bytes=12 * 2**20),
        cost_estimate=lasts(cost),
    )(*in_hbm(lefts), *in_hbm(rights), *in_hbm([after]))


def own_part(lefts, rights, pairs, come, place, after, cost=1):
    length = lefts[0].shape[0]
    rows, whole = come.shape
    columns = whole // len(rights)
    tile = rows // 4

    def at(i, place):
        low, high = place[4], place[5]
        first = jnp.where(i == 0, 1 - low, 3 - high)
        return jnp.where(i < 2, first, jnp.where(i == 2, low, 2 + high))

    def kernel(place_ref, *refs):
        del place_ref
        come_ref = refs[len(lefts) + len(rights)]
        *outs, low_s, sems = refs[-6:]
        step = pl.program_id(0)
        slot = step % 2

        def store(number):
            return pltpu.make_async_copy(
                low_s.at[number % 2], outs[number], sems.at[number % 2]
            )

        for number in (2, 3):

            @pl.when(step == number)
            def _():
                store(number - 2).wait()

        def keep(at, where, value):
            low_s[slot, at, where] = (value + come_ref[at, where].astype(F32)).astype(BF16)

        inputs = refs[:len(lefts)], refs[len(lefts):len(lefts) + len(rights)]
        products(*inputs, pairs, columns, tile, keep)
        for number in range(4):

            @pl.when(step == number)
            def _():
                store(number).start()

        @pl.when(step == 3)
        def _():
            store(2).wait()
            store(3).wait()

    return pl.pallas_call(
        kernel,
        grid_spec=pltpu.PrefetchScalarGridSpec(
            num_scalar_prefetch=1,
            grid=(4,),
            in_specs=[pl.BlockSpec((length, tile), lambda i, place: (0, at(i, place)))]
            * len(lefts)
            + [
                pl.BlockSpec(
                    (length, columns), lambda i, place: (0, 0), pipeline_mode=pl.Buffered(1)
                )
            ]
            * len(rights)
            + [pl.BlockSpec((tile, whole), lambda i, place: (at(i, place), 0)), HBM],
            out_specs=[HBM] * 4,
            scratch_shapes=[
                pltpu.VMEM((2, tile, whole), BF16), pltpu.SemaphoreType.DMA((2,))
            ],
        ),
        out_shape=[pltpu.HBM((tile, whole), BF16)] * 4,
        compiler_params=pltpu.CompilerParams(vmem_limit_bytes=12 * 2**20),
        cost_estimate=lasts(cost),
    )(place, *in_hbm(lefts), *in_hbm(rights), come, *in_hbm([after]))


def add_kernel(split, place_ref, *refs):
    keeps, comes = (refs[0], refs[2]), (refs[1], refs[3])
    outs = refs[5:]
    for half, bit in ((0, 5), (1, 4)):
        keep, come = keeps[half], comes[half]
        if split:
            rows = keep.shape[0] // 2
            side = place_ref[bit]
            for number, where in ((0, 1 - side), (1, side)):
                at = pl.ds(pl.multiple_of(where * rows, rows), rows)
                outs[2 * half + number][...] = (
                    keep[at, :].astype(F32) + come[at, :].astype(F32)
                ).astype(BF16)
        else:
            outs[half][...] = (keep[...].astype(F32) + come[...].astype(F32)).astype(BF16)


def added(keeps, comes, place, split, after, cost):
    rows, columns = keeps[0].shape
    kept = rows // 2 if split else rows
    count = 4 if split else 2
    return pl.pallas_call(
        partial(add_kernel, split),
        grid=(1,),
        in_specs=[SMEM]
        + [pl.BlockSpec((rows, columns), lambda i: (0, 0), pipeline_mode=pl.Buffered(1))] * 4
        + [HBM],
        out_specs=[
            pl.BlockSpec((kept, columns), lambda i: (0, 0), pipeline_mode=pl.Buffered(1))
        ]
        * count,
        out_shape=[pltpu.HBM((kept, columns), BF16)] * count,
        compiler_params=pltpu.CompilerParams(vmem_limit_bytes=12 * 2**20),
        cost_estimate=lasts(cost),
    )(place, keeps[0], comes[0], keeps[1], comes[1], *in_hbm([after]))


class BatchSum:
    def __init__(self, pieces, place):
        send_a, send_b, keep_a, keep_b = pieces
        self.place = place
        self.keeps = keep_a, keep_b
        self.comes = crossed(send_a, 1), crossed(send_b, 2)

    def second(self, after, cost):
        send_a, keep_a, send_b, keep_b = added(self.keeps, self.comes, self.place, True, after, cost)
        self.keeps = keep_a, keep_b
        self.comes = crossed(send_a, 2), crossed(send_b, 1)
        return keep_a

    def third(self, after, cost):
        a, b = added(self.keeps, self.comes, self.place, False, after, cost)
        across_a, across_b = crossed(a, 2), crossed(b, 1)
        self.pieces = [
            a, across_a, crossed(a, 1), crossed(across_a, 1),
            b, across_b, crossed(b, 2), crossed(across_b, 2),
        ]
        return a

    def result(self, shapes, after, cost=1):
        return settle(self.place, self.pieces, shapes, after, cost)


def keep_kernel(place_ref, come_ref, in_ref, out_ref, sem):
    del in_ref
    copy = pltpu.make_async_copy(come_ref, out_ref.at[1 - place_ref[2]], sem)
    copy.start()
    copy.wait()


def with_other_half(kept, come, place, after):
    def kernel(place_ref, come_ref, after_ref, *refs):
        keep_kernel(place_ref, come_ref, *refs)

    return pl.pallas_call(
        kernel,
        in_specs=[SMEM, VMEM, HBM, HBM],
        out_specs=HBM,
        out_shape=pltpu.HBM(kept.shape, kept.dtype),
        scratch_shapes=[pltpu.SemaphoreType.DMA],
        compiler_params=pltpu.CompilerParams(vmem_limit_bytes=4 * 2**20),
        input_output_aliases={3: 0},
        cost_estimate=lasts(3),
    )(place, come, *in_hbm([after]), kept)


def plus_kernel(one, two, after, out):
    del after
    out[...] = one[...] + two[...]


def plus(one, two, after):
    return pl.pallas_call(
        plus_kernel,
        in_specs=[VMEM, VMEM, HBM],
        out_specs=VMEM,
        out_shape=jax.ShapeDtypeStruct(one.shape, one.dtype),
        compiler_params=pltpu.CompilerParams(vmem_limit_bytes=2**20),
        cost_estimate=lasts(1),
    )(one, two, *in_hbm([after]))


def store_rows(place_ref, keep_buf, send_buf, first, source, sem, back):
    rows = source.shape[0]
    half = send_buf.shape[0]
    side = first // half
    at = pl.ds(pl.multiple_of(first - side * half, rows), rows)

    @pl.when(side == place_ref[2])
    def _():
        copy = pltpu.make_async_copy(source, keep_buf.at[side, at], sem)
        getattr(copy, back)()

    @pl.when(side != place_ref[2])
    def _():
        copy = pltpu.make_async_copy(source, send_buf.at[at], sem)
        getattr(copy, back)()


def local(
    tokens, cotangent, document_starts, pre_gain, pre_bias, project_weight, project_bias,
    head_scale, post_gain, post_bias, output_weight, expand_weight, expand_bias, middle_gain,
    middle_bias, reduce_weight, branch_bias,
):
    sections = lax.axis_size("section")
    section = lax.axis_index("section")
    parts = lax.axis_size("mp")
    part = lax.axis_index("mp")
    shard = lax.axis_index("batch")
    micro, rows_here, width = tokens.shape[1:]
    length = rows_here * parts
    chunk = CHUNK
    count = length // chunk
    head = width // (head_scale.shape[1] * parts)
    units = expand_bias.shape[1] * parts
    paired = parts == 2 and micro == 2
    by_links = paired and lax.axis_size("batch") == 4
    block = part * micro // parts
    copies = micro / parts

    def swapped(value):
        return lax.ppermute(value, "mp", [(0, 1), (1, 0)])

    def both(value, axis):
        if paired:
            return value, swapped(value)
        whole = lax.all_gather(value, "mp", axis=axis, tiled=True)
        return tuple(jnp.split(whole, 2, axis=axis))

    def row_source(value):
        if paired:
            theirs = lax.dynamic_index_in_dim(value, 1 - part, 0, keepdims=False)
            return value.reshape(micro * rows_here, width), swapped(theirs)
        whole = lax.all_gather(value, "mp", axis=1, tiled=True)
        whole = lax.dynamic_index_in_dim(whole, block, 0, keepdims=False)
        return whole[:length // 2], whole[length // 2:]

    def spread_rows(kept, sent, after):
        if paired:
            return with_other_half(kept, swapped(sent), place, after)
        whole = lax.all_gather(jnp.concatenate([kept[0], sent]), "mp", axis=0)[:: parts // micro]
        return lax.dynamic_slice_in_dim(whole, part * rows_here, rows_here, 1)

    near_tokens, far_tokens = row_source(tokens[0])
    place = jnp.stack(
        [
            section, jnp.int32(sections), part if paired else jnp.int32(0),
            part * rows_here if paired else jnp.int32(0), shard % 2, shard // 2,
        ]
    ).astype(jnp.int32)
    starts = lax.dynamic_index_in_dim(document_starts[0], block, 0, keepdims=False)[0]
    fields = (
        project_bias[0, 0], jnp.zeros_like(project_bias[0, 0]), project_bias[0, 1],
        jnp.repeat(head_scale[0], head), post_gain[0],
        post_bias[0], expand_bias[0], middle_gain[0], middle_bias[0],
    )
    if paired:
        own = jnp.concatenate(fields)[None]
        other = swapped(own)
    else:
        sides = [both(field, 0) for field in fields]
        own = jnp.concatenate([a for a, _ in sides])[None]
        other = jnp.concatenate([b for _, b in sides])[None]
    gains, biases, branches = pre_gain[0], pre_bias[0], branch_bias[0]
    wp_a, wp_b = both(project_weight[0], 2)
    wo_a, wo_b = both(output_weight[0], 0)
    we_a, we_b = both(expand_weight[0], 1)
    wr_a, wr_b = both(reduce_weight[0], 0)
    wp = loaded(0, wp_a, None, place)
    wo = loaded(0, wo_a, None, wp)
    we = loaded(0, we_a, None, wo)
    wr = loaded(0, wr_a, None, we)
    wr_own = wr
    wp = loaded(1, wp_b, wp, wr)
    wo = loaded(1, wo_b, wo, wp)
    we = loaded(1, we_b, we, wo)
    wr = loaded(1, wr_b, wr, we)
    vectors = jnp.stack([own, other]).astype(F32)
    near_cotangent, far_cotangent = row_source(cotangent[0])

    def sized(columns, dtype):
        return ((length, columns), dtype)

    halves = (((2, length // 2, width), BF16), ((length // 2, width), BF16))

    (
        x_buf, h1_buf, q_buf, o_buf, lse_buf, post_buf, mid_buf,
        h2_buf, g_buf, gp_buf, m_buf, st_buf, hid_keep, hid_send,
        df_buf, dur_buf, dmr_buf, dq_buf, dkr_buf, dvr_buf, ig_keep, ig_send,
    ) = empty(
        [
            sized(width, BF16), sized(width, BF16), sized(width, BF16), sized(width, F32),
            ((count, 128, chunk), F32), sized(width, BF16), sized(width, F32),
            sized(width, BF16), sized(units, BF16), sized(units, BF16), sized(units, BF16),
            sized(128, F32), *halves,
            sized(width, BF16), sized(units, BF16), sized(width, BF16), sized(width, BF16),
            sized(width, BF16), sized(width, BF16), *halves,
        ],
        pltpu.HBM,
    )
    k_all = jnp.zeros((length, width), BF16)
    v_all = jnp.zeros((length, width), BF16)
    dense = 2 * chunk * width

    def shifted(value, distance):
        route = [(i, i + distance) for i in range(sections) if 0 <= i + distance < sections]
        return lax.ppermute(value, "section", route)

    ticks = count + 2 * (sections - 1)
    blank = jnp.zeros((chunk, width), BF16)
    incoming = blank
    sent = None
    rows_in = first_rows(place, near_tokens, far_tokens, 0, chunk, wr_own)
    kept = (
        k_all, v_all, x_buf, h1_buf, q_buf, o_buf, lse_buf, post_buf, hid_keep, hid_send,
        h2_buf, g_buf, gp_buf, m_buf, st_buf, mid_buf,
    )
    for tick in range(ticks):
        now = jnp.full((1,), tick, jnp.int32)
        arriving = shifted(sent, 1) if sent is not None and tick + 1 < ticks else blank
        *kept, sent, rows_in = call(
            forward_kernel,
            (
                now, place, starts, near_tokens, far_tokens, near_cotangent, far_cotangent,
                rows_in, incoming, blank if sent is None else sent, wp, wo, we, wr, vectors, gains, biases, branches,
            ),
            [SMEM, SMEM, SMEM] + [HBM] * 4 + [VMEM] * 11,
            kept,
            [VMEM, VMEM] + [HBM] * 14,
            [jax.ShapeDtypeStruct((chunk, width), BF16)] * 2,
            [VMEM] * 2,
            [
                pltpu.VMEM((chunk, width), F32), *SCR["af"](chunk, width, units, length),
                *SCR["ff"](chunk, width, units, length),
            ],
            LIMITS[0],
            4 * dense * units,
        )
        incoming = arriving

    (
        k_all, v_all, x_buf, h1_buf, q_buf, o_buf, lse_buf, post_buf, hid_keep, hid_send,
        h2_buf, g_buf, gp_buf, m_buf, st_buf, mid_buf,
    ) = kept
    last_out = sent
    wrt = flipped(wr, sent)
    wpt = flipped(wp, wrt)
    wet = flipped(we, wpt)
    wot = flipped(wo, wet)
    dk_acc, dv_acc = empty([sized(width, F32)] * 2, pltpu.VMEM, wpt)
    sum_f = jnp.zeros((4, width), F32)
    sum_w = jnp.zeros((3, units), F32)
    sum_a = jnp.zeros((7, width), F32)
    incoming = blank
    sent = None

    def weight_gradient(left, right, axis):
        full = dot_tn(left, right).astype(BF16)
        total = lax.psum_scatter(full, "mp", scatter_dimension=axis, tiled=True)
        return (total.astype(F32) * copies).astype(BF16)

    def attend_back(now, after, prev, grad_mid, carried, cost=10):
        return call(
            attend_back_kernel,
            (
                now, place, starts, after, near_cotangent, far_cotangent, prev, grad_mid, wot,
                wpt, vectors, gains, k_all, v_all, x_buf, q_buf, o_buf, lse_buf,
            ),
            [SMEM, SMEM, SMEM, HBM, HBM, HBM] + [VMEM] * 8 + [HBM] * 4,
            carried,
            [VMEM, VMEM, VMEM] + [HBM] * 6,
            [jax.ShapeDtypeStruct((chunk, width), BF16)] * 2,
            [VMEM] * 2,
            SCR["ab"](chunk, width, units, length),
            LIMITS[2],
            cost * 11 * 10**8,
        )

    held = []
    carried = (sum_a, dk_acc, dv_acc, dq_buf, dkr_buf, dvr_buf, dmr_buf, ig_keep, ig_send)
    for tick in range(ticks):
        now = jnp.full((1,), tick, jnp.int32)
        arriving = shifted(sent, -1) if sent is not None and tick + 1 < ticks else blank
        sum_f, sum_w, df_buf, dur_buf, grad_mid = call(
            expand_back_kernel,
            (
                now, place, rows_in, incoming, wrt, wet, vectors, gains, g_buf, gp_buf, st_buf,
                mid_buf,
            ),
            [SMEM, SMEM] + [VMEM] * 6 + [HBM] * 4,
            (sum_f, sum_w, df_buf, dur_buf),
            [VMEM, VMEM] + [HBM] * 2,
            [jax.ShapeDtypeStruct((chunk, width), F32)],
            [VMEM],
            SCR["fb"](chunk, width, units, length),
            LIMITS[1],
            2 * dense * units,
        )
        held.append((now, grad_mid))
        if tick + 2 < ticks:
            held.clear()
            prev = blank if sent is None else sent
            *carried, sent, rows_in = attend_back(now, x_buf, prev, grad_mid, carried)
        incoming = arriving

    def gathered(sum_a):
        shared = jnp.stack([sum_a[5], sum_f[1], sum_a[6], sum_f[2], sum_f[3], sum_f[0]])
        narrow = jnp.stack([sum_a[3], sum_a[4], sum_a[2], sum_a[0], sum_a[1]])
        broad = jnp.stack([sum_w[2], sum_w[0], sum_w[1]])
        return shared, narrow, broad

    def packed(side, sum_a):
        shared, narrow, broad = gathered(sum_a)
        cut, wide_cut = width // 2, units // 2
        return jnp.concatenate(
            [
                shared.reshape(-1),
                narrow[:, side * cut:(side + 1) * cut].reshape(-1),
                broad[:, side * wide_cut:(side + 1) * wide_cut].reshape(-1),
            ]
        )

    def forward_chunk(section, last):
        return ticks - 1 - 2 * section

    def backward_chunk(section, last):
        return count - 1 - (ticks - 1 - 2 * (last - section))

    def finished(rows, chunk_of, keep, send):
        return last_rows(place, rows, chunk_of, count, keep, send)

    if by_links:
        reduce_sides = (m_buf,), (df_buf,), (0,)
        expand_sides = (h2_buf,), (dur_buf,), (0,)
        reduce_other = other_part(*reduce_sides, 0, df_buf)
        expand_other = other_part(*expand_sides, 1, reduce_other)
        pieces = own_part(*reduce_sides, swapped(reduce_other), place, expand_other)
        reduce_sum = BatchSum(pieces, place)
        pieces = own_part(*expand_sides, swapped(expand_other), place, pieces[3])
        expand_sum = BatchSum(pieces, place)
        after = pieces[3]
        for number, (now, grad_mid) in enumerate(held):
            *carried, sent, _ = attend_back(now, after, sent, grad_mid, carried, 1)
            after = reduce_sum.second(carried[-1], 1) if number == 0 else carried[-1]
        sum_a, _, _, dq_buf, dkr_buf, dvr_buf, dmr_buf, ig_keep, ig_send = carried
        mixed_sides = (h1_buf, dmr_buf), (dq_buf, dkr_buf, dvr_buf, post_buf), (0, 0, 0, 1)
        mixed_other = other_part(*mixed_sides, 1, after)
        after = expand_sum.second(mixed_other, COSTS[0])
        pieces = own_part(*mixed_sides, swapped(mixed_other), place, after)
        mixed_sum = BatchSum(pieces, place)
        after = reduce_sum.third(pieces[3], COSTS[1])
        kept = finished(last_out, forward_chunk, hid_keep, hid_send)
        after = hidden = spread_rows(*kept, after)
        small_one, small_two = (packed(side, sum_a).reshape(-1, 128) for side in (0, 1))
        small = plus(small_one, swapped(small_two), after)
        after = mixed_sum.second(after, COSTS[2])
        after = expand_sum.third(after, COSTS[3])
        after = mixed_sum.third(after, COSTS[4])
        kept = finished(sent, backward_chunk, ig_keep, ig_send)
        input_gradient = spread_rows(*kept, after)
        small = plus(small, crossed(small, 1), input_gradient)
        (reduce_grad,) = reduce_sum.result((reduce_weight.shape[1:],), input_gradient)
        small = plus(small, crossed(small, 2), reduce_grad)
        (expand_grad,) = expand_sum.result((expand_weight.shape[1:],), reduce_grad)
        project_grad, output_grad = mixed_sum.result(
            (project_weight.shape[1:], output_weight.shape[1:]), expand_grad
        )
        project_grad = project_grad[None]
    else:
        for now, grad_mid in held:
            *carried, sent, _ = attend_back(now, x_buf, sent, grad_mid, carried)
        sum_a, _, _, dq_buf, dkr_buf, dvr_buf, dmr_buf, ig_keep, ig_send = carried
        kept = finished(last_out, forward_chunk, hid_keep, hid_send)
        hidden = spread_rows(*kept, sent)
        kept = finished(sent, backward_chunk, ig_keep, ig_send)
        input_gradient = spread_rows(*kept, sent)
        reduce_grad, expand_grad, output_grad, *project_grad = (
            total.astype(F32)
            for total in lax.psum(
                (
                    weight_gradient(m_buf, df_buf, 0), weight_gradient(h2_buf, dur_buf, 1),
                    weight_gradient(post_buf, dmr_buf, 0), weight_gradient(h1_buf, dq_buf, 1),
                    weight_gradient(h1_buf, dkr_buf, 1), weight_gradient(h1_buf, dvr_buf, 1),
                ),
                "batch",
            )
        )
        project_grad = jnp.stack(project_grad)[None]

    if paired:
        if not by_links:
            small = lax.psum(packed(0, sum_a) + swapped(packed(1, sum_a)), "batch")
        small = small.reshape(-1)
        here, there = width // 2, units // 2
        shared = small[:6 * width].reshape(6, width)
        narrow = small[6 * width:6 * width + 5 * here].reshape(5, here)
        broad = small[6 * width + 5 * here:].reshape(3, there)
    else:
        shared, narrow, broad = gathered(sum_a)
        small = lax.psum(
            jnp.concatenate([shared.reshape(-1), narrow.reshape(-1), broad.reshape(-1)]),
            ("batch", "mp"),
        ) * copies
        shared = small[:6 * width].reshape(6, width)
        narrow = small[6 * width:11 * width].reshape(5, width)
        broad = small[11 * width:].reshape(3, units)
        narrow = lax.dynamic_slice_in_dim(narrow, part * (width // parts), width // parts, 1)
        broad = lax.dynamic_slice_in_dim(broad, part * (units // parts), units // parts, 1)

    return (
        hidden[None, None],
        input_gradient[None, None],
        shared[0:2][None],
        shared[2:4][None],
        project_grad,
        narrow[0:2][None],
        jnp.sum(narrow[2].reshape(-1, head), axis=1)[None],
        narrow[3][None],
        narrow[4][None],
        output_grad[None],
        expand_grad[None],
        broad[0][None],
        broad[1][None],
        broad[2][None],
        reduce_grad[None],
        shared[4:6][None],
    )


def solution(mesh):
    layered = P("section", None, None)
    split = P("section", "mp")
    rows = P("section", "mp", None)
    columns = P("section", None, "mp")
    projected = P("section", None, None, "mp")
    tokens = P("batch", None, "mp", None)
    states = P("section", "batch", None, "mp", None)
    return jax.shard_map(
        local,
        mesh=mesh,
        in_specs=(
            tokens, tokens, P("batch", None, None, None), layered, layered, projected, columns,
            split, split, split, rows, columns, split, split, split, rows, layered,
        ),
        out_specs=(
            states, states, layered, layered, projected, columns, split, split, split, rows,
            columns, split, split, split, rows, layered,
        ),
        check_vma=False,
    )
```
